512 devices in a mesh: seq: 32 (over x, y, core), head: 16 (over z).
Axes of the slice: x: 4, y: 4, z: 16, core: 2. Of those that a mesh axis runs over, the one named last changes fastest.
Arguments:
- query_data: bfloat16 [16384, 2048], P(('seq', 'head')), may hold values from -120 to 120
- key_data: bfloat16 [16384, 2048], P(('seq', 'head')), may hold values from -4 to 4
- value_data: bfloat16 [16384, 2048], P(('seq', 'head')), may hold values from -6 to 6
- output_data: bfloat16 [16384, 2048], P(('seq', 'head')), may hold values from -4 to 4
- output_grad: bfloat16 [16384, 2048], P(('seq', 'head')), may hold values from -6 to 6
- key_lists: int32 [32, 16], replicated, may hold values from 0 to 31, as said below
- key_counts: int32 [32], replicated, may hold values from 1 to 16, as said below
- block_order: int32 [32], replicated, may hold values from 0 to 31, as said below
Outputs:
- query_grad: bfloat16 [16384, 2048], P(('seq', 'head'))
- key_grad: bfloat16 [16384, 2048], P(('seq', 'head'))
- value_grad: bfloat16 [16384, 2048], P(('seq', 'head'))
The draws below stay inside these ranges and needn't reach their ends.
Inputs may be any that keep to these rules, and one draw needn't show every extreme that they name: `key_lists`: row i names sequence blocks: entry 0 is i itself; entries 1 to key_counts[i] - 1 are distinct earlier blocks, each stored on a different device of seq and none on the device that stores block i (device of stored block p: p); the entries after them repeat i. `key_counts`: block 0 uses 1 entry and block 31 uses 16. `block_order`: A permutation of the sequence blocks.
All inputs are finite; a program needn't handle non-finite values.
Results may differ from the reference program's by a relative error of at most 0.011.
Values may be sent and summed in bfloat16 or wider, within the bound.
No kernel may reach another device: no remote copies, remote signals or barrier semaphores. Data moves between devices by JAX's collectives and lax.ppermute only.
A program may use at most 64 MiB of HBM per device.

```python
import math
import jax
import jax.numpy as jnp
from jax import lax

D = 2048
HEADS = 16
HD = 128
BLK = 512
BPD = 1
NB = 32
TOKENS = 16384
MAXK = 16
N_SEQ = 32


def block_pattern(key):
    base = jax.random.fold_in(key, 101)
    key_order, key_pick, key_rank, key_count = jax.random.split(base, 4)
    order = jax.random.permutation(key_order, NB).astype(jnp.int32)
    place_of = jnp.argsort(order).astype(jnp.int32)
    owner = place_of // BPD
    logical = jnp.arange(NB, dtype=jnp.int32)
    allowed = (logical[None, :] < logical[:, None]) & (owner[None, :] != owner[:, None])
    stored_ok = allowed[:, order]
    pick_score = jax.random.randint(key_pick, (NB, NB), 0, 1 << 20) * NB + jnp.arange(NB, dtype=jnp.int32)[None, :]
    pick_score = jnp.where(stored_ok, pick_score, -1).reshape(NB, N_SEQ, BPD)
    best = jnp.argmax(pick_score, axis=2).astype(jnp.int32)
    usable = jnp.max(pick_score, axis=2) >= 0
    chosen = order.reshape(N_SEQ, BPD)[jnp.arange(N_SEQ, dtype=jnp.int32)[None, :], best]
    rank_score = jax.random.randint(key_rank, (NB, N_SEQ), 0, 1 << 20) * N_SEQ + jnp.arange(N_SEQ, dtype=jnp.int32)[None, :]
    rank_score = jnp.where(usable, rank_score, -1)
    ranked = jnp.argsort(-rank_score, axis=1).astype(jnp.int32)
    n_usable = jnp.sum(usable.astype(jnp.int32), axis=1)
    counts = jax.random.randint(key_count, (NB,), MAXK // 2, MAXK + 1)
    counts = jnp.maximum(counts, 1)
    counts = counts.at[NB - 1].set(MAXK)
    counts = jnp.minimum(counts, n_usable + 1).astype(jnp.int32)
    picks = jnp.take_along_axis(chosen, ranked[:, :MAXK - 1], axis=1)
    column = jnp.arange(1, MAXK, dtype=jnp.int32)
    tail = jnp.where(column[None, :] < counts[:, None], picks, logical[:, None])
    lists = jnp.concatenate([logical[:, None], tail], axis=1).astype(jnp.int32)
    return (order, lists, counts)


def aligned_keys(key, nearness):
    base = jax.random.fold_in(key, 202)
    key_main, key_strength = jax.random.split(base)
    values = jnp.clip(jax.random.normal(key_main, (TOKENS, D), jnp.float32), -4.0, 4.0)
    strength = 10.0 + 20.0 * jax.random.uniform(key_strength, (NB, 1, HEADS, 1), jnp.float32)
    blocks = values.reshape(NB, BLK, HEADS, HD)
    first = blocks[:, 0:1]
    second = jnp.where(nearness > 0.0, (1.0 - nearness / strength) * first, blocks[:, 1:2])
    blocks = jnp.concatenate([first, second, blocks[:, 2:]], axis=1)
    return blocks


def draw_block_order(key, part):
    order, lists, counts = block_pattern(key)
    return order


def draw_key_lists(key, part):
    order, lists, counts = block_pattern(key)
    return lists


def draw_key_counts(key, part):
    order, lists, counts = block_pattern(key)
    return counts


def draw_key_data(key, part):
    nearness = 0.0
    blocks = aligned_keys(key, nearness)
    return blocks.reshape(TOKENS, D).astype(jnp.bfloat16)


def draw_query_data(key, part):
    key = jax.random.fold_in(key, 3)
    queries = jnp.clip(jax.random.normal(key, (TOKENS, D), jnp.float32), -4.0, 4.0)
    queries = queries.reshape(NB, BLK, HEADS, HD)
    return queries.reshape(TOKENS, D).astype(jnp.bfloat16)


def block_levels(key, dims, pieces, low, top_value):
    loudness, own = 1.0, jax.random.fold_in(key, 6)
    for position, parts in pieces:
        draws = jnp.exp(jax.random.uniform(jax.random.fold_in(own, position), (parts,), jnp.float32, low / len(pieces), top_value / len(pieces)))
        loudness = loudness * jnp.repeat(draws, dims[position] // parts).reshape([-1 if axis == position else 1 for axis in range(len(dims))])
    return loudness


def gaussian(key, shape, spread, reach, pieces=(), held_as=jnp.bfloat16):
    result = spread * jax.random.normal(key, shape, jnp.float32)
    if pieces:
        result = result * block_levels(key, shape, pieces, -0.22, 0.18)
    return jnp.clip(result, -reach, reach).astype(held_as)


def setup_inputs(seed: int = 0) -> dict:
    streams_of = jax.random.split(jax.random.key(seed), 9)
    return {
        "query_data": draw_query_data(jax.random.fold_in(streams_of[8], 71), 0),
        "key_data": draw_key_data(jax.random.fold_in(streams_of[8], 71), 0),
        "value_data": gaussian(streams_of[2], (TOKENS, D), 1.0, 6.0, ((0, 512),)),
        "output_data": gaussian(streams_of[3], (TOKENS, D), 0.5, 4.0, ((0, 512),)),
        "output_grad": gaussian(streams_of[4], (TOKENS, D), 1.0, 6.0, ((0, 512),)),
        "key_lists": draw_key_lists(jax.random.fold_in(streams_of[8], 71), 0),
        "key_counts": draw_key_counts(jax.random.fold_in(streams_of[8], 71), 0),
        "block_order": draw_block_order(jax.random.fold_in(streams_of[8], 71), 0),
    }


LOW_SCORE = -1e+30

def rounded(values):
    return lax.optimization_barrier(values.astype(jnp.bfloat16)).astype(jnp.float32)

def reference(query_data, key_data, value_data, output_data, output_grad, key_lists, key_counts, block_order):
    scale = 1.0 / math.sqrt(HD)
    place_of = jnp.argsort(block_order).astype(jnp.int32)
    query_blocks = query_data.reshape(NB, BLK, HEADS, HD)
    key_blocks = key_data.reshape(NB, BLK, HEADS, HD)
    value_blocks = value_data.reshape(NB, BLK, HEADS, HD)
    output_blocks = output_data.reshape(NB, BLK, HEADS, HD)
    grad_blocks = output_grad.reshape(NB, BLK, HEADS, HD)
    positions = jnp.arange(BLK, dtype=jnp.int32)
    causal = positions[None, :] <= positions[:, None]

    def visit(carry, stored):
        key_total, value_total = carry
        sequence_block = block_order[stored]
        names = key_lists[sequence_block]
        places = place_of[names].astype(jnp.int32)
        valid = jnp.arange(MAXK, dtype=jnp.int32) < key_counts[sequence_block]
        queries = query_blocks[stored].astype(jnp.float32)
        grads = grad_blocks[stored].astype(jnp.float32)
        outputs = output_blocks[stored].astype(jnp.float32)
        keys_sel = key_blocks[places].astype(jnp.float32)
        values_sel = value_blocks[places].astype(jnp.float32)
        scores = jnp.einsum('rhd,mchd->hrmc', queries, keys_sel) * scale
        allowed = valid[None, None, :, None] & ((names != sequence_block)[None, None, :, None] | causal[None, :, None, :])
        maxima = lax.optimization_barrier(jnp.max(jnp.where(allowed, scores, LOW_SCORE), axis=(2, 3)))
        totals = lax.optimization_barrier(jnp.sum(jnp.where(allowed, jnp.exp(scores - maxima[:, :, None, None]), 0.0), axis=(2, 3)))
        log_norm = maxima + jnp.log(totals)
        row_dot = lax.optimization_barrier(jnp.sum(grads * outputs, axis=2))
        probs = jnp.where(allowed, jnp.exp(scores - log_norm[:, :, None, None]), 0.0)
        probs_low = rounded(probs)
        value_part = jnp.einsum('hrmc,rhd->mchd', probs_low, grads)
        dprob = jnp.einsum('rhd,mchd->hrmc', grads, values_sel)
        dscore_low = rounded(probs * (dprob - jnp.transpose(row_dot)[:, :, None, None]) * scale)
        key_part = jnp.einsum('hrmc,rhd->mchd', dscore_low, queries)
        pair_grad = rounded(jnp.einsum('hrmc,mchd->mrhd', dscore_low, keys_sel))
        query_part = lax.optimization_barrier(jnp.sum(pair_grad, axis=0)).astype(jnp.bfloat16)
        key_total = key_total.at[places].add(key_part)
        value_total = value_total.at[places].add(value_part)
        return ((key_total, value_total), query_part)
    start = (jnp.zeros((NB, BLK, HEADS, HD), jnp.float32), jnp.zeros((NB, BLK, HEADS, HD), jnp.float32))
    (key_total, value_total), query_parts = lax.scan(visit, start, jnp.arange(NB, dtype=jnp.int32))
    query_grad = query_parts.reshape(TOKENS, D)
    key_grad = key_total.reshape(TOKENS, D).astype(jnp.bfloat16)
    value_grad = value_total.reshape(TOKENS, D).astype(jnp.bfloat16)
    return (query_grad, key_grad, value_grad)
```

```python
import math

import jax
import jax.numpy as jnp
from jax import lax
from jax.experimental import pallas as pl
from jax.experimental.pallas import tpu as pltpu
from jax.sharding import Mesh, PartitionSpec as P

HD = 128
BLK = 512
HEADS = 16
ROWS = BLK // HEADS
NX, NY, NC = 4, 4, 2
NQ = NY * NC
NK = NX
NPAIR = NQ * NK
QD_ROWS = 2 * BLK + 16
CHUNK = 256
SCALE = 1.0 / math.sqrt(HD)
SCALE2 = SCALE * math.log2(math.e)
LOW = -1e30
VMEM = 48 * 1024 * 1024


def dot(a, b, contract):
    return lax.dot_general(a, b, ((contract[:1], contract[1:]), ((), ())), preferred_element_type=jnp.float32)


def query_place(code, meta):
    slot = code // NK
    return ((meta[1] - slot % NY) & (NY - 1)) * NC + (meta[2] ^ (slot // NY))


def probs_kernel(pairs, meta, qd, kv, probs, tops, stats):
    t = pl.program_id(0)
    code = pairs[t]
    place = query_place(code, meta)

    @pl.when(t == 0)
    def _():
        stats[:, 0, :] = jnp.full((NQ, BLK), LOW, jnp.float32)
        stats[:, 1, :] = jnp.zeros((NQ, BLK), jnp.float32)

    def visit(diagonal):
        keys = kv[code % NK, :BLK, :]
        for start in range(0, BLK, CHUNK):
            part = slice(start, start + CHUNK)
            scores = dot(keys, qd[0, part, :], (1, 1))
            if diagonal:
                key_row = lax.broadcasted_iota(jnp.int32, scores.shape, 0)
                query_row = lax.broadcasted_iota(jnp.int32, scores.shape, 1) + start
                scores = jnp.where(key_row <= query_row, scores, LOW)
            top = jnp.max(scores, axis=0, keepdims=True) * SCALE2
            values = jnp.exp2(scores * SCALE2 - top)
            total = jnp.sum(values, axis=0, keepdims=True)
            probs[0, :, part] = values.astype(jnp.bfloat16)
            tops[0, :, part] = top
            old_top, old_total = stats[place, 0:1, part], stats[place, 1:2, part]
            new_top = jnp.maximum(old_top, top)
            stats[place, 0:1, part] = new_top
            stats[place, 1:2, part] = old_total * jnp.exp2(old_top - new_top) + total * jnp.exp2(top - new_top)

    @pl.when(t == 0)
    def _():
        visit(True)

    @pl.when((t != 0) & (t < meta[0]))
    def _():
        visit(False)


def dscore_kernel(pairs, meta, qd, kv, probs, tops, stats, dscore, dquery, keys_t, total):
    t = pl.program_id(0)
    code = pairs[t]
    place = query_place(code, meta)
    key = code % NK

    @pl.when(t == 0)
    def _():
        total[...] = jnp.zeros_like(total)
        for i in range(NK):
            keys_t[i] = jnp.transpose(kv[i, :BLK, :])

    @pl.when(t < meta[0])
    def _():
        pieces = qd[0, 2 * BLK :, :].astype(jnp.float32)
        row_dot = pieces[0:4] + pieces[4:8] + pieces[8:12]
        row_dot = jnp.concatenate([row_dot[i : i + 1] for i in range(4)], axis=1)
        weight = jnp.exp2(tops[0] - stats[place, 0:1, :])
        values = kv[key, BLK:, :]
        for start in range(0, BLK, CHUNK):
            part = slice(start, start + CHUNK)
            dprob = dot(values, qd[0, BLK + start : BLK + start + CHUNK, :], (1, 1))
            low = (probs[0, :, part].astype(jnp.float32) * (dprob - row_dot[:, part])).astype(jnp.bfloat16)
            dscore[0, :, part] = low
            total[place, :, part] += dot(keys_t[key], low, (1, 0)) * weight[:, part]

    @pl.when(t == meta[0] - 1)
    def _():
        for i in range(NQ):
            dquery[i] = jnp.transpose(total[i]).astype(jnp.bfloat16)


def log_norms(stats_all):
    tops, sums = stats_all[:, :, 0, :], stats_all[:, :, 1, :]
    top = jnp.max(tops, axis=0)
    return top + jnp.log2(jnp.sum(sums * jnp.exp2(tops - top[None]), axis=0))


def key_kernel(pairs, meta, qd, probs, dscore, tops, stats_all, out, norms, total):
    t = pl.program_id(0)
    code = pairs[t]
    place = query_place(code, meta)
    key = code % NK

    @pl.when(t == 0)
    def _():
        total[...] = jnp.zeros_like(total)
        norms[:, 0, :] = log_norms(stats_all[...])

    @pl.when(t < meta[0])
    def _():
        weight = jnp.exp2(tops[0] - norms[place])
        weight = jnp.transpose(jnp.broadcast_to(weight, (HD, BLK)))
        queries = (qd[0, :BLK, :].astype(jnp.float32) * (weight * SCALE)).astype(jnp.bfloat16)
        grads = (qd[0, BLK : 2 * BLK, :].astype(jnp.float32) * weight).astype(jnp.bfloat16)
        total[key, 0] += dot(dscore[0], queries, (1, 0))
        total[key, 1] += dot(probs[0], grads, (1, 0))

    @pl.when(t == meta[0] - 1)
    def _():
        out[...] = total[...].astype(jnp.bfloat16)


def finish_kernel(meta, dquery, stats_all, own, first, second, third, out):
    place = meta[1] * NC + meta[2]
    tops, sums = stats_all[:, place, 0, :], stats_all[:, place, 1, :]
    top = jnp.max(tops, axis=0, keepdims=True)
    norm = top + jnp.log2(jnp.sum(sums * jnp.exp2(tops - top), axis=0, keepdims=True))
    weight = jnp.transpose(jnp.exp2(tops - norm) * SCALE)
    query_grad = dquery[0].astype(jnp.float32) * weight[:, 0:1]
    for i in range(1, NQ):
        query_grad += dquery[i].astype(jnp.float32) * weight[:, i : i + 1]
    out[:, 0:ROWS, :] = query_grad.astype(jnp.bfloat16).reshape(HEADS, ROWS, HD)
    for i in range(2):
        grad = (own[0, i].astype(jnp.float32) + first[i].astype(jnp.float32)) + (
            second[i].astype(jnp.float32) + third[i].astype(jnp.float32)
        )
        out[:, (i + 1) * ROWS : (i + 2) * ROWS, :] = grad.astype(jnp.bfloat16).reshape(HEADS, ROWS, HD)


def params():
    return pltpu.CompilerParams(vmem_limit_bytes=VMEM)


def by_query(rows=QD_ROWS):
    return pl.BlockSpec((1, rows, HD), lambda t, pairs, meta: (pairs[t] // NK, 0, 0))


def by_pair(*shape):
    return pl.BlockSpec((1, *shape), lambda t, pairs, meta: (jnp.minimum(t, meta[0] - 1), 0, 0))


def whole(*shape):
    return pl.BlockSpec(shape, lambda *_: (0,) * len(shape))


def over_pairs(kernel, pairs, meta, operands, in_specs, out_specs, out_shape, scratch=()):
    return pl.pallas_call(
        kernel,
        grid_spec=pltpu.PrefetchScalarGridSpec(
            num_scalar_prefetch=2,
            grid=(NPAIR,),
            in_specs=in_specs,
            out_specs=out_specs,
            scratch_shapes=scratch,
        ),
        out_shape=out_shape,
        compiler_params=params(),
    )(pairs, meta, *operands)


def pair_list(key_lists, key_counts, block_order, x, y, c):
    slot = jnp.arange(NQ, dtype=jnp.int32)
    query_at = x * NQ + ((y - slot % NY) % NY) * NC + (c ^ (slot // NY))
    key_at = ((x - jnp.arange(NK, dtype=jnp.int32)) % NX) * NQ + y * NC + c
    query_blocks, key_blocks = block_order[query_at], block_order[key_at]
    lists, counts = key_lists[query_blocks], key_counts[query_blocks]
    used = jnp.arange(key_lists.shape[1], dtype=jnp.int32)[None, :] < counts[:, None]
    named = jnp.any((lists[:, None, :] == key_blocks[None, :, None]) & used[:, None, :], axis=2)
    named = named.reshape(NPAIR)
    code = jnp.arange(NPAIR, dtype=jnp.int32)
    rank = jnp.sum((code[None, :] < code[:, None]) & named[None, :], axis=1)
    count = jnp.sum(named.astype(jnp.int32))
    wanted = jnp.minimum(code, count - 1)
    pairs = jnp.sum(jnp.where(named[None, :] & (rank[None, :] == wanted[:, None]), code[None, :], 0), axis=1)
    return pairs.astype(jnp.int32), count


def shifted(array, axis, by, size):
    return lax.ppermute(array, axis, [(i, (i + by) % size) for i in range(size)])


def on_device(query_data, key_data, value_data, output_data, output_grad, key_lists, key_counts, block_order):
    x, y, c = lax.axis_index("x"), lax.axis_index("y"), lax.axis_index("c")

    def heads(array):
        return jnp.transpose(array.reshape(ROWS, HEADS, HD), (1, 0, 2))

    products = output_grad.astype(jnp.float32) * output_data.astype(jnp.float32)
    row_dot = jnp.transpose(jnp.sum(products.reshape(ROWS, HEADS, HD), axis=2))
    high = lax.reduce_precision(row_dot, 8, 7)
    middle = lax.reduce_precision(row_dot - high, 8, 7)
    pieces = jnp.stack([high, middle, row_dot - high - middle], axis=1).astype(jnp.bfloat16)
    pieces = jnp.pad(pieces, ((0, 0), (0, 13), (0, HD - ROWS)))
    packed = jnp.concatenate(
        [heads(query_data), heads(output_grad), heads(key_data), heads(value_data), pieces], axis=1
    )
    packed = lax.all_to_all(packed, "h", 0, 0, tiled=True)

    def rows(i):
        return packed[:, i * ROWS : (i + 1) * ROWS, :].reshape(BLK, HD)

    pieces = jnp.transpose(packed[:, 4 * ROWS : 4 * ROWS + 3, :ROWS], (1, 0, 2)).reshape(12, HD)
    qd = jnp.concatenate([rows(0), rows(1), pieces, jnp.zeros((4, HD), jnp.bfloat16)], axis=0)
    kv = jnp.concatenate([rows(2), rows(3)], axis=0)

    pairs, count = pair_list(key_lists, key_counts, block_order, x, y, c)
    meta = jnp.stack([count, y, c]).astype(jnp.int32)

    kv_all = jnp.stack([kv] + [shifted(kv, "x", i, NX) for i in range(1, NX)])
    qd_own = jnp.stack([qd] + [shifted(qd, "y", i, NY) for i in range(1, NY)])
    qd_all = jnp.concatenate([qd_own, shifted(qd_own, "c", 1, NC)], axis=0)

    bf16, f32 = jnp.bfloat16, jnp.float32
    shape = jax.ShapeDtypeStruct
    square, line = shape((NPAIR, BLK, BLK), bf16), shape((NPAIR, 1, BLK), f32)
    probs, tops, stats = over_pairs(
        probs_kernel, pairs, meta, (qd_all, kv_all),
        [by_query(), whole(NK, 2 * BLK, HD)],
        [by_pair(BLK, BLK), by_pair(1, BLK), whole(NQ, 2, BLK)],
        [square, line, shape((NQ, 2, BLK), f32)],
    )
    stats_all = lax.all_to_all(
        jnp.broadcast_to(stats[None], (NQ, NQ, 2, BLK)), ("y", "c"), 0, 0, tiled=True
    )
    dscore, dquery = over_pairs(
        dscore_kernel, pairs, meta, (qd_all, kv_all, probs, tops, stats),
        [by_query(), whole(NK, 2 * BLK, HD), by_pair(BLK, BLK), by_pair(1, BLK), whole(NQ, 2, BLK)],
        [by_pair(BLK, BLK), whole(NQ, BLK, HD)],
        [square, shape((NQ, BLK, HD), bf16)],
        [pltpu.VMEM((NK, HD, BLK), bf16), pltpu.VMEM((NQ, HD, BLK), f32)],
    )
    dquery = lax.all_to_all(dquery, ("y", "c"), 0, 0, tiled=True)
    dkv = over_pairs(
        key_kernel, pairs, meta, (qd_all, probs, dscore, tops, stats_all),
        [by_query(), by_pair(BLK, BLK), by_pair(BLK, BLK), by_pair(1, BLK), whole(NQ, NQ, 2, BLK)],
        whole(NK, 2, BLK, HD),
        shape((NK, 2, BLK, HD), bf16),
        [pltpu.VMEM((NQ, 1, BLK), f32), pltpu.VMEM((NK, 2, BLK, HD), f32)],
    )
    arrived = [shifted(dkv[i], "x", -i, NX) for i in range(1, NX)]

    part = whole(2, BLK, HD)
    grads = pl.pallas_call(
        finish_kernel,
        grid_spec=pltpu.PrefetchScalarGridSpec(
            num_scalar_prefetch=1,
            grid=(1,),
            in_specs=[whole(NQ, BLK, HD), whole(NQ, NQ, 2, BLK), whole(1, 2, BLK, HD), part, part, part],
            out_specs=whole(HEADS, 3 * ROWS, HD),
        ),
        out_shape=shape((HEADS, 3 * ROWS, HD), bf16),
        compiler_params=params(),
    )(meta, dquery, stats_all, dkv, *arrived)
    grads = lax.all_to_all(grads, "h", 0, 0, tiled=True)

    def tokens(i):
        part = grads[:, i * ROWS : (i + 1) * ROWS, :]
        return jnp.transpose(part, (1, 0, 2)).reshape(ROWS, HEADS * HD)

    return tokens(0), tokens(1), tokens(2)


def solution(mesh):
    wide = Mesh(mesh.devices.reshape(NX, NY, NC, HEADS), ("x", "y", "c", "h"))
    split = P(("x", "y", "c", "h"), None)
    return jax.shard_map(
        on_device,
        mesh=wide,
        in_specs=(split,) * 5 + (P(),) * 3,
        out_specs=(split,) * 3,
        check_vma=False,
    )
```

```python
import functools
import math

import jax
import jax.numpy as jnp
from jax import lax
from jax.experimental import pallas as pl
from jax.experimental.pallas import tpu as pltpu
from jax.sharding import Mesh, PartitionSpec as P

HD = 128
BLK = 512
HEADS = 16
ROWS = BLK // HEADS
NX, NY, NC = 4, 4, 2
NQ = NY * NC
NK = NX
NPAIR = NQ * NK
QD_ROWS = 2 * BLK + 16
UNROLL = 4
DEPTH = 3
SHIFTS = (0, 3, 1, 2)
SCALE = 1.0 / math.sqrt(HD)
SCALE2 = SCALE * math.log2(math.e)
LOW = -1e30
VMEM = 48 * 1024 * 1024


def dot(a, b, contract):
    return lax.dot_general(a, b, ((contract[:1], contract[1:]), ((), ())), preferred_element_type=jnp.float32)


def query_place(code, meta):
    slot = code % NQ
    return ((meta[1] - slot % NY) & (NY - 1)) * NC + (meta[2] ^ (slot // NY))


def fetch_queries(own, other, qd, sems):
    return [
        pltpu.make_async_copy(own, qd.at[pl.ds(0, NY)], sems.at[0]),
        pltpu.make_async_copy(other, qd.at[pl.ds(NY, NY)], sems.at[1]),
    ]


def fetch_keys(blocks, kv, sems):
    return [pltpu.make_async_copy(block, kv.at[i], sems.at[i]) for i, block in enumerate(blocks)]


def probs_kernel(
    pairs, meta, own, other, kv0, kv1, kv2, kv3, probs, tops, stats, qd, kv, held, sems, key_sems, out_sems
):
    fetches = fetch_queries(own, other, qd, sems) + fetch_keys((kv0, kv1, kv2, kv3), kv, key_sems)
    for fetch in fetches:
        fetch.start()
    stats[:, 0, :] = jnp.full((NQ, BLK), LOW, jnp.float32)
    stats[:, 1, :] = jnp.zeros((NQ, BLK), jnp.float32)
    for fetch in fetches:
        fetch.wait()
    count = meta[0]
    steps = (count + UNROLL - 1) // UNROLL

    def store(step):
        return pltpu.make_async_copy(
            held.at[step & 1], probs.at[pl.ds(step * UNROLL, UNROLL)], out_sems.at[step & 1]
        )

    def visit(step, first):
        @pl.when(step >= 2)
        def _():
            store(step).wait()

        found = []
        for u in range(UNROLL):
            code = pairs[step * UNROLL + u]
            scores = dot(kv[code // NQ, :BLK, :], qd[code % NQ, :BLK, :], (1, 1))
            if first and u == 0:
                key_row = lax.broadcasted_iota(jnp.int32, scores.shape, 0)
                query_row = lax.broadcasted_iota(jnp.int32, scores.shape, 1)
                scores = jnp.where(key_row <= query_row, scores, LOW)
            found.append((scores, jnp.max(scores, axis=0, keepdims=True) * SCALE2))
        for u, (scores, top) in enumerate(found):
            t = step * UNROLL + u
            place = query_place(pairs[t], meta)
            values = jnp.exp2(scores * SCALE2 - top)
            total = jnp.sum(values, axis=0, keepdims=True)
            held[step & 1, u] = values.astype(jnp.bfloat16)
            tops[t] = top
            top = jnp.where(t < count, top, LOW)
            total = jnp.where(t < count, total, 0.0)
            old_top, old_total = stats[place, 0:1, :], stats[place, 1:2, :]
            new_top = jnp.maximum(old_top, top)
            stats[place, 0:1, :] = new_top
            stats[place, 1:2, :] = old_total * jnp.exp2(old_top - new_top) + total * jnp.exp2(top - new_top)
        store(step).start()

    visit(0, True)

    def body(step, _):
        visit(step, False)
        return 0

    lax.fori_loop(1, steps, body, 0)
    store(steps - 1).wait()

    @pl.when(steps >= 2)
    def _():
        store(steps - 2).wait()


def dscore_kernel(
    pairs, meta, own, other, kv0, kv1, kv2, kv3, probs, tops, stats, dscore, dquery,
    qd, kv, keys_t, total, read, held, sems, key_sems, in_sems, out_sems,
):
    count = meta[0]
    steps = (count + UNROLL - 1) // UNROLL

    def load(step):
        return pltpu.make_async_copy(
            probs.at[pl.ds(step * UNROLL, UNROLL)], read.at[step & 1], in_sems.at[step & 1]
        )

    def store(step):
        return pltpu.make_async_copy(
            held.at[step & 1], dscore.at[pl.ds(step * UNROLL, UNROLL)], out_sems.at[step & 1]
        )

    key_fetches = fetch_keys((kv0, kv1, kv2, kv3), kv, key_sems)
    fetches = fetch_queries(own, other, qd, sems)
    for fetch in key_fetches + fetches:
        fetch.start()
    load(0).start()
    total[...] = jnp.zeros_like(total)
    for i, fetch in enumerate(key_fetches):
        fetch.wait()
        keys_t[i] = jnp.transpose(kv[i, :BLK, :])
    for fetch in fetches:
        fetch.wait()

    def body(step, _):
        load(step).wait()

        @pl.when(step + 1 < steps)
        def _():
            load(step + 1).start()

        @pl.when(step >= 2)
        def _():
            store(step).wait()

        for u in range(UNROLL):
            t = step * UNROLL + u
            code = pairs[t]
            place, key, query = query_place(code, meta), code // NQ, code % NQ
            pieces = qd[query, 2 * BLK :, :].astype(jnp.float32)
            row_dot = pieces[0:4] + pieces[4:8] + pieces[8:12]
            row_dot = jnp.concatenate([row_dot[i : i + 1] for i in range(4)], axis=1)
            weight = jnp.where(t < count, jnp.exp2(tops[t] - stats[place, 0:1, :]), 0.0)
            dprob = dot(kv[key, BLK:, :], qd[query, BLK : 2 * BLK, :], (1, 1))
            low = (read[step & 1, u].astype(jnp.float32) * (dprob - row_dot)).astype(jnp.bfloat16)
            held[step & 1, u] = low
            total[place] += dot(keys_t[key], low, (1, 0)) * weight
        store(step).start()
        return 0

    lax.fori_loop(0, steps, body, 0)
    for i in range(NQ):
        dquery[i] = jnp.transpose(total[i]).astype(jnp.bfloat16)
    store(steps - 1).wait()

    @pl.when(steps >= 2)
    def _():
        store(steps - 2).wait()


def log_norms(stats_all):
    tops, sums = stats_all[:, :, 0, :], stats_all[:, :, 1, :]
    top = jnp.max(tops, axis=0)
    return top + jnp.log2(jnp.sum(sums * jnp.exp2(tops - top[None]), axis=0))


def key_kernel(
    late, pairs, meta, own, other, probs, dscore, tops, stats_all, out,
    qd, norms, total, p_read, d_read, sems, p_sems, d_sems,
):
    begin, end = (0, meta[3]) if late else (meta[3], meta[0])
    steps = (end - begin + UNROLL - 1) // UNROLL

    def loads(step):
        slot = lax.rem(step, DEPTH)
        copies = []
        for u in range(UNROLL):
            t = jnp.minimum(begin + step * UNROLL + u, end - 1)
            copies.append(pltpu.make_async_copy(probs.at[t], p_read.at[slot, u], p_sems.at[slot, u]))
            copies.append(pltpu.make_async_copy(dscore.at[t], d_read.at[slot, u], d_sems.at[slot, u]))
        return copies

    def prefetch(step):
        @pl.when(step < steps)
        def _():
            for copy in loads(step):
                copy.start()

    fetches = fetch_queries(own, other, qd, sems)
    for fetch in fetches:
        fetch.start()
    for step in range(DEPTH - 1):
        prefetch(step)
    total[...] = jnp.zeros_like(total)
    norms[:, 0, :] = log_norms(stats_all[...])
    for fetch in fetches:
        fetch.wait()

    def body(step, _):
        slot = lax.rem(step, DEPTH)
        for copy in loads(step):
            copy.wait()
        prefetch(step + DEPTH - 1)
        found = []
        for u in range(UNROLL):
            t = begin + step * UNROLL + u
            code = pairs[jnp.minimum(t, end - 1)]
            place, key, query = query_place(code, meta), code // NQ, code % NQ
            weight = jnp.where(t < end, jnp.exp2(tops[jnp.minimum(t, end - 1)] - norms[place]), 0.0)
            weight = jnp.transpose(jnp.broadcast_to(weight, (HD, BLK)))
            queries = (qd[query, :BLK, :].astype(jnp.float32) * (weight * SCALE)).astype(jnp.bfloat16)
            grads = (qd[query, BLK : 2 * BLK, :].astype(jnp.float32) * weight).astype(jnp.bfloat16)
            found.append((key & 1, dot(d_read[slot, u], queries, (1, 0)), dot(p_read[slot, u], grads, (1, 0))))
        for key, key_part, value_part in found:
            total[key, 0] += key_part
            total[key, 1] += value_part
        return 0

    lax.fori_loop(0, steps, body, 0)
    out[...] = total[...].astype(jnp.bfloat16)


def finish_kernel(meta, dquery, stats_all, own, first, second, third, out):
    place = meta[1] * NC + meta[2]
    tops, sums = stats_all[:, place, 0, :], stats_all[:, place, 1, :]
    top = jnp.max(tops, axis=0, keepdims=True)
    norm = top + jnp.log2(jnp.sum(sums * jnp.exp2(tops - top), axis=0, keepdims=True))
    weight = jnp.transpose(jnp.exp2(tops - norm) * SCALE)
    query_grad = dquery[0].astype(jnp.float32) * weight[:, 0:1]
    for i in range(1, NQ):
        query_grad += dquery[i].astype(jnp.float32) * weight[:, i : i + 1]
    out[:, 0:ROWS, :] = query_grad.astype(jnp.bfloat16).reshape(HEADS, ROWS, HD)
    for i in range(2):
        grad = (own[0, i].astype(jnp.float32) + first[i].astype(jnp.float32)) + (
            second[i].astype(jnp.float32) + third[i].astype(jnp.float32)
        )
        out[:, (i + 1) * ROWS : (i + 2) * ROWS, :] = grad.astype(jnp.bfloat16).reshape(HEADS, ROWS, HD)


def params():
    return pltpu.CompilerParams(vmem_limit_bytes=VMEM)


def whole(*shape):
    return pl.BlockSpec(shape, lambda *_: (0,) * len(shape))


def over_pairs(kernel, pairs, meta, operands, in_specs, out_specs, out_shape, scratch):
    return pl.pallas_call(
        kernel,
        grid_spec=pltpu.PrefetchScalarGridSpec(
            num_scalar_prefetch=2,
            grid=(1,),
            in_specs=in_specs,
            out_specs=out_specs,
            scratch_shapes=scratch,
        ),
        out_shape=out_shape,
        compiler_params=params(),
    )(pairs, meta, *operands)


def pair_list(key_lists, key_counts, block_order, x, y, c):
    slot = jnp.arange(NQ, dtype=jnp.int32)
    query_at = x * NQ + ((y - slot % NY) % NY) * NC + (c ^ (slot // NY))
    key_at = ((x - jnp.array(SHIFTS, jnp.int32)) % NX) * NQ + y * NC + c
    query_blocks, key_blocks = block_order[query_at], block_order[key_at]
    lists, counts = key_lists[query_blocks], key_counts[query_blocks]
    used = jnp.arange(key_lists.shape[1], dtype=jnp.int32)[None, :] < counts[:, None]
    named = jnp.any((lists[None, :, :] == key_blocks[:, None, None]) & used[None, :, :], axis=2)
    named = named.reshape(NPAIR)
    code = jnp.arange(NPAIR, dtype=jnp.int32)
    rank = jnp.sum((code[None, :] < code[:, None]) & named[None, :], axis=1)
    count = jnp.sum(named.astype(jnp.int32))
    wanted = jnp.minimum(code, count - 1)
    pairs = jnp.sum(jnp.where(named[None, :] & (rank[None, :] == wanted[:, None]), code[None, :], 0), axis=1)
    return pairs.astype(jnp.int32), count, jnp.sum(named[: 2 * NQ].astype(jnp.int32))


def shifted(array, axis, by, size):
    return lax.ppermute(array, axis, [(i, (i + by) % size) for i in range(size)])


def on_device(query_data, key_data, value_data, output_data, output_grad, key_lists, key_counts, block_order):
    x, y, c = lax.axis_index("x"), lax.axis_index("y"), lax.axis_index("c")

    def heads(array):
        return jnp.transpose(array.reshape(ROWS, HEADS, HD), (1, 0, 2))

    products = output_grad.astype(jnp.float32) * output_data.astype(jnp.float32)
    row_dot = jnp.transpose(jnp.sum(products.reshape(ROWS, HEADS, HD), axis=2))
    high = lax.reduce_precision(row_dot, 8, 7)
    middle = lax.reduce_precision(row_dot - high, 8, 7)
    pieces = jnp.stack([high, middle, row_dot - high - middle], axis=1).astype(jnp.bfloat16)
    pieces = jnp.pad(pieces, ((0, 0), (0, 13), (0, HD - ROWS)))
    def regrouped(*parts):
        return lax.all_to_all(jnp.concatenate(parts, axis=1), "h", 0, 0, tiled=True)

    def rows(packed, i):
        return packed[:, i * ROWS : (i + 1) * ROWS, :].reshape(BLK, HD)

    packed = regrouped(heads(query_data), heads(output_grad), pieces)
    pieces = jnp.transpose(packed[:, 2 * ROWS : 2 * ROWS + 3, :ROWS], (1, 0, 2)).reshape(12, HD)
    qd = jnp.concatenate([rows(packed, 0), rows(packed, 1), pieces, jnp.zeros((4, HD), jnp.bfloat16)], axis=0)
    packed = regrouped(heads(key_data), heads(value_data))
    kv = jnp.concatenate([rows(packed, 0), rows(packed, 1)], axis=0)

    pairs, count, early = pair_list(key_lists, key_counts, block_order, x, y, c)
    meta = jnp.stack([count, y, c, early]).astype(jnp.int32)

    own = jnp.stack([qd] + [shifted(qd, "y", i, NY) for i in range(1, NY)])
    queries = (own, shifted(own, "c", 1, NC))
    keys = tuple(shifted(kv, "x", i, NX) if i else kv for i in SHIFTS)

    bf16, f32 = jnp.bfloat16, jnp.float32
    shape, anywhere, vmem = jax.ShapeDtypeStruct, pl.BlockSpec(memory_space=pl.ANY), pl.BlockSpec(memory_space=pltpu.VMEM)
    square, line = shape((NPAIR, BLK, BLK), bf16), shape((NPAIR, 1, BLK), f32)
    qd_scratch, kv_scratch = pltpu.VMEM((NQ, QD_ROWS, HD), bf16), pltpu.VMEM((NK, 2 * BLK, HD), bf16)
    dma = pltpu.SemaphoreType.DMA
    probs, tops, stats = over_pairs(
        probs_kernel, pairs, meta, (*queries, *keys),
        [anywhere] * 6,
        [anywhere, vmem, vmem],
        [square, line, shape((NQ, 2, BLK), f32)],
        [qd_scratch, kv_scratch, pltpu.VMEM((2, UNROLL, BLK, BLK), bf16), dma((2,)), dma((NK,)), dma((2,))],
    )
    stats_all = lax.all_to_all(
        jnp.broadcast_to(stats[None], (NQ, NQ, 2, BLK)), ("y", "c"), 0, 0, tiled=True
    )
    dscore, dquery = over_pairs(
        dscore_kernel, pairs, meta, (*queries, *keys, probs, tops, stats),
        [anywhere] * 7 + [vmem] * 2,
        [anywhere, vmem],
        [square, shape((NQ, BLK, HD), bf16)],
        [
            qd_scratch, kv_scratch, pltpu.VMEM((NK, HD, BLK), bf16), pltpu.VMEM((NQ, HD, BLK), f32),
            pltpu.VMEM((2, UNROLL, BLK, BLK), bf16), pltpu.VMEM((2, UNROLL, BLK, BLK), bf16),
            dma((2,)), dma((NK,)), dma((2,)), dma((2,)),
        ],
    )
    dquery = lax.all_to_all(dquery, ("y", "c"), 0, 0, tiled=True)

    def key_grads(late):
        return over_pairs(
            functools.partial(key_kernel, late), pairs, meta, (*queries, probs, dscore, tops, stats_all),
            [anywhere] * 4 + [vmem] * 2,
            vmem,
            shape((2, 2, BLK, HD), bf16),
            [
                qd_scratch, pltpu.VMEM((NQ, 1, BLK), f32), pltpu.VMEM((2, 2, BLK, HD), f32),
                pltpu.VMEM((DEPTH, UNROLL, BLK, BLK), bf16), pltpu.VMEM((DEPTH, UNROLL, BLK, BLK), bf16),
                dma((2,)), dma((DEPTH, UNROLL)), dma((DEPTH, UNROLL)),
            ],
        )

    sent_first, sent_last = key_grads(False), key_grads(True)
    arrived = [shifted(sent_first[i], "x", -SHIFTS[2 + i], NX) for i in range(2)]
    arrived.append(shifted(sent_last[1], "x", -SHIFTS[1], NX))

    part = whole(2, BLK, HD)
    grads = pl.pallas_call(
        finish_kernel,
        grid_spec=pltpu.PrefetchScalarGridSpec(
            num_scalar_prefetch=1,
            grid=(1,),
            in_specs=[whole(NQ, BLK, HD), whole(NQ, NQ, 2, BLK), whole(1, 2, BLK, HD), part, part, part],
            out_specs=whole(HEADS, 3 * ROWS, HD),
        ),
        out_shape=shape((HEADS, 3 * ROWS, HD), bf16),
        compiler_params=params(),
    )(meta, dquery, stats_all, sent_last, *arrived)
    grads = lax.all_to_all(grads, "h", 0, 0, tiled=True)

    def tokens(i):
        part = grads[:, i * ROWS : (i + 1) * ROWS, :]
        return jnp.transpose(part, (1, 0, 2)).reshape(ROWS, HEADS * HD)

    return tokens(0), tokens(1), tokens(2)


def solution(mesh):
    wide = Mesh(mesh.devices.reshape(NX, NY, NC, HEADS), ("x", "y", "c", "h"))
    split = P(("x", "y", "c", "h"), None)
    return jax.shard_map(
        on_device,
        mesh=wide,
        in_specs=(split,) * 5 + (P(),) * 3,
        out_specs=(split,) * 3,
        check_vma=False,
    )
```

```python
import functools
import math

import jax
import jax.numpy as jnp
from jax import lax
from jax.experimental import pallas as pl
from jax.experimental.pallas import tpu as pltpu
from jax.sharding import Mesh, PartitionSpec as P

HD = 128
BLK = 512
HEADS = 16
ROWS = BLK // HEADS
NX, NY, NC = 4, 4, 2
NQ = NY * NC
NK = NX
NPAIR = NQ * NK
PACKED = 4 * ROWS + 16
QD_ROWS = 2 * BLK + 16
UNROLL = 4
DEPTH = 3
SCALE = 1.0 / math.sqrt(HD)
SCALE2 = SCALE * math.log2(math.e)
LOW = -1e30
MIB = 1024 * 1024


def dot(a, b, contract):
    return lax.dot_general(a, b, ((contract[:1], contract[1:]), ((), ())), preferred_element_type=jnp.float32)


def query_slot(code, meta):
    return (code & NY) | ((code + meta[1]) & (NY - 1))


def query_place(code, meta):
    slot = query_slot(code, meta)
    return (slot & (NY - 1)) * NC + (meta[2] ^ (slot // NY))


def fetch_keys(blocks, kv, sems):
    return [pltpu.make_async_copy(block, kv.at[i], sems.at[i]) for i, block in enumerate(blocks)]


def fetch_queries(own, other, qd, sems):
    return [
        pltpu.make_async_copy(own, qd.at[pl.ds(0, NY)], sems.at[0]),
        pltpu.make_async_copy(other, qd.at[pl.ds(NY, NY)], sems.at[1]),
    ]


def probs_kernel(
    pairs, meta, own, other, kv0, kv1, kv2, kv3, probs, tops, stats, qd, kv, held, sems, key_sems, out_sems
):
    fetches = fetch_queries(own, other, qd, sems) + fetch_keys((kv0, kv1, kv2, kv3), kv, key_sems)
    for fetch in fetches:
        fetch.start()
    stats[:, 0, :] = jnp.full((NQ, BLK), LOW, jnp.float32)
    stats[:, 1, :] = jnp.zeros((NQ, BLK), jnp.float32)
    for fetch in fetches:
        fetch.wait()
    count = meta[0]
    steps = (count + UNROLL - 1) // UNROLL

    def store(step):
        return pltpu.make_async_copy(
            held.at[step & 1], probs.at[pl.ds(step * UNROLL, UNROLL)], out_sems.at[step & 1]
        )

    def visit(step, first):
        @pl.when(step >= 2)
        def _():
            store(step).wait()

        found = []
        for u in range(UNROLL):
            code = pairs[step * UNROLL + u]
            scores = dot(kv[code // NQ, :BLK, :], qd[query_slot(code, meta), :BLK, :], (1, 1))
            if first and u == 0:
                key_row = lax.broadcasted_iota(jnp.int32, scores.shape, 0)
                query_row = lax.broadcasted_iota(jnp.int32, scores.shape, 1)
                scores = jnp.where(key_row <= query_row, scores, LOW)
            found.append((scores, jnp.max(scores, axis=0, keepdims=True) * SCALE2))
        for u, (scores, top) in enumerate(found):
            t = step * UNROLL + u
            place = query_place(pairs[t], meta)
            values = jnp.exp2(scores * SCALE2 - top)
            total = jnp.sum(values, axis=0, keepdims=True)
            held[step & 1, u] = values.astype(jnp.bfloat16)
            tops[t] = top
            top = jnp.where(t < count, top, LOW)
            total = jnp.where(t < count, total, 0.0)
            old_top, old_total = stats[place, 0:1, :], stats[place, 1:2, :]
            new_top = jnp.maximum(old_top, top)
            stats[place, 0:1, :] = new_top
            stats[place, 1:2, :] = old_total * jnp.exp2(old_top - new_top) + total * jnp.exp2(top - new_top)
        store(step).start()

    visit(0, True)

    def body(step, _):
        visit(step, False)
        return 0

    lax.fori_loop(1, steps, body, 0)
    store(steps - 1).wait()

    @pl.when(steps >= 2)
    def _():
        store(steps - 2).wait()


def dscore_kernel(
    pairs, meta, own, other, kv0, kv1, kv2, kv3, probs, tops, stats, dscore, dquery,
    qd, kv, keys_t, total, read, held, dquery_held, sems, key_sems, in_sems, out_sems, dquery_sems,
):
    count = meta[0]
    steps = (count + UNROLL - 1) // UNROLL

    def load(step):
        return pltpu.make_async_copy(
            probs.at[pl.ds(step * UNROLL, UNROLL)], read.at[step & 1], in_sems.at[step & 1]
        )

    def store(step):
        return pltpu.make_async_copy(
            held.at[step & 1], dscore.at[pl.ds(step * UNROLL, UNROLL)], out_sems.at[step & 1]
        )

    key_fetches = fetch_keys((kv0, kv1, kv2, kv3), kv, key_sems)
    fetches = fetch_queries(own, other, qd, sems)
    for fetch in key_fetches + fetches:
        fetch.start()
    load(0).start()
    total[...] = jnp.zeros_like(total)
    for i, fetch in enumerate(key_fetches):
        fetch.wait()
        keys_t[i] = jnp.transpose(kv[i, :BLK, :])
    for fetch in fetches:
        fetch.wait()

    def body(step, _):
        load(step).wait()

        @pl.when(step + 1 < steps)
        def _():
            load(step + 1).start()

        @pl.when(step >= 2)
        def _():
            store(step).wait()

        for u in range(UNROLL):
            t = step * UNROLL + u
            code = pairs[t]
            place, key, query = query_place(code, meta), code // NQ, query_slot(code, meta)
            pieces = qd[query, 2 * BLK :, :].astype(jnp.float32)
            row_dot = pieces[0:4] + pieces[4:8] + pieces[8:12]
            row_dot = jnp.concatenate([row_dot[i : i + 1] for i in range(4)], axis=1)
            weight = jnp.where(t < count, jnp.exp2(tops[t] - stats[place, 0:1, :]), 0.0)
            dprob = dot(kv[key, BLK:, :], qd[query, BLK : 2 * BLK, :], (1, 1))
            low = (read[step & 1, u].astype(jnp.float32) * (dprob - row_dot)).astype(jnp.bfloat16)
            held[step & 1, u] = low
            total[place] += dot(keys_t[key], low, (1, 0)) * weight
        store(step).start()
        return 0

    lax.fori_loop(0, steps, body, 0)
    sent = [pltpu.make_async_copy(dquery_held.at[i], dquery.at[i], dquery_sems.at[i]) for i in range(NQ)]
    for i in range(NQ):
        dquery_held[i] = jnp.transpose(total[i]).astype(jnp.bfloat16)
        sent[i].start()
    for copy in sent:
        copy.wait()
    store(steps - 1).wait()

    @pl.when(steps >= 2)
    def _():
        store(steps - 2).wait()


def log_norms(stats_all):
    tops, sums = stats_all[:, :, 0, :], stats_all[:, :, 1, :]
    top = jnp.max(tops, axis=0)
    return top + jnp.log2(jnp.sum(sums * jnp.exp2(tops - top[None]), axis=0))


def key_kernel(
    late, pairs, meta, own, other, probs, dscore, tops, stats_all, out0, out1,
    qd, norms, total, held, p_read, d_read, sems, p_sems, d_sems, out_sems,
):
    begin, end = (0, meta[3]) if late else (meta[3], meta[0])
    steps = (end - begin + UNROLL - 1) // UNROLL

    def loads(step):
        slot = lax.rem(step, DEPTH)
        copies = []
        for u in range(UNROLL):
            t = jnp.minimum(begin + step * UNROLL + u, end - 1)
            copies.append(pltpu.make_async_copy(probs.at[t], p_read.at[slot, u], p_sems.at[slot, u]))
            copies.append(pltpu.make_async_copy(dscore.at[t], d_read.at[slot, u], d_sems.at[slot, u]))
        return copies

    def prefetch(step):
        @pl.when(step < steps)
        def _():
            for copy in loads(step):
                copy.start()

    fetches = fetch_queries(own, other, qd, sems)
    for fetch in fetches:
        fetch.start()
    for step in range(DEPTH - 1):
        prefetch(step)
    total[...] = jnp.zeros_like(total)
    norms[:, 0, :] = log_norms(stats_all[...])
    for fetch in fetches:
        fetch.wait()

    def body(step, _):
        slot = lax.rem(step, DEPTH)
        for copy in loads(step):
            copy.wait()
        prefetch(step + DEPTH - 1)
        found = []
        for u in range(UNROLL):
            t = begin + step * UNROLL + u
            code = pairs[jnp.minimum(t, end - 1)]
            place, key, query = query_place(code, meta), code // NQ, query_slot(code, meta)
            weight = jnp.where(t < end, jnp.exp2(tops[jnp.minimum(t, end - 1)] - norms[place]), 0.0)
            weight = jnp.transpose(jnp.broadcast_to(weight, (HD, BLK)))
            queries = (qd[query, :BLK, :].astype(jnp.float32) * (weight * SCALE)).astype(jnp.bfloat16)
            grads = (qd[query, BLK : 2 * BLK, :].astype(jnp.float32) * weight).astype(jnp.bfloat16)
            found.append((key & 1, dot(d_read[slot, u], queries, (1, 0)), dot(p_read[slot, u], grads, (1, 0))))
        for key, key_part, value_part in found:
            total[key, 0] += key_part
            total[key, 1] += value_part
        return 0

    lax.fori_loop(0, steps, body, 0)
    sent = [pltpu.make_async_copy(held.at[i], out, out_sems.at[i]) for i, out in enumerate((out0, out1))]
    for i in range(2):
        held[i] = total[i].astype(jnp.bfloat16)
        sent[i].start()
    for copy in sent:
        copy.wait()


def pack_kernel(query, key, value, output, grad, out):
    lane = lax.broadcasted_iota(jnp.int32, (ROWS, HD), 1)
    row_dot = jnp.zeros((ROWS, HD), jnp.float32)
    for h in range(HEADS):
        part = slice(h * HD, (h + 1) * HD)
        for i, array in enumerate((query, grad, key, value)):
            out[h, i * ROWS : (i + 1) * ROWS, :] = array[:, part]
        products = grad[:, part].astype(jnp.float32) * output[:, part].astype(jnp.float32)
        row_dot = jnp.where(lane == h, jnp.sum(products, axis=1, keepdims=True), row_dot)
    row_dot = jnp.concatenate([row_dot, jnp.zeros((HD - ROWS, HD), jnp.float32)], axis=0)
    row_dot = jnp.transpose(row_dot)[:HEADS]
    high = row_dot.astype(jnp.bfloat16).astype(jnp.float32)
    middle = (row_dot - high).astype(jnp.bfloat16).astype(jnp.float32)
    row = lax.broadcasted_iota(jnp.int32, (HEADS, 16, HD), 1)
    pieces = jnp.zeros((HEADS, 16, HD), jnp.float32)
    for i, piece in enumerate((high, middle, row_dot - high - middle)):
        pieces = jnp.where(row == i, piece[:, None, :], pieces)
    out[:, 4 * ROWS :, :] = pieces.astype(jnp.bfloat16)


def finish_kernel(meta, dquery_in, stats_in, own_in, first, second, third, out, dquery, stats_all, parts, sems):
    fetches = [
        pltpu.make_async_copy(source, parts.at[i], sems.at[i])
        for i, source in enumerate((own_in, first, second, third))
    ]
    fetches.append(pltpu.make_async_copy(stats_in, stats_all, sems.at[4]))
    fetches.append(pltpu.make_async_copy(dquery_in, dquery, sems.at[5]))
    for fetch in fetches:
        fetch.start()
    for fetch in fetches[:4]:
        fetch.wait()
    for i in range(2):
        grad = (parts[0, i].astype(jnp.float32) + parts[1, i].astype(jnp.float32)) + (
            parts[2, i].astype(jnp.float32) + parts[3, i].astype(jnp.float32)
        )
        out[:, (i + 1) * ROWS : (i + 2) * ROWS, :] = grad.astype(jnp.bfloat16).reshape(HEADS, ROWS, HD)
    for fetch in fetches[4:]:
        fetch.wait()
    place = meta[1] * NC + meta[2]
    tops, sums = stats_all[:, place, 0, :], stats_all[:, place, 1, :]
    top = jnp.max(tops, axis=0, keepdims=True)
    norm = top + jnp.log2(jnp.sum(sums * jnp.exp2(tops - top), axis=0, keepdims=True))
    weight = jnp.transpose(jnp.exp2(tops - norm) * SCALE)
    query_grad = dquery[0].astype(jnp.float32) * weight[:, 0:1]
    for i in range(1, NQ):
        query_grad += dquery[i].astype(jnp.float32) * weight[:, i : i + 1]
    out[:, 0:ROWS, :] = query_grad.astype(jnp.bfloat16).reshape(HEADS, ROWS, HD)


def in_hbm(array):
    return pltpu.with_memory_space_constraint(array, pltpu.HBM)


def params(mib):
    return pltpu.CompilerParams(vmem_limit_bytes=mib * MIB)


def over_pairs(kernel, mib, pairs, meta, operands, in_specs, out_specs, out_shape, scratch):
    return pl.pallas_call(
        kernel,
        grid_spec=pltpu.PrefetchScalarGridSpec(
            num_scalar_prefetch=2,
            grid=(1,),
            in_specs=in_specs,
            out_specs=out_specs,
            scratch_shapes=scratch,
        ),
        out_shape=out_shape,
        compiler_params=params(mib),
    )(pairs, meta, *operands)


def pair_list(key_lists, key_counts, block_order, x, y, c):
    slot = jnp.arange(NQ, dtype=jnp.int32)
    query_at = x * NQ + ((y + slot) % NY) * NC + (c ^ (slot // NY))
    key_at = ((x - jnp.arange(NK, dtype=jnp.int32)) % NX) * NQ + y * NC + c
    query_blocks, key_blocks = block_order[query_at], block_order[key_at]
    lists, counts = key_lists[query_blocks], key_counts[query_blocks]
    used = jnp.arange(key_lists.shape[1], dtype=jnp.int32)[None, :] < counts[:, None]
    named = jnp.any((lists[None, :, :] == key_blocks[:, None, None]) & used[None, :, :], axis=2)
    named = named.reshape(NPAIR)
    code = jnp.arange(NPAIR, dtype=jnp.int32)
    rank = jnp.sum((code[None, :] < code[:, None]) & named[None, :], axis=1)
    count = jnp.sum(named.astype(jnp.int32))
    wanted = jnp.minimum(code, count - 1)
    pairs = jnp.sum(jnp.where(named[None, :] & (rank[None, :] == wanted[:, None]), code[None, :], 0), axis=1)
    return pairs.astype(jnp.int32), count, jnp.sum(named[: 2 * NQ].astype(jnp.int32))


def shifted(array, axis, by, size):
    return lax.ppermute(array, axis, [(i, (i + by) % size) for i in range(size)])


def on_device(query_data, key_data, value_data, output_data, output_grad, key_lists, key_counts, block_order):
    x, y, c = lax.axis_index("x"), lax.axis_index("y"), lax.axis_index("c")

    bf16, f32 = jnp.bfloat16, jnp.float32
    shape, vmem = jax.ShapeDtypeStruct, pl.BlockSpec(memory_space=pltpu.VMEM)
    anywhere = pl.BlockSpec(memory_space=pltpu.HBM)
    dma = pltpu.SemaphoreType.DMA

    packed = pl.pallas_call(
        pack_kernel,
        in_specs=[vmem] * 5,
        out_specs=vmem,
        out_shape=shape((HEADS, PACKED, HD), bf16),
        compiler_params=params(8),
    )(query_data, key_data, value_data, output_data, output_grad)
    packed = lax.all_to_all(packed, "h", 0, 0, tiled=True)

    def rows(i):
        return packed[:, i * ROWS : (i + 1) * ROWS, :].reshape(BLK, HD)

    pieces = jnp.transpose(packed[:, 4 * ROWS : 4 * ROWS + 3, :ROWS], (1, 0, 2)).reshape(12, HD)
    qd = jnp.concatenate([rows(0), rows(1), pieces, jnp.zeros((4, HD), bf16)], axis=0)
    kv = jnp.concatenate([rows(2), rows(3)], axis=0)

    pairs, count, early = pair_list(key_lists, key_counts, block_order, x, y, c)
    meta = jnp.stack([count, y, c, early]).astype(jnp.int32)

    own = lax.all_to_all(jnp.broadcast_to(qd[None], (NY, *qd.shape)), "y", 0, 0, tiled=True)
    keys = (kv, *(shifted(kv, "x", i, NX) for i in range(1, NX)))
    own, *keys = lax.optimization_barrier((own, *keys))
    queries = (own, shifted(own, "c", 1, NC))

    square, line = pltpu.HBM((NPAIR, BLK, BLK), bf16), shape((NPAIR, 1, BLK), f32)
    qd_scratch, kv_scratch = pltpu.VMEM((NQ, QD_ROWS, HD), bf16), pltpu.VMEM((NK, 2 * BLK, HD), bf16)
    probs, tops, stats = over_pairs(
        probs_kernel, 28, pairs, meta, (*queries, *keys),
        [anywhere] * 6,
        [anywhere, vmem, vmem],
        [square, line, shape((NQ, 2, BLK), f32)],
        [qd_scratch, kv_scratch, pltpu.VMEM((2, UNROLL, BLK, BLK), bf16), dma((2,)), dma((NK,)), dma((2,))],
    )
    stats_all = lax.all_to_all(
        jnp.broadcast_to(stats[None], (NQ, NQ, 2, BLK)), ("y", "c"), 0, 0, tiled=True
    )
    dscore, dquery = over_pairs(
        dscore_kernel, 32, pairs, meta, (*queries, *keys, in_hbm(probs), tops, stats),
        [anywhere] * 7 + [vmem] * 2,
        [anywhere, anywhere],
        [square, pltpu.HBM((NQ, BLK, HD), bf16)],
        [
            qd_scratch, kv_scratch, pltpu.VMEM((NK, HD, BLK), bf16), pltpu.VMEM((NQ, HD, BLK), f32),
            pltpu.VMEM((2, UNROLL, BLK, BLK), bf16), pltpu.VMEM((2, UNROLL, BLK, BLK), bf16),
            pltpu.VMEM((NQ, BLK, HD), bf16), dma((2,)), dma((NK,)), dma((2,)), dma((2,)), dma((NQ,)),
        ],
    )
    dquery = lax.all_to_all(dquery, ("y", "c"), 0, 0, tiled=True)

    def key_grads(late, pairs):
        return over_pairs(
            functools.partial(key_kernel, late), 40, pairs, meta, (*queries, in_hbm(probs), in_hbm(dscore), tops, stats_all),
            [anywhere] * 4 + [vmem] * 2,
            [anywhere] * 2,
            [pltpu.HBM((2, BLK, HD), bf16)] * 2,
            [
                qd_scratch, pltpu.VMEM((NQ, 1, BLK), f32), pltpu.VMEM((2, 2, BLK, HD), f32),
                pltpu.VMEM((2, 2, BLK, HD), bf16),
                pltpu.VMEM((DEPTH, UNROLL, BLK, BLK), bf16), pltpu.VMEM((DEPTH, UNROLL, BLK, BLK), bf16),
                dma((2,)), dma((DEPTH, UNROLL)), dma((DEPTH, UNROLL)), dma((2,)),
            ],
        )

    second, third = key_grads(False, pairs)
    second, third, pairs = lax.optimization_barrier((second, third, pairs))
    kept, first = key_grads(True, pairs)
    arrived = [shifted(grad, "x", -i - 1, NX) for i, grad in enumerate((first, second, third))]

    grads = pl.pallas_call(
        finish_kernel,
        grid_spec=pltpu.PrefetchScalarGridSpec(
            num_scalar_prefetch=1,
            grid=(1,),
            in_specs=[anywhere] * 6,
            out_specs=vmem,
            scratch_shapes=[
                pltpu.VMEM((NQ, BLK, HD), bf16), pltpu.VMEM((NQ, NQ, 2, BLK), f32),
                pltpu.VMEM((NK, 2, BLK, HD), bf16), dma((6,)),
            ],
        ),
        out_shape=shape((HEADS, 3 * ROWS, HD), bf16),
        compiler_params=params(12),
    )(meta, dquery, stats_all, in_hbm(kept), in_hbm(arrived[0]), *arrived[1:])
    grads = lax.all_to_all(grads, "h", 0, 0, tiled=True)

    def tokens(i):
        part = grads[:, i * ROWS : (i + 1) * ROWS, :]
        return jnp.transpose(part, (1, 0, 2)).reshape(ROWS, HEADS * HD)

    return tokens(0), tokens(1), tokens(2)


def solution(mesh):
    wide = Mesh(mesh.devices.reshape(NX, NY, NC, HEADS), ("x", "y", "c", "h"))
    split = P(("x", "y", "c", "h"), None)
    return jax.shard_map(
        on_device,
        mesh=wide,
        in_specs=(split,) * 5 + (P(),) * 3,
        out_specs=(split,) * 3,
        check_vma=False,
    )
```

```python
import functools
import math

import jax
import jax.numpy as jnp
from jax import lax
from jax.experimental import pallas as pl
from jax.experimental.pallas import tpu as pltpu
from jax.sharding import Mesh, PartitionSpec as P

HD = 128
BLK = 512
HEADS = 16
ROWS = BLK // HEADS
NX, NY, NC = 4, 4, 2
NQ = NY * NC
NK = NX
NPAIR = NQ * NK
PACKED = 4 * ROWS + 16
QD_ROWS = 2 * BLK + 16
UNROLL = 4
SCALE = 1.0 / math.sqrt(HD)
SCALE2 = SCALE * math.log2(math.e)
LOW = -1e30
MIB = 1024 * 1024


def dot(a, b, contract):
    return lax.dot_general(a, b, ((contract[:1], contract[1:]), ((), ())), preferred_element_type=jnp.float32)


def query_slot(code, meta):
    return (code & NY) | ((code + meta[1]) & (NY - 1))


def query_place(code, meta):
    slot = query_slot(code, meta)
    return (slot & (NY - 1)) * NC + (meta[2] ^ (slot // NY))


def fetch_keys(blocks, kv, sems):
    return [pltpu.make_async_copy(block, kv.at[i], sems.at[i]) for i, block in enumerate(blocks)]


def fetch_queries(own, other, qd, sems):
    return [
        pltpu.make_async_copy(own, qd.at[pl.ds(0, NY)], sems.at[0]),
        pltpu.make_async_copy(other, qd.at[pl.ds(NY, NY)], sems.at[1]),
    ]


def probs_kernel(
    pairs, meta, own, other, kv0, kv1, kv2, kv3, probs, tops, copies, qd, kv, stats, held, sems, key_sems, out_sems, copy_sems
):
    fetches = fetch_queries(own, other, qd, sems) + fetch_keys((kv0, kv1, kv2, kv3), kv, key_sems)
    for fetch in fetches:
        fetch.start()
    stats[:, 0, :] = jnp.full((NQ, BLK), LOW, jnp.float32)
    stats[:, 1, :] = jnp.zeros((NQ, BLK), jnp.float32)
    for fetch in fetches:
        fetch.wait()
    count = meta[0]
    steps = (count + UNROLL - 1) // UNROLL

    def store(step):
        return pltpu.make_async_copy(
            held.at[step & 1], probs.at[pl.ds(step * UNROLL, UNROLL)], out_sems.at[step & 1]
        )

    def visit(step, first):
        @pl.when(step >= 2)
        def _():
            store(step - 2).wait()

        found = []
        for u in range(UNROLL):
            code = pairs[step * UNROLL + u]
            scores = dot(kv[code // NQ, :BLK, :], qd[query_slot(code, meta), :BLK, :], (1, 1))
            if first and u == 0:
                key_row = lax.broadcasted_iota(jnp.int32, scores.shape, 0)
                query_row = lax.broadcasted_iota(jnp.int32, scores.shape, 1)
                scores = jnp.where(key_row <= query_row, scores, LOW)
            found.append((scores, jnp.max(scores, axis=0, keepdims=True) * SCALE2))
        for u, (scores, top) in enumerate(found):
            t = step * UNROLL + u
            place = query_place(pairs[t], meta)
            values = jnp.exp2(scores * SCALE2 - top)
            total = jnp.sum(values, axis=0, keepdims=True)
            held[step & 1, u] = values.astype(jnp.bfloat16)
            tops[t] = top
            top = jnp.where(t < count, top, LOW)
            total = jnp.where(t < count, total, 0.0)
            old_top, old_total = stats[place, 0:1, :], stats[place, 1:2, :]
            new_top = jnp.maximum(old_top, top)
            stats[place, 0:1, :] = new_top
            stats[place, 1:2, :] = old_total * jnp.exp2(old_top - new_top) + total * jnp.exp2(top - new_top)
        store(step).start()

    visit(0, True)

    def body(step, _):
        visit(step, False)
        return 0

    lax.fori_loop(1, steps, body, 0)
    sent = [pltpu.make_async_copy(stats, copies.at[i], copy_sems.at[i]) for i in range(NQ)]
    for copy in sent:
        copy.start()
    for copy in sent:
        copy.wait()
    store(steps - 1).wait()

    @pl.when(steps >= 2)
    def _():
        store(steps - 2).wait()


def dscore_kernel(
    pairs, meta, own, other, kv0, kv1, kv2, kv3, probs_in, stats_in, tops, dscore, dquery,
    qd, kv, keys_t, total, stats, probs, held, dquery_held, sems, key_sems, in_sems, out_sems, dquery_sems,
):
    count = meta[0]
    steps = (count + UNROLL - 1) // UNROLL

    def load(step):
        span = pl.ds(step * UNROLL, UNROLL)
        return pltpu.make_async_copy(probs_in.at[span], probs.at[span], in_sems.at[step])

    def store(step):
        return pltpu.make_async_copy(
            held.at[step & 1], dscore.at[pl.ds(step * UNROLL, UNROLL)], out_sems.at[step & 1]
        )

    key_fetches = fetch_keys((kv0, kv1, kv2, kv3), kv, key_sems)
    fetches = fetch_queries(own, other, qd, sems)
    fetches.append(pltpu.make_async_copy(stats_in.at[0], stats, sems.at[2]))
    for fetch in key_fetches + fetches:
        fetch.start()

    def start(step, _):
        load(step).start()
        return 0

    lax.fori_loop(0, steps, start, 0)
    total[...] = jnp.zeros_like(total)
    for i, fetch in enumerate(key_fetches):
        fetch.wait()
        keys_t[i] = jnp.transpose(kv[i, :BLK, :])
    for fetch in fetches:
        fetch.wait()

    def body(step, _):
        load(step).wait()

        @pl.when(step >= 2)
        def _():
            store(step - 2).wait()

        found = []
        for u in range(UNROLL):
            t = step * UNROLL + u
            code = pairs[t]
            place, key, query = query_place(code, meta), code // NQ, query_slot(code, meta)
            pieces = qd[query, 2 * BLK :, :].astype(jnp.float32)
            row_dot = pieces[0:4] + pieces[4:8] + pieces[8:12]
            row_dot = jnp.concatenate([row_dot[i : i + 1] for i in range(4)], axis=1)
            weight = jnp.where(t < count, jnp.exp2(tops[t] - stats[place, 0:1, :]), 0.0)
            dprob = dot(kv[key, BLK:, :], qd[query, BLK : 2 * BLK, :], (1, 1))
            low = (probs[t].astype(jnp.float32) * (dprob - row_dot)).astype(jnp.bfloat16)
            held[step & 1, u] = low
            found.append((place, dot(keys_t[key], low, (1, 0)) * weight))
        for place, part in found:
            total[place] += part
        store(step).start()
        return 0

    lax.fori_loop(0, steps, body, 0)
    sent = [pltpu.make_async_copy(dquery_held.at[i], dquery.at[i], dquery_sems.at[i]) for i in range(NQ)]
    for i in range(NQ):
        dquery_held[i] = jnp.transpose(total[i]).astype(jnp.bfloat16)
        sent[i].start()
    for copy in sent:
        copy.wait()
    store(steps - 1).wait()

    @pl.when(steps >= 2)
    def _():
        store(steps - 2).wait()


def log_norms(stats_all):
    tops, sums = stats_all[:, :, 0, :], stats_all[:, :, 1, :]
    top = jnp.max(tops, axis=0)
    return top + jnp.log2(jnp.sum(sums * jnp.exp2(tops - top[None]), axis=0))


def key_kernel(pairs, meta, own, other, probs_in, dscore_in, tops, stats_all, *rest):
    *outs, qd, norms, total, kept, probs, dscore, sems, probs_sems, dscore_sems = rest
    count = meta[0]
    steps = (count + UNROLL - 1) // UNROLL

    def loads(step):
        span = pl.ds(step * UNROLL, UNROLL)
        return (
            pltpu.make_async_copy(dscore_in.at[span], dscore.at[span], dscore_sems.at[step]),
            pltpu.make_async_copy(probs_in.at[span], probs.at[span], probs_sems.at[step]),
        )

    def start(step, _):
        for copy in loads(step):
            copy.start()
        return 0

    fetches = fetch_queries(own, other, qd, sems)
    for fetch in fetches:
        fetch.start()
    lax.fori_loop(0, steps, start, 0)
    total[...] = jnp.zeros_like(total)
    norms[:, 0, :] = log_norms(stats_all[...])
    for fetch in fetches:
        fetch.wait()

    def body(step, _):
        for copy in loads(step):
            copy.wait()
        found = []
        for u in range(UNROLL):
            t = step * UNROLL + u
            code = pairs[t]
            place, key, query = query_place(code, meta), code // NQ, query_slot(code, meta)
            weight = jnp.where(t < count, jnp.exp2(tops[t] - norms[place]), 0.0)
            weight = jnp.transpose(jnp.broadcast_to(weight, (HD, BLK)))
            queries = (qd[query, :BLK, :].astype(jnp.float32) * (weight * SCALE)).astype(jnp.bfloat16)
            grads = (qd[query, BLK : 2 * BLK, :].astype(jnp.float32) * weight).astype(jnp.bfloat16)
            found.append((key, dot(dscore[t], queries, (1, 0)), dot(probs[t], grads, (1, 0))))
        for key, key_part, value_part in found:
            total[key, 0] += key_part
            total[key, 1] += value_part
        return 0

    lax.fori_loop(0, steps, body, 0)
    kept[...] = total[0].astype(jnp.bfloat16)
    sent = pltpu.make_async_copy(kept, outs[0], sems.at[2])
    sent.start()
    for i, out in enumerate(outs[1:]):
        out[...] = total[i + 1].astype(jnp.bfloat16)
    sent.wait()


def pack_kernel(query_in, key_in, value_in, output_in, grad_in, out, held, sems):
    fetches = [
        pltpu.make_async_copy(source, held.at[i], sems.at[i])
        for i, source in enumerate((query_in, key_in, value_in, output_in, grad_in))
    ]
    for fetch in fetches:
        fetch.start()
    for fetch in fetches:
        fetch.wait()
    query, key, value, output, grad = (held.at[i] for i in range(5))
    lane = lax.broadcasted_iota(jnp.int32, (ROWS, HD), 1)
    row_dot = jnp.zeros((ROWS, HD), jnp.float32)
    for h in range(HEADS):
        part = slice(h * HD, (h + 1) * HD)
        for i, array in enumerate((query, grad, key, value)):
            out[h, i * ROWS : (i + 1) * ROWS, :] = array[:, part]
        products = grad[:, part].astype(jnp.float32) * output[:, part].astype(jnp.float32)
        row_dot = jnp.where(lane == h, jnp.sum(products, axis=1, keepdims=True), row_dot)
    row_dot = jnp.concatenate([row_dot, jnp.zeros((HD - ROWS, HD), jnp.float32)], axis=0)
    row_dot = jnp.transpose(row_dot)[:HEADS]
    high = row_dot.astype(jnp.bfloat16).astype(jnp.float32)
    middle = (row_dot - high).astype(jnp.bfloat16).astype(jnp.float32)
    row = lax.broadcasted_iota(jnp.int32, (HEADS, 16, HD), 1)
    pieces = jnp.zeros((HEADS, 16, HD), jnp.float32)
    for i, piece in enumerate((high, middle, row_dot - high - middle)):
        pieces = jnp.where(row == i, piece[:, None, :], pieces)
    out[:, 4 * ROWS :, :] = pieces.astype(jnp.bfloat16)


def finish_kernel(meta, dquery_in, stats_in, own_in, first, second, third, out, dquery, stats_all, parts, sems):
    fetches = [
        pltpu.make_async_copy(source, parts.at[i], sems.at[i])
        for i, source in enumerate((own_in, first, second, third))
    ]
    fetches.append(pltpu.make_async_copy(stats_in, stats_all, sems.at[4]))
    fetches.append(pltpu.make_async_copy(dquery_in, dquery, sems.at[5]))
    for fetch in fetches:
        fetch.start()
    for fetch in fetches[:4]:
        fetch.wait()
    for i in range(2):
        grad = (parts[0, i].astype(jnp.float32) + parts[1, i].astype(jnp.float32)) + (
            parts[2, i].astype(jnp.float32) + parts[3, i].astype(jnp.float32)
        )
        out[:, (i + 1) * ROWS : (i + 2) * ROWS, :] = grad.astype(jnp.bfloat16).reshape(HEADS, ROWS, HD)
    for fetch in fetches[4:]:
        fetch.wait()
    place = meta[1] * NC + meta[2]
    tops, sums = stats_all[:, place, 0, :], stats_all[:, place, 1, :]
    top = jnp.max(tops, axis=0, keepdims=True)
    norm = top + jnp.log2(jnp.sum(sums * jnp.exp2(tops - top), axis=0, keepdims=True))
    weight = jnp.transpose(jnp.exp2(tops - norm) * SCALE)
    query_grad = dquery[0].astype(jnp.float32) * weight[:, 0:1]
    for i in range(1, NQ):
        query_grad += dquery[i].astype(jnp.float32) * weight[:, i : i + 1]
    out[:, 0:ROWS, :] = query_grad.astype(jnp.bfloat16).reshape(HEADS, ROWS, HD)


def in_hbm(array):
    return pltpu.with_memory_space_constraint(array, pltpu.HBM)


def params(mib):
    return pltpu.CompilerParams(vmem_limit_bytes=mib * MIB)


def over_pairs(kernel, mib, pairs, meta, operands, in_specs, out_specs, out_shape, scratch):
    return pl.pallas_call(
        kernel,
        grid_spec=pltpu.PrefetchScalarGridSpec(
            num_scalar_prefetch=2,
            grid=(1,),
            in_specs=in_specs,
            out_specs=out_specs,
            scratch_shapes=scratch,
        ),
        out_shape=out_shape,
        compiler_params=params(mib),
    )(pairs, meta, *operands)


def pair_list(key_lists, key_counts, block_order, x, y, c):
    slot = jnp.arange(NQ, dtype=jnp.int32)
    query_at = x * NQ + ((y + slot) % NY) * NC + (c ^ (slot // NY))
    key_at = ((x - jnp.arange(NK, dtype=jnp.int32)) % NX) * NQ + y * NC + c
    query_blocks, key_blocks = block_order[query_at], block_order[key_at]
    lists, counts = key_lists[query_blocks], key_counts[query_blocks]
    used = jnp.arange(key_lists.shape[1], dtype=jnp.int32)[None, :] < counts[:, None]
    named = jnp.any((lists[None, :, :] == key_blocks[:, None, None]) & used[None, :, :], axis=2)
    named = named.reshape(NPAIR)
    code = jnp.arange(NPAIR, dtype=jnp.int32)
    rank = jnp.sum((code[None, :] < code[:, None]) & named[None, :], axis=1)
    count = jnp.sum(named.astype(jnp.int32))
    wanted = jnp.minimum(code, count - 1)
    pairs = jnp.sum(jnp.where(named[None, :] & (rank[None, :] == wanted[:, None]), code[None, :], 0), axis=1)
    return pairs.astype(jnp.int32), count


def shifted(array, axis, by, size):
    return lax.ppermute(array, axis, [(i, (i + by) % size) for i in range(size)])


def on_device(query_data, key_data, value_data, output_data, output_grad, key_lists, key_counts, block_order):
    x, y, c = lax.axis_index("x"), lax.axis_index("y"), lax.axis_index("c")

    bf16, f32 = jnp.bfloat16, jnp.float32
    shape, vmem = jax.ShapeDtypeStruct, pl.BlockSpec(memory_space=pltpu.VMEM)
    anywhere = pl.BlockSpec(memory_space=pltpu.HBM)
    dma = pltpu.SemaphoreType.DMA

    packed = pl.pallas_call(
        pack_kernel,
        in_specs=[anywhere] * 5,
        out_specs=vmem,
        out_shape=shape((HEADS, PACKED, HD), bf16),
        scratch_shapes=[pltpu.VMEM((5, ROWS, HEADS * HD), bf16), dma((5,))],
        compiler_params=params(8),
    )(*(in_hbm(array) for array in (query_data, key_data, value_data, output_data, output_grad)))
    packed = lax.all_to_all(packed, "h", 0, 0, tiled=True)
    pairs, count = pair_list(key_lists, key_counts, block_order, x, y, c)
    meta = jnp.stack([count, y, c]).astype(jnp.int32)
    packed, pairs, meta = lax.optimization_barrier((packed, pairs, meta))

    def rows(i):
        return packed[:, i * ROWS : (i + 1) * ROWS, :].reshape(BLK, HD)

    pieces = jnp.transpose(packed[:, 4 * ROWS : 4 * ROWS + 3, :ROWS], (1, 0, 2)).reshape(12, HD)
    qd = jnp.concatenate([rows(0), rows(1), pieces, jnp.zeros((4, HD), bf16)], axis=0)
    kv = jnp.concatenate([rows(2), rows(3)], axis=0)

    own = lax.all_to_all(jnp.broadcast_to(qd[None], (NY, *qd.shape)), "y", 0, 0, tiled=True)
    keys = (kv, *(shifted(kv, "x", i, NX) for i in range(1, NX)))
    own, *keys = lax.optimization_barrier((own, *keys))
    queries = (own, shifted(own, "c", 1, NC))

    square, line = pltpu.HBM((NPAIR, BLK, BLK), bf16), shape((NPAIR, 1, BLK), f32)
    qd_scratch, kv_scratch = pltpu.VMEM((NQ, QD_ROWS, HD), bf16), pltpu.VMEM((NK, 2 * BLK, HD), bf16)
    probs, tops, stats = over_pairs(
        probs_kernel, 28, pairs, meta, (*queries, *keys),
        [anywhere] * 6,
        [anywhere, vmem, anywhere],
        [square, line, pltpu.HBM((NQ, NQ, 2, BLK), f32)],
        [qd_scratch, kv_scratch, pltpu.VMEM((NQ, 2, BLK), f32), pltpu.VMEM((2, UNROLL, BLK, BLK), bf16), dma((2,)), dma((NK,)), dma((2,)), dma((NQ,))],
    )
    stats_all = lax.all_to_all(stats, ("y", "c"), 0, 0, tiled=True)
    tiles, two_steps = pltpu.VMEM((NPAIR, BLK, BLK), bf16), pltpu.VMEM((2, UNROLL, BLK, BLK), bf16)
    step_dma = dma((NPAIR // UNROLL,))
    dscore, dquery = over_pairs(
        dscore_kernel, 44, pairs, meta, (*queries, *keys, in_hbm(probs), in_hbm(stats), tops),
        [anywhere] * 8 + [vmem],
        [anywhere, anywhere],
        [square, pltpu.HBM((NQ, BLK, HD), bf16)],
        [
            qd_scratch, kv_scratch, pltpu.VMEM((NK, HD, BLK), bf16), pltpu.VMEM((NQ, HD, BLK), f32),
            pltpu.VMEM((NQ, 2, BLK), f32), tiles, two_steps, pltpu.VMEM((NQ, BLK, HD), bf16), dma((3,)), dma((NK,)), step_dma, dma((2,)), dma((NQ,)),
        ],
    )
    dquery = lax.all_to_all(dquery, ("y", "c"), 0, 0, tiled=True)

    kept, *sent = over_pairs(
        key_kernel, 50, pairs, meta, (*queries, in_hbm(probs), in_hbm(dscore), tops, stats_all),
        [anywhere] * 4 + [vmem] * 2,
        [anywhere] + [vmem] * (NK - 1),
        [pltpu.HBM((2, BLK, HD), bf16)] + [shape((2, BLK, HD), bf16)] * (NK - 1),
        [
            qd_scratch, pltpu.VMEM((NQ, 1, BLK), f32), pltpu.VMEM((NK, 2, BLK, HD), f32),
            pltpu.VMEM((2, BLK, HD), bf16), tiles, tiles, dma((3,)), step_dma, step_dma,
        ],
    )
    arrived = [shifted(grad, "x", -i - 1, NX) for i, grad in enumerate(sent)]

    grads = pl.pallas_call(
        finish_kernel,
        grid_spec=pltpu.PrefetchScalarGridSpec(
            num_scalar_prefetch=1,
            grid=(1,),
            in_specs=[anywhere] * 6,
            out_specs=vmem,
            scratch_shapes=[
                pltpu.VMEM((NQ, BLK, HD), bf16), pltpu.VMEM((NQ, NQ, 2, BLK), f32),
                pltpu.VMEM((NK, 2, BLK, HD), bf16), dma((6,)),
            ],
        ),
        out_shape=shape((HEADS, 3 * ROWS, HD), bf16),
        compiler_params=params(12),
    )(meta, dquery, stats_all, in_hbm(kept), *arrived)
    grads = lax.all_to_all(grads, "h", 0, 0, tiled=True)

    def tokens(i):
        part = grads[:, i * ROWS : (i + 1) * ROWS, :]
        return jnp.transpose(part, (1, 0, 2)).reshape(ROWS, HEADS * HD)

    return tokens(0), tokens(1), tokens(2)


def solution(mesh):
    wide = Mesh(mesh.devices.reshape(NX, NY, NC, HEADS), ("x", "y", "c", "h"))
    split = P(("x", "y", "c", "h"), None)
    return jax.shard_map(
        on_device,
        mesh=wide,
        in_specs=(split,) * 5 + (P(),) * 3,
        out_specs=(split,) * 3,
        check_vma=False,
    )
```

```python
import functools
import math

import jax
import jax.numpy as jnp
from jax import lax
from jax.experimental import pallas as pl
from jax.experimental.pallas import tpu as pltpu
from jax.sharding import Mesh, PartitionSpec as P

HD = 128
BLK = 512
HEADS = 16
ROWS = BLK // HEADS
NX, NY, NC = 4, 4, 2
NQ = NY * NC
NK = NX
NPAIR = NQ * NK
PACKED = 4 * ROWS + 8
QD_ROWS = 2 * BLK + 16
UNROLL = 4
SCALE = 1.0 / math.sqrt(HD)
SCALE2 = SCALE * math.log2(math.e)
LOW = -1e30
MIB = 1024 * 1024


def dot(a, b, contract):
    return lax.dot_general(a, b, ((contract[:1], contract[1:]), ((), ())), preferred_element_type=jnp.float32)


def query_slot(code, meta):
    return (code & NY) | ((code + meta[1]) & (NY - 1))


def query_place(code, meta):
    slot = query_slot(code, meta)
    return (slot & (NY - 1)) * NC + (meta[2] ^ (slot // NY))


def fetch_keys(blocks, kv, sems):
    return [pltpu.make_async_copy(block, kv.at[i], sems.at[i]) for i, block in enumerate(blocks)]


def fetch_queries(own, other, qd, sems):
    return [
        pltpu.make_async_copy(own, qd.at[pl.ds(0, NY)], sems.at[0]),
        pltpu.make_async_copy(other, qd.at[pl.ds(NY, NY)], sems.at[1]),
    ]


def probs_kernel(
    pairs, meta, own, other, kv0, kv1, kv2, kv3, probs, tops, copies, qd, kv, stats, held, sems, key_sems, out_sems, copy_sems
):
    fetches = fetch_queries(own, other, qd, sems) + fetch_keys((kv0, kv1, kv2, kv3), kv, key_sems)
    for fetch in fetches:
        fetch.start()
    stats[:, 0, :] = jnp.full((NQ, BLK), LOW, jnp.float32)
    stats[:, 1, :] = jnp.zeros((NQ, BLK), jnp.float32)
    for fetch in fetches:
        fetch.wait()
    count = meta[0]
    steps = (count + UNROLL - 1) // UNROLL

    def store(step):
        return pltpu.make_async_copy(
            held.at[step & 1], probs.at[pl.ds(step * UNROLL, UNROLL)], out_sems.at[step & 1]
        )

    def visit(step, first):
        @pl.when(step >= 2)
        def _():
            store(step - 2).wait()

        found = []
        for u in range(UNROLL):
            code = pairs[step * UNROLL + u]
            scores = dot(kv[code // NQ, :BLK, :], qd[query_slot(code, meta), :BLK, :], (1, 1))
            if first and u == 0:
                key_row = lax.broadcasted_iota(jnp.int32, scores.shape, 0)
                query_row = lax.broadcasted_iota(jnp.int32, scores.shape, 1)
                scores = jnp.where(key_row <= query_row, scores, LOW)
            found.append((scores, jnp.max(scores, axis=0, keepdims=True) * SCALE2))
        for u, (scores, top) in enumerate(found):
            t = step * UNROLL + u
            place = query_place(pairs[t], meta)
            values = jnp.exp2(scores * SCALE2 - top)
            total = jnp.sum(values, axis=0, keepdims=True)
            held[step & 1, u] = values.astype(jnp.bfloat16)
            tops[t] = top
            top = jnp.where(t < count, top, LOW)
            total = jnp.where(t < count, total, 0.0)
            old_top, old_total = stats[place, 0:1, :], stats[place, 1:2, :]
            new_top = jnp.maximum(old_top, top)
            stats[place, 0:1, :] = new_top
            stats[place, 1:2, :] = old_total * jnp.exp2(old_top - new_top) + total * jnp.exp2(top - new_top)
        store(step).start()

    visit(0, True)

    def body(step, _):
        visit(step, False)
        return 0

    lax.fori_loop(1, steps, body, 0)
    sent = [pltpu.make_async_copy(stats, copies.at[i], copy_sems.at[i]) for i in range(NQ)]
    for copy in sent:
        copy.start()
    for copy in sent:
        copy.wait()
    store(steps - 1).wait()

    @pl.when(steps >= 2)
    def _():
        store(steps - 2).wait()


def dscore_kernel(
    pairs, meta, own, other, kv0, kv1, kv2, kv3, probs_in, stats_in, tops, dscore, dquery,
    qd, kv, keys_t, total, stats, probs, held, dquery_held, sems, key_sems, in_sems, out_sems, dquery_sems,
):
    count = meta[0]
    steps = (count + UNROLL - 1) // UNROLL

    def load(step):
        span = pl.ds(step * UNROLL, UNROLL)
        return pltpu.make_async_copy(probs_in.at[span], probs.at[span], in_sems.at[step])

    def store(step):
        return pltpu.make_async_copy(
            held.at[step & 1], dscore.at[pl.ds(step * UNROLL, UNROLL)], out_sems.at[step & 1]
        )

    key_fetches = fetch_keys((kv0, kv1, kv2, kv3), kv, key_sems)
    fetches = fetch_queries(own, other, qd, sems)
    fetches.append(pltpu.make_async_copy(stats_in.at[0], stats, sems.at[2]))
    for fetch in key_fetches + fetches:
        fetch.start()

    def start(step, _):
        load(step).start()
        return 0

    lax.fori_loop(0, steps, start, 0)
    total[...] = jnp.zeros_like(total)
    for i, fetch in enumerate(key_fetches):
        fetch.wait()
        keys_t[i] = jnp.transpose(kv[i, :BLK, :])
    for fetch in fetches:
        fetch.wait()

    def body(step, _):
        load(step).wait()

        @pl.when(step >= 2)
        def _():
            store(step - 2).wait()

        found = []
        for u in range(UNROLL):
            t = step * UNROLL + u
            code = pairs[t]
            place, key, query = query_place(code, meta), code // NQ, query_slot(code, meta)
            pieces = qd[query, 2 * BLK :, :].astype(jnp.float32)
            row_dot = pieces[0:4] + pieces[4:8] + pieces[8:12]
            row_dot = jnp.concatenate([row_dot[i : i + 1] for i in range(4)], axis=1)
            weight = jnp.where(t < count, jnp.exp2(tops[t] - stats[place, 0:1, :]), 0.0)
            dprob = dot(kv[key, BLK:, :], qd[query, BLK : 2 * BLK, :], (1, 1))
            low = (probs[t].astype(jnp.float32) * (dprob - row_dot)).astype(jnp.bfloat16)
            held[step & 1, u] = low
            found.append((place, dot(keys_t[key], low, (1, 0)) * weight))
        for place, part in found:
            total[place] += part
        store(step).start()
        return 0

    lax.fori_loop(0, steps, body, 0)
    sent = [pltpu.make_async_copy(dquery_held.at[i], dquery.at[i], dquery_sems.at[i]) for i in range(NQ)]
    for i in range(NQ):
        dquery_held[i] = jnp.transpose(total[i]).astype(jnp.bfloat16)
        sent[i].start()
    for copy in sent:
        copy.wait()
    store(steps - 1).wait()

    @pl.when(steps >= 2)
    def _():
        store(steps - 2).wait()


def log_norms(stats_all):
    tops, sums = stats_all[:, :, 0, :], stats_all[:, :, 1, :]
    top = jnp.max(tops, axis=0)
    return top + jnp.log2(jnp.sum(sums * jnp.exp2(tops - top[None]), axis=0))


def key_kernel(late, pairs, meta, own, other, probs_in, dscore_in, tops, stats_all, *rest):
    *outs, qd, norms, total, probs, dscore, sems, probs_sems, dscore_sems = rest
    begin, end = (0, meta[3]) if late else (meta[3], meta[0])
    steps = (end - begin + UNROLL - 1) // UNROLL

    def loads(step):
        copies = []
        for u in range(UNROLL):
            t = jnp.minimum(begin + step * UNROLL + u, end - 1)
            held = step * UNROLL + u
            copies.append(pltpu.make_async_copy(dscore_in.at[t], dscore.at[held], dscore_sems.at[held]))
            copies.append(pltpu.make_async_copy(probs_in.at[t], probs.at[held], probs_sems.at[held]))
        return copies

    def start(step, _):
        for copy in loads(step):
            copy.start()
        return 0

    fetches = fetch_queries(own, other, qd, sems)
    for fetch in fetches:
        fetch.start()
    lax.fori_loop(0, steps, start, 0)
    total[...] = jnp.zeros_like(total)
    norms[:, 0, :] = log_norms(stats_all[...])
    for fetch in fetches:
        fetch.wait()

    def body(step, _):
        for copy in loads(step):
            copy.wait()
        found = []
        for u in range(UNROLL):
            held = step * UNROLL + u
            t = jnp.minimum(begin + held, end - 1)
            code = pairs[t]
            place, key, query = query_place(code, meta), code // NQ, query_slot(code, meta)
            weight = jnp.where(begin + held < end, jnp.exp2(tops[t] - norms[place]), 0.0)
            weight = jnp.transpose(jnp.broadcast_to(weight, (HD, BLK)))
            queries = (qd[query, :BLK, :].astype(jnp.float32) * (weight * SCALE)).astype(jnp.bfloat16)
            grads = (qd[query, BLK : 2 * BLK, :].astype(jnp.float32) * weight).astype(jnp.bfloat16)
            slot = 0 if late else key - 1
            found.append((slot, dot(dscore[held], queries, (1, 0)), dot(probs[held], grads, (1, 0))))
        for slot, key_part, value_part in found:
            total[slot, 0] += key_part
            total[slot, 1] += value_part
        return 0

    lax.fori_loop(0, steps, body, 0)
    for i, out in enumerate(outs):
        out[...] = total[i].astype(jnp.bfloat16)


def pack_kernel(query_in, key_in, value_in, output_in, grad_in, out, held, sems):
    fetches = [
        pltpu.make_async_copy(source, held.at[i], sems.at[i])
        for i, source in enumerate((query_in, key_in, value_in, output_in, grad_in))
    ]
    for fetch in fetches:
        fetch.start()
    for fetch in fetches:
        fetch.wait()
    query, key, value, output, grad = (held.at[i] for i in range(5))
    lane = lax.broadcasted_iota(jnp.int32, (ROWS, HD), 1)
    row_dot = jnp.zeros((ROWS, HD), jnp.float32)
    for h in range(HEADS):
        part = slice(h * HD, (h + 1) * HD)
        for i, array in enumerate((query, grad, key, value)):
            out[h, i * ROWS : (i + 1) * ROWS, :] = array[:, part]
        products = grad[:, part].astype(jnp.float32) * output[:, part].astype(jnp.float32)
        row_dot = jnp.where(lane == h, jnp.sum(products, axis=1, keepdims=True), row_dot)
    row_dot = jnp.concatenate([row_dot, jnp.zeros((HD - ROWS, HD), jnp.float32)], axis=0)
    row_dot = jnp.transpose(row_dot)[:HEADS]
    high = row_dot.astype(jnp.bfloat16).astype(jnp.float32)
    middle = (row_dot - high).astype(jnp.bfloat16).astype(jnp.float32)
    row = lax.broadcasted_iota(jnp.int32, (HEADS, 8, HD), 1)
    pieces = jnp.zeros((HEADS, 8, HD), jnp.float32)
    for i, piece in enumerate((high, middle, row_dot - high - middle)):
        pieces = jnp.where(row == i, piece[:, None, :], pieces)
    out[:, 4 * ROWS :, :] = pieces.astype(jnp.bfloat16)


def finish_queries_kernel(meta, dquery_in, stats_in, out, dquery, stats_all, sems):
    fetches = [
        pltpu.make_async_copy(stats_in, stats_all, sems.at[0]),
        pltpu.make_async_copy(dquery_in, dquery, sems.at[1]),
    ]
    for fetch in fetches:
        fetch.start()
    for fetch in fetches:
        fetch.wait()
    place = meta[1] * NC + meta[2]
    tops, sums = stats_all[:, place, 0, :], stats_all[:, place, 1, :]
    top = jnp.max(tops, axis=0, keepdims=True)
    norm = top + jnp.log2(jnp.sum(sums * jnp.exp2(tops - top), axis=0, keepdims=True))
    weight = jnp.transpose(jnp.exp2(tops - norm) * SCALE)
    grad = dquery[0].astype(jnp.float32) * weight[:, 0:1]
    for i in range(1, NQ):
        grad += dquery[i].astype(jnp.float32) * weight[:, i : i + 1]
    out[...] = grad.astype(jnp.bfloat16)


def finish_kernel(query_grad, kept, first, second, third, out, parts, query_held, sems):
    fetches = [
        pltpu.make_async_copy(source, parts.at[i], sems.at[i])
        for i, source in enumerate((kept, first, second, third))
    ]
    fetches.append(pltpu.make_async_copy(query_grad, query_held, sems.at[4]))
    for fetch in fetches:
        fetch.start()
    for fetch in fetches:
        fetch.wait()
    out[:, 0:ROWS, :] = query_held[...].reshape(HEADS, ROWS, HD)
    for i in range(2):
        grad = (parts[0, i].astype(jnp.float32) + parts[1, i].astype(jnp.float32)) + (
            parts[2, i].astype(jnp.float32) + parts[3, i].astype(jnp.float32)
        )
        out[:, (i + 1) * ROWS : (i + 2) * ROWS, :] = grad.astype(jnp.bfloat16).reshape(HEADS, ROWS, HD)


def in_hbm(array):
    return pltpu.with_memory_space_constraint(array, pltpu.HBM)


def params(mib):
    return pltpu.CompilerParams(vmem_limit_bytes=mib * MIB)


def over_pairs(kernel, mib, pairs, meta, operands, in_specs, out_specs, out_shape, scratch):
    return pl.pallas_call(
        kernel,
        grid_spec=pltpu.PrefetchScalarGridSpec(
            num_scalar_prefetch=2,
            grid=(1,),
            in_specs=in_specs,
            out_specs=out_specs,
            scratch_shapes=scratch,
        ),
        out_shape=out_shape,
        compiler_params=params(mib),
    )(pairs, meta, *operands)


def pair_list(key_lists, key_counts, block_order, x, y, c):
    slot = jnp.arange(NQ, dtype=jnp.int32)
    query_at = x * NQ + ((y + slot) % NY) * NC + (c ^ (slot // NY))
    key_at = ((x - jnp.arange(NK, dtype=jnp.int32)) % NX) * NQ + y * NC + c
    query_blocks, key_blocks = block_order[query_at], block_order[key_at]
    lists, counts = key_lists[query_blocks], key_counts[query_blocks]
    used = jnp.arange(key_lists.shape[1], dtype=jnp.int32)[None, :] < counts[:, None]
    named = jnp.any((lists[None, :, :] == key_blocks[:, None, None]) & used[None, :, :], axis=2)
    named = named.reshape(NPAIR)
    code = jnp.arange(NPAIR, dtype=jnp.int32)
    rank = jnp.sum((code[None, :] < code[:, None]) & named[None, :], axis=1)
    count = jnp.sum(named.astype(jnp.int32))
    wanted = jnp.minimum(code, count - 1)
    pairs = jnp.sum(jnp.where(named[None, :] & (rank[None, :] == wanted[:, None]), code[None, :], 0), axis=1)
    return pairs.astype(jnp.int32), count, jnp.sum(named[:NQ].astype(jnp.int32))


def shifted(array, axis, by, size):
    return lax.ppermute(array, axis, [(i, (i + by) % size) for i in range(size)])


def on_device(query_data, key_data, value_data, output_data, output_grad, key_lists, key_counts, block_order):
    x, y, c = lax.axis_index("x"), lax.axis_index("y"), lax.axis_index("c")

    bf16, f32 = jnp.bfloat16, jnp.float32
    shape, vmem = jax.ShapeDtypeStruct, pl.BlockSpec(memory_space=pltpu.VMEM)
    anywhere = pl.BlockSpec(memory_space=pltpu.HBM)
    dma = pltpu.SemaphoreType.DMA

    packed = pl.pallas_call(
        pack_kernel,
        in_specs=[anywhere] * 5,
        out_specs=vmem,
        out_shape=shape((HEADS, PACKED, HD), bf16),
        scratch_shapes=[pltpu.VMEM((5, ROWS, HEADS * HD), bf16), dma((5,))],
        compiler_params=params(8),
    )(*(in_hbm(array) for array in (query_data, key_data, value_data, output_data, output_grad)))
    packed = lax.all_to_all(packed, "h", 0, 0, tiled=True)
    pairs, count, near = pair_list(key_lists, key_counts, block_order, x, y, c)
    meta = jnp.stack([count, y, c, near]).astype(jnp.int32)
    packed, pairs, meta = lax.optimization_barrier((packed, pairs, meta))

    def rows(i):
        return packed[:, i * ROWS : (i + 1) * ROWS, :].reshape(BLK, HD)

    pieces = jnp.transpose(packed[:, 4 * ROWS : 4 * ROWS + 3, :ROWS], (1, 0, 2)).reshape(12, HD)
    qd = jnp.concatenate([rows(0), rows(1), pieces, jnp.zeros((4, HD), bf16)], axis=0)
    kv = jnp.concatenate([rows(2), rows(3)], axis=0)

    own = lax.all_to_all(jnp.broadcast_to(qd[None], (NY, *qd.shape)), "y", 0, 0, tiled=True)
    keys = (kv, *(shifted(kv, "x", i, NX) for i in range(1, NX)))
    own, *keys = lax.optimization_barrier((own, *keys))
    queries = (own, shifted(own, "c", 1, NC))

    square, line = pltpu.HBM((NPAIR, BLK, BLK), bf16), shape((NPAIR, 1, BLK), f32)
    qd_scratch, kv_scratch = pltpu.VMEM((NQ, QD_ROWS, HD), bf16), pltpu.VMEM((NK, 2 * BLK, HD), bf16)
    probs, tops, stats = over_pairs(
        probs_kernel, 28, pairs, meta, (*queries, *keys),
        [anywhere] * 6,
        [anywhere, vmem, anywhere],
        [square, line, pltpu.HBM((NQ, NQ, 2, BLK), f32)],
        [qd_scratch, kv_scratch, pltpu.VMEM((NQ, 2, BLK), f32), pltpu.VMEM((2, UNROLL, BLK, BLK), bf16), dma((2,)), dma((NK,)), dma((2,)), dma((NQ,))],
    )
    stats_all = lax.all_to_all(stats, ("y", "c"), 0, 0, tiled=True)
    tiles, two_steps = pltpu.VMEM((NPAIR, BLK, BLK), bf16), pltpu.VMEM((2, UNROLL, BLK, BLK), bf16)
    step_dma = dma((NPAIR // UNROLL,))
    dscore, dquery = over_pairs(
        dscore_kernel, 44, pairs, meta, (*queries, *keys, in_hbm(probs), in_hbm(stats), tops),
        [anywhere] * 8 + [vmem],
        [anywhere, anywhere],
        [square, pltpu.HBM((NQ, BLK, HD), bf16)],
        [
            qd_scratch, kv_scratch, pltpu.VMEM((NK, HD, BLK), bf16), pltpu.VMEM((NQ, HD, BLK), f32),
            pltpu.VMEM((NQ, 2, BLK), f32), tiles, two_steps, pltpu.VMEM((NQ, BLK, HD), bf16), dma((3,)), dma((NK,)), step_dma, dma((2,)), dma((NQ,)),
        ],
    )
    dquery = lax.all_to_all(dquery, ("y", "c"), 0, 0, tiled=True)


    def key_grads(late, pairs):
        slots = 1 if late else NK - 1
        most = slots * NQ
        held = pltpu.VMEM((most, BLK, BLK), bf16)
        return over_pairs(
            functools.partial(key_kernel, late), 50, pairs, meta,
            (*queries, in_hbm(probs), in_hbm(dscore), tops, stats_all),
            [anywhere] * 4 + [vmem] * 2,
            [vmem] * slots,
            [shape((2, BLK, HD), bf16)] * slots,
            [
                qd_scratch, pltpu.VMEM((NQ, 1, BLK), f32), pltpu.VMEM((slots, 2, BLK, HD), f32), held, held,
                dma((2,)), dma((most,)), dma((most,)),
            ],
        )

    *sent, pairs = lax.optimization_barrier((*key_grads(False, pairs), pairs))
    arrived = {i: shifted(sent[i - 1], "x", -i, NX) for i in (2, 1, 3)}
    (kept,) = key_grads(True, pairs)
    query_grad = pl.pallas_call(
        finish_queries_kernel,
        grid_spec=pltpu.PrefetchScalarGridSpec(
            num_scalar_prefetch=1,
            grid=(1,),
            in_specs=[anywhere] * 2,
            out_specs=vmem,
            scratch_shapes=[pltpu.VMEM((NQ, BLK, HD), bf16), pltpu.VMEM((NQ, NQ, 2, BLK), f32), dma((2,))],
        ),
        out_shape=shape((BLK, HD), bf16),
        compiler_params=params(12),
    )(meta, dquery, stats_all)
    grads = pl.pallas_call(
        finish_kernel,
        in_specs=[anywhere] * 5,
        out_specs=vmem,
        out_shape=shape((HEADS, 3 * ROWS, HD), bf16),
        scratch_shapes=[pltpu.VMEM((NK, 2, BLK, HD), bf16), pltpu.VMEM((BLK, HD), bf16), dma((5,))],
        compiler_params=params(12),
    )(query_grad, kept, arrived[1], arrived[2], arrived[3])
    grads = lax.all_to_all(grads, "h", 0, 0, tiled=True)

    def tokens(i):
        part = grads[:, i * ROWS : (i + 1) * ROWS, :]
        return jnp.transpose(part, (1, 0, 2)).reshape(ROWS, HEADS * HD)

    return tokens(0), tokens(1), tokens(2)


def solution(mesh):
    wide = Mesh(mesh.devices.reshape(NX, NY, NC, HEADS), ("x", "y", "c", "h"))
    split = P(("x", "y", "c", "h"), None)
    return jax.shard_map(
        on_device,
        mesh=wide,
        in_specs=(split,) * 5 + (P(),) * 3,
        out_specs=(split,) * 3,
        check_vma=False,
    )
```

```python
import functools
import math

import jax
import jax.numpy as jnp
from jax import lax
from jax.experimental import pallas as pl
from jax.experimental.pallas import tpu as pltpu
from jax.sharding import Mesh, PartitionSpec as P

HD = 128
BLK = 512
HEADS = 16
ROWS = BLK // HEADS
NX, NY, NC = 4, 4, 2
NQ = NY * NC
NK = NX
NPAIR = NQ * NK
PACKED = 4 * ROWS + 8
QD_ROWS = 2 * BLK + 16
UNROLL = 4
SCALE = 1.0 / math.sqrt(HD)
SCALE2 = SCALE * math.log2(math.e)
LOW = -1e30
MIB = 1024 * 1024


def dot(a, b, contract):
    return lax.dot_general(a, b, ((contract[:1], contract[1:]), ((), ())), preferred_element_type=jnp.float32)


def query_slot(code, meta):
    return (code & NY) | ((code + meta[1]) & (NY - 1))


def query_place(code, meta):
    slot = query_slot(code, meta)
    return (slot & (NY - 1)) * NC + (meta[2] ^ (slot // NY))


def fetch_keys(blocks, kv, sems):
    return [pltpu.make_async_copy(block, kv.at[i], sems.at[i]) for i, block in enumerate(blocks)]


def fetch_queries(own, other, qd, sems):
    return [
        pltpu.make_async_copy(own, qd.at[pl.ds(0, NY)], sems.at[0]),
        pltpu.make_async_copy(other, qd.at[pl.ds(NY, NY)], sems.at[1]),
    ]


def probs_kernel(
    pairs, meta, own, other, kv0, kv1, kv2, kv3, probs, tops, copies, qd, kv, stats, held, sems, key_sems, out_sems, copy_sems
):
    fetches = fetch_queries(own, other, qd, sems) + fetch_keys((kv0, kv1, kv2, kv3), kv, key_sems)
    for fetch in fetches:
        fetch.start()
    stats[:, 0, :] = jnp.full((NQ, BLK), LOW, jnp.float32)
    stats[:, 1, :] = jnp.zeros((NQ, BLK), jnp.float32)
    for fetch in fetches:
        fetch.wait()
    count = meta[0]
    steps = (count + UNROLL - 1) // UNROLL

    def store(step, u):
        return pltpu.make_async_copy(
            held.at[step & 1, u], probs.at[step * UNROLL + u], out_sems.at[step & 1, u]
        )

    def wait_stores(step):
        for u in range(UNROLL):
            store(step, u).wait()

    def visit(step, first):
        @pl.when(step >= 2)
        def _():
            wait_stores(step - 2)

        found = []
        for u in range(UNROLL):
            code = pairs[step * UNROLL + u]
            scores = dot(kv[code // NQ, :BLK, :], qd[query_slot(code, meta), :BLK, :], (1, 1))
            if first and u == 0:
                key_row = lax.broadcasted_iota(jnp.int32, scores.shape, 0)
                query_row = lax.broadcasted_iota(jnp.int32, scores.shape, 1)
                scores = jnp.where(key_row <= query_row, scores, LOW)
            found.append((scores, jnp.max(scores, axis=0, keepdims=True) * SCALE2))
        for u, (scores, top) in enumerate(found):
            t = step * UNROLL + u
            place = query_place(pairs[t], meta)
            values = jnp.exp2(scores * SCALE2 - top)
            total = jnp.sum(values, axis=0, keepdims=True)
            held[step & 1, u] = values.astype(jnp.bfloat16)
            store(step, u).start()
            tops[t] = top
            top = jnp.where(t < count, top, LOW)
            total = jnp.where(t < count, total, 0.0)
            old_top, old_total = stats[place, 0:1, :], stats[place, 1:2, :]
            new_top = jnp.maximum(old_top, top)
            stats[place, 0:1, :] = new_top
            stats[place, 1:2, :] = old_total * jnp.exp2(old_top - new_top) + total * jnp.exp2(top - new_top)

    visit(0, True)

    def body(step, _):
        visit(step, False)
        return 0

    lax.fori_loop(1, steps, body, 0)
    sent = [pltpu.make_async_copy(stats, copies.at[i], copy_sems.at[i]) for i in range(NQ)]
    for copy in sent:
        copy.start()
    for copy in sent:
        copy.wait()
    wait_stores(steps - 1)

    @pl.when(steps >= 2)
    def _():
        wait_stores(steps - 2)


def dscore_kernel(
    pairs, meta, own, other, kv0, kv1, kv2, kv3, probs_in, stats_in, tops, dscore, dquery,
    qd, kv, keys_t, total, stats, probs, held, dquery_held, sems, key_sems, in_sems, out_sems, dquery_sems,
):
    count = meta[0]
    steps = (count + UNROLL - 1) // UNROLL

    def load(step):
        span = pl.ds(step * UNROLL, UNROLL)
        return pltpu.make_async_copy(probs_in.at[span], probs.at[span], in_sems.at[step])

    def store(step, u):
        return pltpu.make_async_copy(
            held.at[step & 1, u], dscore.at[step * UNROLL + u], out_sems.at[step & 1, u]
        )

    def wait_stores(step):
        for u in range(UNROLL):
            store(step, u).wait()

    key_fetches = fetch_keys((kv0, kv1, kv2, kv3), kv, key_sems)
    fetches = fetch_queries(own, other, qd, sems)
    fetches.append(pltpu.make_async_copy(stats_in.at[0], stats, sems.at[2]))
    for fetch in key_fetches + fetches:
        fetch.start()

    def start(step, _):
        load(step).start()
        return 0

    lax.fori_loop(0, steps, start, 0)
    total[...] = jnp.zeros_like(total)
    for i, fetch in enumerate(key_fetches):
        fetch.wait()
        keys_t[i] = jnp.transpose(kv[i, :BLK, :])
    for fetch in fetches:
        fetch.wait()

    def body(step, _):
        load(step).wait()

        @pl.when(step >= 2)
        def _():
            wait_stores(step - 2)

        found = []
        for u in range(UNROLL):
            t = step * UNROLL + u
            code = pairs[t]
            place, key, query = query_place(code, meta), code // NQ, query_slot(code, meta)
            pieces = qd[query, 2 * BLK :, :].astype(jnp.float32)
            row_dot = pieces[0:4] + pieces[4:8] + pieces[8:12]
            row_dot = jnp.concatenate([row_dot[i : i + 1] for i in range(4)], axis=1)
            weight = jnp.where(t < count, jnp.exp2(tops[t] - stats[place, 0:1, :]), 0.0)
            dprob = dot(kv[key, BLK:, :], qd[query, BLK : 2 * BLK, :], (1, 1))
            low = (probs[t].astype(jnp.float32) * (dprob - row_dot)).astype(jnp.bfloat16)
            held[step & 1, u] = low
            store(step, u).start()
            found.append((place, dot(keys_t[key], low, (1, 0)) * weight))
        for place, part in found:
            total[place] += part
        return 0

    lax.fori_loop(0, steps, body, 0)
    sent = [pltpu.make_async_copy(dquery_held.at[i], dquery.at[i], dquery_sems.at[i]) for i in range(NQ)]
    for i in range(NQ):
        dquery_held[i] = total[i].astype(jnp.bfloat16)
        sent[i].start()
    for copy in sent:
        copy.wait()
    wait_stores(steps - 1)

    @pl.when(steps >= 2)
    def _():
        wait_stores(steps - 2)


def log_norms(stats_all):
    tops, sums = stats_all[:, :, 0, :], stats_all[:, :, 1, :]
    top = jnp.max(tops, axis=0)
    return top + jnp.log2(jnp.sum(sums * jnp.exp2(tops - top[None]), axis=0))


def key_kernel(late, pairs, meta, own, other, probs_in, dscore_in, tops, stats_all, *rest):
    *outs, qd, norms, total, probs, dscore, sems, probs_sems, dscore_sems = rest
    begin, end = (0, meta[3]) if late else (meta[3], meta[0])
    steps = (end - begin + UNROLL - 1) // UNROLL

    def loads(step):
        copies = []
        for u in range(UNROLL):
            t = jnp.minimum(begin + step * UNROLL + u, end - 1)
            held = step * UNROLL + u
            copies.append(pltpu.make_async_copy(dscore_in.at[t], dscore.at[held], dscore_sems.at[held]))
            copies.append(pltpu.make_async_copy(probs_in.at[t], probs.at[held], probs_sems.at[held]))
        return copies

    def start(step, _):
        for copy in loads(step):
            copy.start()
        return 0

    lax.fori_loop(0, jnp.minimum(steps, 1), start, 0)
    fetches = fetch_queries(own, other, qd, sems)
    for fetch in fetches:
        fetch.start()
    lax.fori_loop(1, steps, start, 0)
    total[...] = jnp.zeros_like(total)
    norms[:, 0, :] = log_norms(stats_all[...])
    for fetch in fetches:
        fetch.wait()

    def body(step, _):
        for copy in loads(step):
            copy.wait()
        found = []
        for u in range(UNROLL):
            held = step * UNROLL + u
            t = jnp.minimum(begin + held, end - 1)
            code = pairs[t]
            place, key, query = query_place(code, meta), code // NQ, query_slot(code, meta)
            weight = jnp.where(begin + held < end, jnp.exp2(tops[t] - norms[place]), 0.0)
            weight = jnp.transpose(jnp.broadcast_to(weight, (HD, BLK)))
            queries = (qd[query, :BLK, :].astype(jnp.float32) * (weight * SCALE)).astype(jnp.bfloat16)
            grads = (qd[query, BLK : 2 * BLK, :].astype(jnp.float32) * weight).astype(jnp.bfloat16)
            slot = 0 if late else key - 1
            found.append((slot, dot(dscore[held], queries, (1, 0)), dot(probs[held], grads, (1, 0))))
        for slot, key_part, value_part in found:
            total[slot, 0] += key_part
            total[slot, 1] += value_part
        return 0

    lax.fori_loop(0, steps, body, 0)
    for i, out in enumerate(outs):
        out[...] = total[i].astype(jnp.bfloat16)


def pack_kernel(query_in, key_in, value_in, output_in, grad_in, out, held, sems):
    fetches = [
        pltpu.make_async_copy(source, held.at[i], sems.at[i])
        for i, source in enumerate((query_in, key_in, value_in, output_in, grad_in))
    ]
    for fetch in fetches:
        fetch.start()
    for fetch in fetches:
        fetch.wait()
    query, key, value, output, grad = (held.at[i] for i in range(5))
    lane = lax.broadcasted_iota(jnp.int32, (ROWS, HD), 1)
    row_dot = jnp.zeros((ROWS, HD), jnp.float32)
    for h in range(HEADS):
        part = slice(h * HD, (h + 1) * HD)
        for i, array in enumerate((query, grad, key, value)):
            out[h, i * ROWS : (i + 1) * ROWS, :] = array[:, part]
        products = grad[:, part].astype(jnp.float32) * output[:, part].astype(jnp.float32)
        row_dot = jnp.where(lane == h, jnp.sum(products, axis=1, keepdims=True), row_dot)
    row_dot = jnp.concatenate([row_dot, jnp.zeros((HD - ROWS, HD), jnp.float32)], axis=0)
    row_dot = jnp.transpose(row_dot)[:HEADS]
    high = row_dot.astype(jnp.bfloat16).astype(jnp.float32)
    middle = (row_dot - high).astype(jnp.bfloat16).astype(jnp.float32)
    row = lax.broadcasted_iota(jnp.int32, (HEADS, 8, HD), 1)
    pieces = jnp.zeros((HEADS, 8, HD), jnp.float32)
    for i, piece in enumerate((high, middle, row_dot - high - middle)):
        pieces = jnp.where(row == i, piece[:, None, :], pieces)
    out[:, 4 * ROWS :, :] = pieces.astype(jnp.bfloat16)


def finish_queries_kernel(meta, dquery_in, stats_in, out, dquery, stats_all, sems):
    fetches = [
        pltpu.make_async_copy(stats_in, stats_all, sems.at[0]),
        pltpu.make_async_copy(dquery_in, dquery, sems.at[1]),
    ]
    for fetch in fetches:
        fetch.start()
    for fetch in fetches:
        fetch.wait()
    place = meta[1] * NC + meta[2]
    tops, sums = stats_all[:, place, 0, :], stats_all[:, place, 1, :]
    top = jnp.max(tops, axis=0, keepdims=True)
    norm = top + jnp.log2(jnp.sum(sums * jnp.exp2(tops - top), axis=0, keepdims=True))
    weight = jnp.exp2(tops - norm) * SCALE
    grad = dquery[0].astype(jnp.float32) * weight[0:1]
    for i in range(1, NQ):
        grad += dquery[i].astype(jnp.float32) * weight[i : i + 1]
    out[...] = jnp.transpose(grad).astype(jnp.bfloat16)


def finish_kernel(query_grad, kept, first, second, third, out, parts, query_held, sems):
    fetches = [
        pltpu.make_async_copy(source, parts.at[i], sems.at[i])
        for i, source in enumerate((kept, first, second, third))
    ]
    fetches.append(pltpu.make_async_copy(query_grad, query_held, sems.at[4]))
    for fetch in fetches:
        fetch.start()
    for fetch in fetches:
        fetch.wait()
    out[:, 0:ROWS, :] = query_held[...].reshape(HEADS, ROWS, HD)
    for i in range(2):
        grad = (parts[0, i].astype(jnp.float32) + parts[1, i].astype(jnp.float32)) + (
            parts[2, i].astype(jnp.float32) + parts[3, i].astype(jnp.float32)
        )
        out[:, (i + 1) * ROWS : (i + 2) * ROWS, :] = grad.astype(jnp.bfloat16).reshape(HEADS, ROWS, HD)


def in_hbm(array):
    return pltpu.with_memory_space_constraint(array, pltpu.HBM)


def params(mib):
    return pltpu.CompilerParams(vmem_limit_bytes=mib * MIB)


def over_pairs(kernel, mib, pairs, meta, operands, in_specs, out_specs, out_shape, scratch):
    return pl.pallas_call(
        kernel,
        grid_spec=pltpu.PrefetchScalarGridSpec(
            num_scalar_prefetch=2,
            grid=(1,),
            in_specs=in_specs,
            out_specs=out_specs,
            scratch_shapes=scratch,
        ),
        out_shape=out_shape,
        compiler_params=params(mib),
    )(pairs, meta, *operands)


def pair_list(key_lists, key_counts, block_order, x, y, c):
    slot = jnp.arange(NQ, dtype=jnp.int32)
    query_at = x * NQ + ((y + slot) % NY) * NC + (c ^ (slot // NY))
    key_at = ((x - jnp.arange(NK, dtype=jnp.int32)) % NX) * NQ + y * NC + c
    query_blocks, key_blocks = block_order[query_at], block_order[key_at]
    lists, counts = key_lists[query_blocks], key_counts[query_blocks]
    used = jnp.arange(key_lists.shape[1], dtype=jnp.int32)[None, :] < counts[:, None]
    named = jnp.any((lists[None, :, :] == key_blocks[:, None, None]) & used[None, :, :], axis=2)
    named = named.reshape(NPAIR)
    code = jnp.arange(NPAIR, dtype=jnp.int32)
    rank = jnp.sum((code[None, :] < code[:, None]) & named[None, :], axis=1)
    count = jnp.sum(named.astype(jnp.int32))
    wanted = jnp.minimum(code, count - 1)
    pairs = jnp.sum(jnp.where(named[None, :] & (rank[None, :] == wanted[:, None]), code[None, :], 0), axis=1)
    return pairs.astype(jnp.int32), count, jnp.sum(named[:NQ].astype(jnp.int32))


def shifted(array, axis, by, size):
    return lax.ppermute(array, axis, [(i, (i + by) % size) for i in range(size)])


def on_device(query_data, key_data, value_data, output_data, output_grad, key_lists, key_counts, block_order):
    x, y, c = lax.axis_index("x"), lax.axis_index("y"), lax.axis_index("c")

    bf16, f32 = jnp.bfloat16, jnp.float32
    shape, vmem = jax.ShapeDtypeStruct, pl.BlockSpec(memory_space=pltpu.VMEM)
    anywhere = pl.BlockSpec(memory_space=pltpu.HBM)
    dma = pltpu.SemaphoreType.DMA

    packed = pl.pallas_call(
        pack_kernel,
        in_specs=[anywhere] * 5,
        out_specs=vmem,
        out_shape=shape((HEADS, PACKED, HD), bf16),
        scratch_shapes=[pltpu.VMEM((5, ROWS, HEADS * HD), bf16), dma((5,))],
        compiler_params=params(8),
    )(*(in_hbm(array) for array in (query_data, key_data, value_data, output_data, output_grad)))
    packed = lax.all_to_all(packed, "h", 0, 0, tiled=True)
    pairs, count, near = pair_list(key_lists, key_counts, block_order, x, y, c)
    meta = jnp.stack([count, y, c, near]).astype(jnp.int32)
    packed, pairs, meta = lax.optimization_barrier((packed, pairs, meta))

    def rows(i):
        return packed[:, i * ROWS : (i + 1) * ROWS, :].reshape(BLK, HD)

    pieces = jnp.transpose(packed[:, 4 * ROWS : 4 * ROWS + 3, :ROWS], (1, 0, 2)).reshape(12, HD)
    qd = jnp.concatenate([rows(0), rows(1), pieces, jnp.zeros((4, HD), bf16)], axis=0)
    kv = jnp.concatenate([rows(2), rows(3)], axis=0)

    own = lax.all_to_all(jnp.broadcast_to(qd[None], (NY, *qd.shape)), "y", 0, 0, tiled=True)
    keys = (kv, *(shifted(kv, "x", i, NX) for i in range(1, NX)))
    own, *keys = lax.optimization_barrier((own, *keys))
    queries = (own, shifted(own, "c", 1, NC))

    square, line = pltpu.HBM((NPAIR, BLK, BLK), bf16), shape((NPAIR, 1, BLK), f32)
    qd_scratch, kv_scratch = pltpu.VMEM((NQ, QD_ROWS, HD), bf16), pltpu.VMEM((NK, 2 * BLK, HD), bf16)
    probs, tops, stats = over_pairs(
        probs_kernel, 28, pairs, meta, (*queries, *keys),
        [anywhere] * 6,
        [anywhere, vmem, anywhere],
        [square, line, pltpu.HBM((NQ, NQ, 2, BLK), f32)],
        [qd_scratch, kv_scratch, pltpu.VMEM((NQ, 2, BLK), f32), pltpu.VMEM((2, UNROLL, BLK, BLK), bf16), dma((2,)), dma((NK,)), dma((2, UNROLL)), dma((NQ,))],
    )
    stats_all = lax.all_to_all(stats, ("y", "c"), 0, 0, tiled=True)
    tiles, two_steps = pltpu.VMEM((NPAIR, BLK, BLK), bf16), pltpu.VMEM((2, UNROLL, BLK, BLK), bf16)
    step_dma = dma((NPAIR // UNROLL,))
    dscore, dquery = over_pairs(
        dscore_kernel, 44, pairs, meta, (*queries, *keys, in_hbm(probs), in_hbm(stats), tops),
        [anywhere] * 8 + [vmem],
        [anywhere, anywhere],
        [square, pltpu.HBM((NQ, HD, BLK), bf16)],
        [
            qd_scratch, kv_scratch, pltpu.VMEM((NK, HD, BLK), bf16), pltpu.VMEM((NQ, HD, BLK), f32),
            pltpu.VMEM((NQ, 2, BLK), f32), tiles, two_steps, pltpu.VMEM((NQ, HD, BLK), bf16), dma((3,)), dma((NK,)), step_dma, dma((2, UNROLL)), dma((NQ,)),
        ],
    )
    dquery = lax.all_to_all(dquery, ("y", "c"), 0, 0, tiled=True)


    def key_grads(late, pairs):
        slots = 1 if late else NK - 1
        most = slots * NQ
        held = pltpu.VMEM((most, BLK, BLK), bf16)
        return over_pairs(
            functools.partial(key_kernel, late), 50, pairs, meta,
            (*queries, in_hbm(probs), in_hbm(dscore), tops, stats_all),
            [anywhere] * 4 + [vmem] * 2,
            [vmem] * slots,
            [shape((2, BLK, HD), bf16)] * slots,
            [
                qd_scratch, pltpu.VMEM((NQ, 1, BLK), f32), pltpu.VMEM((slots, 2, BLK, HD), f32), held, held,
                dma((2,)), dma((most,)), dma((most,)),
            ],
        )

    *sent, pairs = lax.optimization_barrier((*key_grads(False, pairs), pairs))
    arrived = {i: shifted(sent[i - 1], "x", -i, NX) for i in (2, 1, 3)}
    (kept,) = key_grads(True, pairs)
    query_grad = pl.pallas_call(
        finish_queries_kernel,
        grid_spec=pltpu.PrefetchScalarGridSpec(
            num_scalar_prefetch=1,
            grid=(1,),
            in_specs=[anywhere] * 2,
            out_specs=vmem,
            scratch_shapes=[pltpu.VMEM((NQ, HD, BLK), bf16), pltpu.VMEM((NQ, NQ, 2, BLK), f32), dma((2,))],
        ),
        out_shape=shape((BLK, HD), bf16),
        compiler_params=params(12),
    )(meta, dquery, stats_all)
    grads = pl.pallas_call(
        finish_kernel,
        in_specs=[anywhere] * 5,
        out_specs=vmem,
        out_shape=shape((HEADS, 3 * ROWS, HD), bf16),
        scratch_shapes=[pltpu.VMEM((NK, 2, BLK, HD), bf16), pltpu.VMEM((BLK, HD), bf16), dma((5,))],
        compiler_params=params(12),
    )(query_grad, kept, arrived[1], arrived[2], arrived[3])
    grads = lax.all_to_all(grads, "h", 0, 0, tiled=True)

    def tokens(i):
        part = grads[:, i * ROWS : (i + 1) * ROWS, :]
        return jnp.transpose(part, (1, 0, 2)).reshape(ROWS, HEADS * HD)

    return tokens(0), tokens(1), tokens(2)


def solution(mesh):
    wide = Mesh(mesh.devices.reshape(NX, NY, NC, HEADS), ("x", "y", "c", "h"))
    split = P(("x", "y", "c", "h"), None)
    return jax.shard_map(
        on_device,
        mesh=wide,
        in_specs=(split,) * 5 + (P(),) * 3,
        out_specs=(split,) * 3,
        check_vma=False,
    )
```

```python
import functools
import math

import jax
import jax.numpy as jnp
from jax import lax
from jax.experimental import pallas as pl
from jax.experimental.pallas import tpu as pltpu
from jax.sharding import Mesh, PartitionSpec as P

HD = 128
BLK = 512
HEADS = 16
ROWS = BLK // HEADS
NX, NY, NC = 4, 4, 2
NQ = NY * NC
NK = NX
NPAIR = NQ * NK
PACKED = 4 * ROWS + 8
QD_ROWS = 2 * BLK + 16
UNROLL = 4
CHUNK = 256
CHUNKS = BLK // CHUNK
SCALE = 1.0 / math.sqrt(HD)
SCALE2 = SCALE * math.log2(math.e)
LOW = -1e30
MIB = 1024 * 1024


def dot(a, b, contract):
    return lax.dot_general(a, b, ((contract[:1], contract[1:]), ((), ())), preferred_element_type=jnp.float32)


def query_slot(code, meta):
    return (code & NY) | ((code + meta[1]) & (NY - 1))


def query_place(code, meta):
    slot = query_slot(code, meta)
    return (slot & (NY - 1)) * NC + (meta[2] ^ (slot // NY))


def fetch_keys(blocks, kv, sems):
    return [pltpu.make_async_copy(block, kv.at[i], sems.at[i]) for i, block in enumerate(blocks)]


def fetch_queries(own, other, qd, sems):
    return [
        pltpu.make_async_copy(own, qd.at[pl.ds(0, NY)], sems.at[0]),
        pltpu.make_async_copy(other, qd.at[pl.ds(NY, NY)], sems.at[1]),
    ]


def chunk(index):
    start = index % CHUNKS * CHUNK
    return index // CHUNKS, start, slice(start, start + CHUNK)


def probs_kernel(
    pairs, meta, own, other, kv0, kv1, kv2, kv3, probs, tops, copies,
    qd, kv, stats, scores, tops_held, held, sems, key_sems, out_sems, copy_sems,
):
    fetches = fetch_queries(own, other, qd, sems) + fetch_keys((kv0, kv1, kv2, kv3), kv, key_sems)
    for fetch in fetches:
        fetch.start()
    stats[:, 0, :] = jnp.full((NQ, BLK), LOW, jnp.float32)
    stats[:, 1, :] = jnp.zeros((NQ, BLK), jnp.float32)
    for fetch in fetches:
        fetch.wait()
    count = meta[0]
    steps = (count + UNROLL - 1) // UNROLL

    def store(step, u):
        return pltpu.make_async_copy(
            held.at[step & 1, u], probs.at[step * UNROLL + u], out_sems.at[step & 1, u]
        )

    def wait_stores(step):
        for u in range(UNROLL):
            store(step, u).wait()

    def product(step, index, first):
        u, start, part = chunk(index)
        code = pairs[jnp.minimum(step * UNROLL + u, NPAIR - 1)]
        found = dot(kv[code // NQ, :BLK, :], qd[query_slot(code, meta), part, :], (1, 1))
        if first and u == 0:
            key_row = lax.broadcasted_iota(jnp.int32, found.shape, 0)
            query_row = lax.broadcasted_iota(jnp.int32, found.shape, 1) + start
            found = jnp.where(key_row <= query_row, found, LOW)
        tops_held[index % 2][...] = jnp.max(found, axis=0, keepdims=True) * SCALE2
        scores[index % 2][...] = found

    def normalize(step, index):
        u, _, part = chunk(index)
        t = step * UNROLL + u
        place = query_place(pairs[t], meta)
        top = tops_held[index % 2][...]
        values = jnp.exp2(scores[index % 2][...] * SCALE2 - top)
        total = jnp.sum(values, axis=0, keepdims=True)
        held[step & 1, u, :, part] = values.astype(jnp.bfloat16)
        tops[t, :, part] = top
        top = jnp.where(t < count, top, LOW)
        total = jnp.where(t < count, total, 0.0)
        old_top, old_total = stats[place, 0:1, part], stats[place, 1:2, part]
        new_top = jnp.maximum(old_top, top)
        stats[place, 0:1, part] = new_top
        stats[place, 1:2, part] = old_total * jnp.exp2(old_top - new_top) + total * jnp.exp2(top - new_top)

    def visit(step, first):
        @pl.when(step >= 2)
        def _():
            wait_stores(step - 2)

        for index in range(UNROLL * CHUNKS):
            product(step, index + 1, first)
            normalize(step, index)
            if index % CHUNKS == CHUNKS - 1:
                store(step, index // CHUNKS).start()

    product(0, 0, True)
    visit(0, True)

    def body(step, _):
        visit(step, False)
        return 0

    lax.fori_loop(1, steps, body, 0)
    sent = [pltpu.make_async_copy(stats, copies.at[i], copy_sems.at[i]) for i in range(NQ)]
    for copy in sent:
        copy.start()
    for copy in sent:
        copy.wait()
    wait_stores(steps - 1)

    @pl.when(steps >= 2)
    def _():
        wait_stores(steps - 2)


def dscore_kernel(
    pairs, meta, own, other, kv0, kv1, kv2, kv3, probs_in, stats_in, tops, dscore, dquery,
    qd, kv, keys_t, total, stats, dprob, probs, held, dquery_held, sems, key_sems, in_sems, out_sems, dquery_sems,
):
    count = meta[0]
    steps = (count + UNROLL - 1) // UNROLL

    def load(step):
        span = pl.ds(step * UNROLL, UNROLL)
        return pltpu.make_async_copy(probs_in.at[span], probs.at[span], in_sems.at[step])

    def store(step, u):
        return pltpu.make_async_copy(
            held.at[step & 1, u], dscore.at[step * UNROLL + u], out_sems.at[step & 1, u]
        )

    def wait_stores(step):
        for u in range(UNROLL):
            store(step, u).wait()

    key_fetches = fetch_keys((kv0, kv1, kv2, kv3), kv, key_sems)
    fetches = fetch_queries(own, other, qd, sems)
    fetches.append(pltpu.make_async_copy(stats_in.at[0], stats, sems.at[2]))
    for fetch in key_fetches + fetches:
        fetch.start()

    def start(step, _):
        load(step).start()
        return 0

    lax.fori_loop(0, steps, start, 0)
    total[...] = jnp.zeros_like(total)
    for i, fetch in enumerate(key_fetches):
        fetch.wait()
        keys_t[i] = jnp.transpose(kv[i, :BLK, :])
    for fetch in fetches:
        fetch.wait()

    def product(step, index):
        u, start, _ = chunk(index)
        code = pairs[jnp.minimum(step * UNROLL + u, NPAIR - 1)]
        grads = qd[query_slot(code, meta), BLK + start : BLK + start + CHUNK, :]
        dprob[index % 2][...] = dot(kv[code // NQ, BLK:, :], grads, (1, 1))

    def differentiate(step, index):
        u, start, part = chunk(index)
        t = step * UNROLL + u
        pieces = qd[query_slot(pairs[t], meta), 2 * BLK :, :].astype(jnp.float32)
        row_dot = pieces[0:4] + pieces[4:8] + pieces[8:12]
        lines = range(start // HD, (start + CHUNK) // HD)
        row_dot = jnp.concatenate([row_dot[i : i + 1] for i in lines], axis=1)
        low = probs[t, :, part].astype(jnp.float32) * (dprob[index % 2][...] - row_dot)
        held[step & 1, u, :, part] = low.astype(jnp.bfloat16)

    def accumulate(step, index):
        u, _, part = chunk(index)
        t = step * UNROLL + u
        code = pairs[t]
        place = query_place(code, meta)
        weight = jnp.where(t < count, jnp.exp2(tops[t, :, part] - stats[place, 0:1, part]), 0.0)
        total[place, :, part] += dot(keys_t[code // NQ], held[step & 1, u, :, part], (1, 0)) * weight

    def body(step, _):
        load(step).wait()

        @pl.when(step >= 2)
        def _():
            wait_stores(step - 2)

        for index in range(UNROLL * CHUNKS):
            product(step, index + 1)
            if index > 0:
                accumulate(step, index - 1)
            differentiate(step, index)
            if index % CHUNKS == CHUNKS - 1:
                store(step, index // CHUNKS).start()
        accumulate(step, UNROLL * CHUNKS - 1)
        return 0

    product(0, 0)
    lax.fori_loop(0, steps, body, 0)
    sent = [pltpu.make_async_copy(dquery_held.at[i], dquery.at[i], dquery_sems.at[i]) for i in range(NQ)]
    for i in range(NQ):
        dquery_held[i] = total[i].astype(jnp.bfloat16)
        sent[i].start()
    for copy in sent:
        copy.wait()
    wait_stores(steps - 1)

    @pl.when(steps >= 2)
    def _():
        wait_stores(steps - 2)


def log_norms(stats_all):
    tops, sums = stats_all[:, :, 0, :], stats_all[:, :, 1, :]
    top = jnp.max(tops, axis=0)
    return top + jnp.log2(jnp.sum(sums * jnp.exp2(tops - top[None]), axis=0))


def key_kernel(late, pairs, meta, own, other, probs_in, dscore_in, tops, stats_all, *rest):
    *outs, qd, norms, total, probs, dscore, sems, probs_sems, dscore_sems = rest
    begin, end = (0, meta[3]) if late else (meta[3], meta[0])
    steps = (end - begin + UNROLL - 1) // UNROLL

    def loads(step):
        copies = []
        for u in range(UNROLL):
            t = jnp.minimum(begin + step * UNROLL + u, end - 1)
            held = step * UNROLL + u
            copies.append(pltpu.make_async_copy(dscore_in.at[t], dscore.at[held], dscore_sems.at[held]))
            copies.append(pltpu.make_async_copy(probs_in.at[t], probs.at[held], probs_sems.at[held]))
        return copies

    def start(step, _):
        for copy in loads(step):
            copy.start()
        return 0

    lax.fori_loop(0, jnp.minimum(steps, 1), start, 0)
    fetches = fetch_queries(own, other, qd, sems)
    for fetch in fetches:
        fetch.start()
    lax.fori_loop(1, steps, start, 0)
    total[...] = jnp.zeros_like(total)
    norms[:, 0, :] = log_norms(stats_all[...])
    for fetch in fetches:
        fetch.wait()

    def body(step, _):
        for copy in loads(step):
            copy.wait()
        found = []
        for u in range(UNROLL):
            held = step * UNROLL + u
            t = jnp.minimum(begin + held, end - 1)
            code = pairs[t]
            place, key, query = query_place(code, meta), code // NQ, query_slot(code, meta)
            weight = jnp.where(begin + held < end, jnp.exp2(tops[t] - norms[place]), 0.0)
            weight = jnp.transpose(jnp.broadcast_to(weight, (HD, BLK)))
            queries = (qd[query, :BLK, :].astype(jnp.float32) * (weight * SCALE)).astype(jnp.bfloat16)
            grads = (qd[query, BLK : 2 * BLK, :].astype(jnp.float32) * weight).astype(jnp.bfloat16)
            slot = 0 if late else key - 1
            found.append((slot, dot(dscore[held], queries, (1, 0)), dot(probs[held], grads, (1, 0))))
        for slot, key_part, value_part in found:
            total[slot, 0] += key_part
            total[slot, 1] += value_part
        return 0

    lax.fori_loop(0, steps, body, 0)
    for i, out in enumerate(outs):
        out[...] = total[i].astype(jnp.bfloat16)


def pack_kernel(query_in, key_in, value_in, output_in, grad_in, out, held, sems):
    fetches = [
        pltpu.make_async_copy(source, held.at[i], sems.at[i])
        for i, source in enumerate((query_in, key_in, value_in, output_in, grad_in))
    ]
    for fetch in fetches:
        fetch.start()
    for fetch in fetches:
        fetch.wait()
    query, key, value, output, grad = (held.at[i] for i in range(5))
    lane = lax.broadcasted_iota(jnp.int32, (ROWS, HD), 1)
    row_dot = jnp.zeros((ROWS, HD), jnp.float32)
    for h in range(HEADS):
        part = slice(h * HD, (h + 1) * HD)
        for i, array in enumerate((query, grad, key, value)):
            out[h, i * ROWS : (i + 1) * ROWS, :] = array[:, part]
        products = grad[:, part].astype(jnp.float32) * output[:, part].astype(jnp.float32)
        row_dot = jnp.where(lane == h, jnp.sum(products, axis=1, keepdims=True), row_dot)
    row_dot = jnp.concatenate([row_dot, jnp.zeros((HD - ROWS, HD), jnp.float32)], axis=0)
    row_dot = jnp.transpose(row_dot)[:HEADS]
    high = row_dot.astype(jnp.bfloat16).astype(jnp.float32)
    middle = (row_dot - high).astype(jnp.bfloat16).astype(jnp.float32)
    row = lax.broadcasted_iota(jnp.int32, (HEADS, 8, HD), 1)
    pieces = jnp.zeros((HEADS, 8, HD), jnp.float32)
    for i, piece in enumerate((high, middle, row_dot - high - middle)):
        pieces = jnp.where(row == i, piece[:, None, :], pieces)
    out[:, 4 * ROWS :, :] = pieces.astype(jnp.bfloat16)


def finish_queries_kernel(meta, dquery_in, stats_in, out, dquery, stats_all, sems):
    fetches = [
        pltpu.make_async_copy(stats_in, stats_all, sems.at[0]),
        pltpu.make_async_copy(dquery_in, dquery, sems.at[1]),
    ]
    for fetch in fetches:
        fetch.start()
    for fetch in fetches:
        fetch.wait()
    place = meta[1] * NC + meta[2]
    tops, sums = stats_all[:, place, 0, :], stats_all[:, place, 1, :]
    top = jnp.max(tops, axis=0, keepdims=True)
    norm = top + jnp.log2(jnp.sum(sums * jnp.exp2(tops - top), axis=0, keepdims=True))
    weight = jnp.exp2(tops - norm) * SCALE
    grad = dquery[0].astype(jnp.float32) * weight[0:1]
    for i in range(1, NQ):
        grad += dquery[i].astype(jnp.float32) * weight[i : i + 1]
    out[...] = jnp.transpose(grad).astype(jnp.bfloat16)


def finish_kernel(query_grad, kept, first, second, third, out, parts, query_held, sems):
    fetches = [
        pltpu.make_async_copy(source, parts.at[i], sems.at[i])
        for i, source in enumerate((kept, first, second, third))
    ]
    fetches.append(pltpu.make_async_copy(query_grad, query_held, sems.at[4]))
    for fetch in fetches:
        fetch.start()
    for fetch in fetches:
        fetch.wait()
    out[:, 0:ROWS, :] = query_held[...].reshape(HEADS, ROWS, HD)
    for i in range(2):
        grad = (parts[0, i].astype(jnp.float32) + parts[1, i].astype(jnp.float32)) + (
            parts[2, i].astype(jnp.float32) + parts[3, i].astype(jnp.float32)
        )
        out[:, (i + 1) * ROWS : (i + 2) * ROWS, :] = grad.astype(jnp.bfloat16).reshape(HEADS, ROWS, HD)


def in_hbm(array):
    return pltpu.with_memory_space_constraint(array, pltpu.HBM)


def params(mib):
    return pltpu.CompilerParams(vmem_limit_bytes=mib * MIB)


def over_pairs(kernel, mib, pairs, meta, operands, in_specs, out_specs, out_shape, scratch):
    return pl.pallas_call(
        kernel,
        grid_spec=pltpu.PrefetchScalarGridSpec(
            num_scalar_prefetch=2,
            grid=(1,),
            in_specs=in_specs,
            out_specs=out_specs,
            scratch_shapes=scratch,
        ),
        out_shape=out_shape,
        compiler_params=params(mib),
    )(pairs, meta, *operands)


def pair_list(key_lists, key_counts, block_order, x, y, c):
    slot = jnp.arange(NQ, dtype=jnp.int32)
    query_at = x * NQ + ((y + slot) % NY) * NC + (c ^ (slot // NY))
    key_at = ((x - jnp.arange(NK, dtype=jnp.int32)) % NX) * NQ + y * NC + c
    query_blocks, key_blocks = block_order[query_at], block_order[key_at]
    lists, counts = key_lists[query_blocks], key_counts[query_blocks]
    used = jnp.arange(key_lists.shape[1], dtype=jnp.int32)[None, :] < counts[:, None]
    named = jnp.any((lists[None, :, :] == key_blocks[:, None, None]) & used[None, :, :], axis=2)
    named = named.reshape(NPAIR)
    code = jnp.arange(NPAIR, dtype=jnp.int32)
    rank = jnp.sum((code[None, :] < code[:, None]) & named[None, :], axis=1)
    count = jnp.sum(named.astype(jnp.int32))
    wanted = jnp.minimum(code, count - 1)
    pairs = jnp.sum(jnp.where(named[None, :] & (rank[None, :] == wanted[:, None]), code[None, :], 0), axis=1)
    return pairs.astype(jnp.int32), count, jnp.sum(named[:NQ].astype(jnp.int32))


def shifted(array, axis, by, size):
    return lax.ppermute(array, axis, [(i, (i + by) % size) for i in range(size)])


def on_device(query_data, key_data, value_data, output_data, output_grad, key_lists, key_counts, block_order):
    x, y, c = lax.axis_index("x"), lax.axis_index("y"), lax.axis_index("c")

    bf16, f32 = jnp.bfloat16, jnp.float32
    shape, vmem = jax.ShapeDtypeStruct, pl.BlockSpec(memory_space=pltpu.VMEM)
    anywhere = pl.BlockSpec(memory_space=pltpu.HBM)
    dma = pltpu.SemaphoreType.DMA

    packed = pl.pallas_call(
        pack_kernel,
        in_specs=[anywhere] * 5,
        out_specs=vmem,
        out_shape=shape((HEADS, PACKED, HD), bf16),
        scratch_shapes=[pltpu.VMEM((5, ROWS, HEADS * HD), bf16), dma((5,))],
        compiler_params=params(8),
    )(*(in_hbm(array) for array in (query_data, key_data, value_data, output_data, output_grad)))
    packed = lax.all_to_all(packed, "h", 0, 0, tiled=True)
    pairs, count, near = pair_list(key_lists, key_counts, block_order, x, y, c)
    meta = jnp.stack([count, y, c, near]).astype(jnp.int32)
    packed, pairs, meta = lax.optimization_barrier((packed, pairs, meta))

    def rows(i):
        return packed[:, i * ROWS : (i + 1) * ROWS, :].reshape(BLK, HD)

    pieces = jnp.transpose(packed[:, 4 * ROWS : 4 * ROWS + 3, :ROWS], (1, 0, 2)).reshape(12, HD)
    qd = jnp.concatenate([rows(0), rows(1), pieces, jnp.zeros((4, HD), bf16)], axis=0)
    kv = jnp.concatenate([rows(2), rows(3)], axis=0)

    own = lax.all_to_all(jnp.broadcast_to(qd[None], (NY, *qd.shape)), "y", 0, 0, tiled=True)
    keys = (kv, *(shifted(kv, "x", i, NX) for i in range(1, NX)))
    own, *keys = lax.optimization_barrier((own, *keys))
    queries = (own, shifted(own, "c", 1, NC))

    square, line = pltpu.HBM((NPAIR, BLK, BLK), bf16), shape((NPAIR, 1, BLK), f32)
    qd_scratch, kv_scratch = pltpu.VMEM((NQ, QD_ROWS, HD), bf16), pltpu.VMEM((NK, 2 * BLK, HD), bf16)
    probs, tops, stats = over_pairs(
        probs_kernel, 28, pairs, meta, (*queries, *keys),
        [anywhere] * 6,
        [anywhere, vmem, anywhere],
        [square, line, pltpu.HBM((NQ, NQ, 2, BLK), f32)],
        [
            qd_scratch, kv_scratch, pltpu.VMEM((NQ, 2, BLK), f32), [pltpu.VMEM((BLK, CHUNK), f32)] * 2,
            [pltpu.VMEM((1, CHUNK), f32)] * 2, pltpu.VMEM((2, UNROLL, BLK, BLK), bf16),
            dma((2,)), dma((NK,)), dma((2, UNROLL)), dma((NQ,)),
        ],
    )
    stats_all = lax.all_to_all(stats, ("y", "c"), 0, 0, tiled=True)
    tiles, two_steps = pltpu.VMEM((NPAIR, BLK, BLK), bf16), pltpu.VMEM((2, UNROLL, BLK, BLK), bf16)
    step_dma = dma((NPAIR // UNROLL,))
    dscore, dquery = over_pairs(
        dscore_kernel, 44, pairs, meta, (*queries, *keys, in_hbm(probs), in_hbm(stats), tops),
        [anywhere] * 8 + [vmem],
        [anywhere, anywhere],
        [square, pltpu.HBM((NQ, HD, BLK), bf16)],
        [
            qd_scratch, kv_scratch, pltpu.VMEM((NK, HD, BLK), bf16), pltpu.VMEM((NQ, HD, BLK), f32),
            pltpu.VMEM((NQ, 2, BLK), f32), [pltpu.VMEM((BLK, CHUNK), f32)] * 2, tiles, two_steps, pltpu.VMEM((NQ, HD, BLK), bf16), dma((3,)), dma((NK,)), step_dma, dma((2, UNROLL)), dma((NQ,)),
        ],
    )
    dquery = lax.all_to_all(dquery, ("y", "c"), 0, 0, tiled=True)


    def key_grads(late, pairs):
        slots = 1 if late else NK - 1
        most = slots * NQ
        held = pltpu.VMEM((most, BLK, BLK), bf16)
        return over_pairs(
            functools.partial(key_kernel, late), 50, pairs, meta,
            (*queries, in_hbm(probs), in_hbm(dscore), tops, stats_all),
            [anywhere] * 4 + [vmem] * 2,
            [vmem] * slots,
            [shape((2, BLK, HD), bf16)] * slots,
            [
                qd_scratch, pltpu.VMEM((NQ, 1, BLK), f32), pltpu.VMEM((slots, 2, BLK, HD), f32), held, held,
                dma((2,)), dma((most,)), dma((most,)),
            ],
        )

    *sent, pairs = lax.optimization_barrier((*key_grads(False, pairs), pairs))
    arrived = {i: shifted(sent[i - 1], "x", -i, NX) for i in (2, 1, 3)}
    (kept,) = key_grads(True, pairs)
    query_grad = pl.pallas_call(
        finish_queries_kernel,
        grid_spec=pltpu.PrefetchScalarGridSpec(
            num_scalar_prefetch=1,
            grid=(1,),
            in_specs=[anywhere] * 2,
            out_specs=vmem,
            scratch_shapes=[pltpu.VMEM((NQ, HD, BLK), bf16), pltpu.VMEM((NQ, NQ, 2, BLK), f32), dma((2,))],
        ),
        out_shape=shape((BLK, HD), bf16),
        compiler_params=params(12),
    )(meta, dquery, stats_all)
    grads = pl.pallas_call(
        finish_kernel,
        in_specs=[anywhere] * 5,
        out_specs=vmem,
        out_shape=shape((HEADS, 3 * ROWS, HD), bf16),
        scratch_shapes=[pltpu.VMEM((NK, 2, BLK, HD), bf16), pltpu.VMEM((BLK, HD), bf16), dma((5,))],
        compiler_params=params(12),
    )(query_grad, kept, arrived[1], arrived[2], arrived[3])
    grads = lax.all_to_all(grads, "h", 0, 0, tiled=True)

    def tokens(i):
        part = grads[:, i * ROWS : (i + 1) * ROWS, :]
        return jnp.transpose(part, (1, 0, 2)).reshape(ROWS, HEADS * HD)

    return tokens(0), tokens(1), tokens(2)


def solution(mesh):
    wide = Mesh(mesh.devices.reshape(NX, NY, NC, HEADS), ("x", "y", "c", "h"))
    split = P(("x", "y", "c", "h"), None)
    return jax.shard_map(
        on_device,
        mesh=wide,
        in_specs=(split,) * 5 + (P(),) * 3,
        out_specs=(split,) * 3,
        check_vma=False,
    )
```

```python
import functools
import math

import jax
import jax.numpy as jnp
from jax import lax
from jax.experimental import pallas as pl
from jax.experimental.pallas import tpu as pltpu
from jax.sharding import Mesh, PartitionSpec as P

HD = 128
BLK = 512
HEADS = 16
ROWS = BLK // HEADS
NX, NY, NC = 4, 4, 2
NQ = NY * NC
NK = NX
NPAIR = NQ * NK
PACKED = 4 * ROWS + 16
QD_ROWS = 2 * BLK + 16
UNROLL = 4
CHUNK = 256
CHUNKS = BLK // CHUNK
SCALE = 1.0 / math.sqrt(HD)
SCALE2 = SCALE * math.log2(math.e)
LOW = -1e30
MIB = 1024 * 1024


def dot(a, b, contract):
    return lax.dot_general(a, b, ((contract[:1], contract[1:]), ((), ())), preferred_element_type=jnp.float32)


def query_slot(code, meta):
    return (code & NY) | ((code + meta[1]) & (NY - 1))


def query_place(code, meta):
    slot = query_slot(code, meta)
    return (slot & (NY - 1)) * NC + (meta[2] ^ (slot // NY))


def fetch_keys(blocks, kv, sems):
    return [pltpu.make_async_copy(block, kv.at[i], sems.at[i]) for i, block in enumerate(blocks)]


def fetch_queries(own, other, qd, sems):
    return [
        pltpu.make_async_copy(own, qd.at[pl.ds(0, NY)], sems.at[0]),
        pltpu.make_async_copy(other, qd.at[pl.ds(NY, NY)], sems.at[1]),
    ]


def chunk(index):
    start = index % CHUNKS * CHUNK
    return index // CHUNKS, start, slice(start, start + CHUNK)


def probs_kernel(
    pairs, meta, own, other, kv0, kv1, kv2, kv3, probs, tops, copies,
    qd, kv, stats, scores, tops_held, held, sems, key_sems, out_sems, copy_sems,
):
    fetches = fetch_queries(own, other, qd, sems) + fetch_keys((kv0, kv1, kv2, kv3), kv, key_sems)
    for fetch in fetches:
        fetch.start()
    stats[:, 0, :] = jnp.full((NQ, BLK), LOW, jnp.float32)
    stats[:, 1, :] = jnp.zeros((NQ, BLK), jnp.float32)
    for fetch in fetches:
        fetch.wait()
    count = meta[0]
    steps = (count + UNROLL - 1) // UNROLL

    def store(step, u):
        return pltpu.make_async_copy(
            held.at[step & 1, u], probs.at[step * UNROLL + u], out_sems.at[step & 1, u]
        )

    def wait_stores(step):
        for u in range(UNROLL):
            store(step, u).wait()

    def product(step, index, first):
        u, start, part = chunk(index)
        code = pairs[jnp.minimum(step * UNROLL + u, NPAIR - 1)]
        found = dot(kv[code // NQ, :BLK, :], qd[query_slot(code, meta), part, :], (1, 1))
        if first and u == 0:
            key_row = lax.broadcasted_iota(jnp.int32, found.shape, 0)
            query_row = lax.broadcasted_iota(jnp.int32, found.shape, 1) + start
            found = jnp.where(key_row <= query_row, found, LOW)
        tops_held[index % 2][...] = jnp.max(found, axis=0, keepdims=True) * SCALE2
        scores[index % 2][...] = found

    def normalize(step, index):
        u, _, part = chunk(index)
        t = step * UNROLL + u
        place = query_place(pairs[t], meta)
        top = tops_held[index % 2][...]
        values = jnp.exp2(scores[index % 2][...] * SCALE2 - top)
        total = jnp.sum(values, axis=0, keepdims=True)
        held[step & 1, u, :, part] = values.astype(jnp.bfloat16)
        tops[t, :, part] = top
        top = jnp.where(t < count, top, LOW)
        total = jnp.where(t < count, total, 0.0)
        old_top, old_total = stats[place, 0:1, part], stats[place, 1:2, part]
        new_top = jnp.maximum(old_top, top)
        stats[place, 0:1, part] = new_top
        stats[place, 1:2, part] = old_total * jnp.exp2(old_top - new_top) + total * jnp.exp2(top - new_top)

    def visit(step, first):
        @pl.when(step >= 2)
        def _():
            wait_stores(step - 2)

        for index in range(UNROLL * CHUNKS):
            product(step, index + 1, first)
            normalize(step, index)
            if index % CHUNKS == CHUNKS - 1:
                store(step, index // CHUNKS).start()

    product(0, 0, True)
    visit(0, True)

    def body(step, _):
        visit(step, False)
        return 0

    lax.fori_loop(1, steps, body, 0)
    sent = [pltpu.make_async_copy(stats, copies.at[i], copy_sems.at[i]) for i in range(NQ)]
    for copy in sent:
        copy.start()
    for copy in sent:
        copy.wait()
    wait_stores(steps - 1)

    @pl.when(steps >= 2)
    def _():
        wait_stores(steps - 2)


def dscore_kernel(
    pairs, meta, own, other, kv0, kv1, kv2, kv3, probs_in, stats_in, tops, dscore, dquery,
    qd, kv, keys_t, total, stats, dprob, probs, held, dquery_held, sems, key_sems, in_sems, out_sems, dquery_sems,
):
    count = meta[0]
    steps = (count + UNROLL - 1) // UNROLL

    def load(step):
        span = pl.ds(step * UNROLL, UNROLL)
        return pltpu.make_async_copy(probs_in.at[span], probs.at[span], in_sems.at[step])

    def store(step, u):
        return pltpu.make_async_copy(
            held.at[step & 1, u], dscore.at[step * UNROLL + u], out_sems.at[step & 1, u]
        )

    def wait_stores(step):
        for u in range(UNROLL):
            store(step, u).wait()

    key_fetches = fetch_keys((kv0, kv1, kv2, kv3), kv, key_sems)
    fetches = fetch_queries(own, other, qd, sems)
    fetches.append(pltpu.make_async_copy(stats_in.at[0], stats, sems.at[2]))
    for fetch in key_fetches + fetches:
        fetch.start()

    def start(step, _):
        load(step).start()
        return 0

    lax.fori_loop(0, steps, start, 0)
    total[...] = jnp.zeros_like(total)
    for i, fetch in enumerate(key_fetches):
        fetch.wait()
        keys_t[i] = jnp.transpose(kv[i, :BLK, :])
    for fetch in fetches:
        fetch.wait()

    def product(step, index):
        u, start, _ = chunk(index)
        code = pairs[jnp.minimum(step * UNROLL + u, NPAIR - 1)]
        grads = qd[query_slot(code, meta), BLK + start : BLK + start + CHUNK, :]
        dprob[index % 2][...] = dot(kv[code // NQ, BLK:, :], grads, (1, 1))

    def differentiate(step, index):
        u, start, part = chunk(index)
        t = step * UNROLL + u
        pieces = qd[query_slot(pairs[t], meta), 2 * BLK :, :].astype(jnp.float32)
        row_dot = pieces[0:4] + pieces[4:8] + pieces[8:12]
        lines = range(start // HD, (start + CHUNK) // HD)
        row_dot = jnp.concatenate([row_dot[i : i + 1] for i in lines], axis=1)
        low = probs[t, :, part].astype(jnp.float32) * (dprob[index % 2][...] - row_dot)
        held[step & 1, u, :, part] = low.astype(jnp.bfloat16)

    def accumulate(step, index):
        u, _, part = chunk(index)
        t = step * UNROLL + u
        code = pairs[t]
        place = query_place(code, meta)
        weight = jnp.where(t < count, jnp.exp2(tops[t, :, part] - stats[place, 0:1, part]), 0.0)
        total[place, :, part] += dot(keys_t[code // NQ], held[step & 1, u, :, part], (1, 0)) * weight

    def body(step, _):
        load(step).wait()

        @pl.when(step >= 2)
        def _():
            wait_stores(step - 2)

        for index in range(UNROLL * CHUNKS):
            product(step, index + 1)
            if index > 0:
                accumulate(step, index - 1)
            differentiate(step, index)
            if index % CHUNKS == CHUNKS - 1:
                store(step, index // CHUNKS).start()
        accumulate(step, UNROLL * CHUNKS - 1)
        return 0

    product(0, 0)
    lax.fori_loop(0, steps, body, 0)
    sent = [pltpu.make_async_copy(dquery_held.at[i], dquery.at[i], dquery_sems.at[i]) for i in range(NQ)]
    for i in range(NQ):
        dquery_held[i] = total[i].astype(jnp.bfloat16)
        sent[i].start()
    for copy in sent:
        copy.wait()
    wait_stores(steps - 1)

    @pl.when(steps >= 2)
    def _():
        wait_stores(steps - 2)


def log_norms(stats_all):
    tops, sums = stats_all[:, :, 0, :], stats_all[:, :, 1, :]
    top = jnp.max(tops, axis=0)
    return top + jnp.log2(jnp.sum(sums * jnp.exp2(tops - top[None]), axis=0))


def key_kernel(late, pairs, meta, own, other, probs_in, dscore_in, tops, stats_all, *rest):
    *outs, qd, norms, total, probs, dscore, sems, probs_sems, dscore_sems = rest
    begin, end = (0, meta[3]) if late else (meta[3], meta[0])
    steps = (end - begin + UNROLL - 1) // UNROLL

    def loads(step):
        copies = []
        for u in range(UNROLL):
            t = jnp.minimum(begin + step * UNROLL + u, end - 1)
            held = step * UNROLL + u
            copies.append(pltpu.make_async_copy(dscore_in.at[t], dscore.at[held], dscore_sems.at[held]))
            copies.append(pltpu.make_async_copy(probs_in.at[t], probs.at[held], probs_sems.at[held]))
        return copies

    def start(step, _):
        for copy in loads(step):
            copy.start()
        return 0

    lax.fori_loop(0, jnp.minimum(steps, 1), start, 0)
    fetches = fetch_queries(own, other, qd, sems)
    for fetch in fetches:
        fetch.start()
    lax.fori_loop(1, steps, start, 0)
    total[...] = jnp.zeros_like(total)
    norms[:, 0, :] = log_norms(stats_all[...])
    for fetch in fetches:
        fetch.wait()

    def body(step, _):
        for copy in loads(step):
            copy.wait()
        found = []
        for u in range(UNROLL):
            held = step * UNROLL + u
            t = jnp.minimum(begin + held, end - 1)
            code = pairs[t]
            place, key, query = query_place(code, meta), code // NQ, query_slot(code, meta)
            weight = jnp.where(begin + held < end, jnp.exp2(tops[t] - norms[place]), 0.0)
            weight = jnp.transpose(jnp.broadcast_to(weight, (HD, BLK)))
            queries = (qd[query, :BLK, :].astype(jnp.float32) * (weight * SCALE)).astype(jnp.bfloat16)
            grads = (qd[query, BLK : 2 * BLK, :].astype(jnp.float32) * weight).astype(jnp.bfloat16)
            slot = 0 if late else key - 1
            found.append((slot, dot(dscore[held], queries, (1, 0)), dot(probs[held], grads, (1, 0))))
        for slot, key_part, value_part in found:
            total[slot, 0] += key_part
            total[slot, 1] += value_part
        return 0

    lax.fori_loop(0, steps, body, 0)
    for i, out in enumerate(outs):
        out[...] = total[i].astype(jnp.bfloat16)


def pack_kernel(query_in, key_in, value_in, output_in, grad_in, out, held, sems):
    fetches = [
        pltpu.make_async_copy(source, held.at[i], sems.at[i])
        for i, source in enumerate((query_in, key_in, value_in, output_in, grad_in))
    ]
    for fetch in fetches:
        fetch.start()
    for fetch in fetches:
        fetch.wait()
    query, key, value, output, grad = (held.at[i] for i in range(5))
    lane = lax.broadcasted_iota(jnp.int32, (ROWS, HD), 1)
    row_dot = jnp.zeros((ROWS, HD), jnp.float32)
    for h in range(HEADS):
        part = slice(h * HD, (h + 1) * HD)
        for i, array in enumerate((query, grad, key, value)):
            out[h, i * ROWS : (i + 1) * ROWS, :] = array[:, part]
        products = grad[:, part].astype(jnp.float32) * output[:, part].astype(jnp.float32)
        row_dot = jnp.where(lane == h, jnp.sum(products, axis=1, keepdims=True), row_dot)
    row_dot = jnp.concatenate([row_dot, jnp.zeros((HD - ROWS, HD), jnp.float32)], axis=0)
    row_dot = jnp.transpose(row_dot)[:HEADS]
    high = row_dot.astype(jnp.bfloat16).astype(jnp.float32)
    middle = (row_dot - high).astype(jnp.bfloat16).astype(jnp.float32)
    row = lax.broadcasted_iota(jnp.int32, (HEADS, 16, HD), 1)
    pieces = jnp.zeros((HEADS, 16, HD), jnp.float32)
    for i, piece in enumerate((high, middle, row_dot - high - middle)):
        pieces = jnp.where(row == i, piece[:, None, :], pieces)
    out[:, 4 * ROWS :, :] = pieces.astype(jnp.bfloat16)


def finish_queries_kernel(meta, dquery_in, stats_in, out, dquery, stats_all, sems):
    fetches = [
        pltpu.make_async_copy(stats_in, stats_all, sems.at[0]),
        pltpu.make_async_copy(dquery_in, dquery, sems.at[1]),
    ]
    for fetch in fetches:
        fetch.start()
    for fetch in fetches:
        fetch.wait()
    place = meta[1] * NC + meta[2]
    tops, sums = stats_all[:, place, 0, :], stats_all[:, place, 1, :]
    top = jnp.max(tops, axis=0, keepdims=True)
    norm = top + jnp.log2(jnp.sum(sums * jnp.exp2(tops - top), axis=0, keepdims=True))
    weight = jnp.exp2(tops - norm) * SCALE
    grad = dquery[0].astype(jnp.float32) * weight[0:1]
    for i in range(1, NQ):
        grad += dquery[i].astype(jnp.float32) * weight[i : i + 1]
    out[...] = jnp.transpose(grad).astype(jnp.bfloat16)


def finish_kernel(query_grad, kept, first, second, third, out, parts, query_held, sems):
    fetches = [
        pltpu.make_async_copy(source, parts.at[i], sems.at[i])
        for i, source in enumerate((kept, first, second, third))
    ]
    fetches.append(pltpu.make_async_copy(query_grad, query_held, sems.at[4]))
    for fetch in fetches:
        fetch.start()
    for fetch in fetches:
        fetch.wait()
    out[:, 0:ROWS, :] = query_held[...].reshape(HEADS, ROWS, HD)
    for i in range(2):
        grad = (parts[0, i].astype(jnp.float32) + parts[1, i].astype(jnp.float32)) + (
            parts[2, i].astype(jnp.float32) + parts[3, i].astype(jnp.float32)
        )
        out[:, (i + 1) * ROWS : (i + 2) * ROWS, :] = grad.astype(jnp.bfloat16).reshape(HEADS, ROWS, HD)


def unpack_kernel(grads, *outs):
    for h in range(HEADS):
        for i, out in enumerate(outs):
            out[:, h * HD : (h + 1) * HD] = grads[h, i * ROWS : (i + 1) * ROWS, :]


def in_hbm(array):
    return pltpu.with_memory_space_constraint(array, pltpu.HBM)


def params(mib):
    return pltpu.CompilerParams(vmem_limit_bytes=mib * MIB)


def over_pairs(kernel, mib, pairs, meta, operands, in_specs, out_specs, out_shape, scratch):
    return pl.pallas_call(
        kernel,
        grid_spec=pltpu.PrefetchScalarGridSpec(
            num_scalar_prefetch=2,
            grid=(1,),
            in_specs=in_specs,
            out_specs=out_specs,
            scratch_shapes=scratch,
        ),
        out_shape=out_shape,
        compiler_params=params(mib),
    )(pairs, meta, *operands)


def pair_list(key_lists, key_counts, block_order, x, y, c):
    slot = jnp.arange(NQ, dtype=jnp.int32)
    query_at = x * NQ + ((y + slot) % NY) * NC + (c ^ (slot // NY))
    key_at = ((x - jnp.arange(NK, dtype=jnp.int32)) % NX) * NQ + y * NC + c
    query_blocks, key_blocks = block_order[query_at], block_order[key_at]
    lists, counts = key_lists[query_blocks], key_counts[query_blocks]
    used = jnp.arange(key_lists.shape[1], dtype=jnp.int32)[None, :] < counts[:, None]
    named = jnp.any((lists[None, :, :] == key_blocks[:, None, None]) & used[None, :, :], axis=2)
    named = named.reshape(NPAIR)
    code = jnp.arange(NPAIR, dtype=jnp.int32)
    rank = jnp.sum((code[None, :] < code[:, None]) & named[None, :], axis=1)
    count = jnp.sum(named.astype(jnp.int32))
    wanted = jnp.minimum(code, count - 1)
    pairs = jnp.sum(jnp.where(named[None, :] & (rank[None, :] == wanted[:, None]), code[None, :], 0), axis=1)
    return pairs.astype(jnp.int32), count, jnp.sum(named[:NQ].astype(jnp.int32))


def shifted(array, axis, by, size):
    return lax.ppermute(array, axis, [(i, (i + by) % size) for i in range(size)])


def on_device(query_data, key_data, value_data, output_data, output_grad, key_lists, key_counts, block_order):
    x, y, c = lax.axis_index("x"), lax.axis_index("y"), lax.axis_index("c")

    bf16, f32 = jnp.bfloat16, jnp.float32
    shape, vmem = jax.ShapeDtypeStruct, pl.BlockSpec(memory_space=pltpu.VMEM)
    anywhere = pl.BlockSpec(memory_space=pltpu.HBM)
    dma = pltpu.SemaphoreType.DMA

    packed = pl.pallas_call(
        pack_kernel,
        in_specs=[anywhere] * 5,
        out_specs=vmem,
        out_shape=shape((HEADS, PACKED, HD), bf16),
        scratch_shapes=[pltpu.VMEM((5, ROWS, HEADS * HD), bf16), dma((5,))],
        compiler_params=params(8),
    )(*(in_hbm(array) for array in (query_data, key_data, value_data, output_data, output_grad)))
    packed = lax.all_to_all(packed, "h", 0, 0, tiled=True)
    pairs, count, near = pair_list(key_lists, key_counts, block_order, x, y, c)
    meta = jnp.stack([count, y, c, near]).astype(jnp.int32)
    packed, pairs, meta = lax.optimization_barrier((packed, pairs, meta))

    def rows(i):
        return packed[:, i * ROWS : (i + 1) * ROWS, :].reshape(BLK, HD)

    pieces = jnp.transpose(packed[:, 4 * ROWS : 4 * ROWS + 3, :ROWS], (1, 0, 2)).reshape(12, HD)
    qd = jnp.concatenate([rows(0), rows(1), pieces, jnp.zeros((4, HD), bf16)], axis=0)
    kv = jnp.concatenate([rows(2), rows(3)], axis=0)

    own = lax.all_to_all(jnp.broadcast_to(qd[None], (NY, *qd.shape)), "y", 0, 0, tiled=True)
    keys = (kv, *(shifted(kv, "x", i, NX) for i in range(1, NX)))
    own, *keys = lax.optimization_barrier((own, *keys))
    queries = (own, shifted(own, "c", 1, NC))

    square, line = pltpu.HBM((NPAIR, BLK, BLK), bf16), shape((NPAIR, 1, BLK), f32)
    qd_scratch, kv_scratch = pltpu.VMEM((NQ, QD_ROWS, HD), bf16), pltpu.VMEM((NK, 2 * BLK, HD), bf16)
    probs, tops, stats = over_pairs(
        probs_kernel, 28, pairs, meta, (*queries, *keys),
        [anywhere] * 6,
        [anywhere, vmem, anywhere],
        [square, line, pltpu.HBM((NQ, NQ, 2, BLK), f32)],
        [
            qd_scratch, kv_scratch, pltpu.VMEM((NQ, 2, BLK), f32), [pltpu.VMEM((BLK, CHUNK), f32)] * 2,
            [pltpu.VMEM((1, CHUNK), f32)] * 2, pltpu.VMEM((2, UNROLL, BLK, BLK), bf16),
            dma((2,)), dma((NK,)), dma((2, UNROLL)), dma((NQ,)),
        ],
    )
    stats_all = lax.all_to_all(stats, ("y", "c"), 0, 0, tiled=True)
    tiles, two_steps = pltpu.VMEM((NPAIR, BLK, BLK), bf16), pltpu.VMEM((2, UNROLL, BLK, BLK), bf16)
    step_dma = dma((NPAIR // UNROLL,))
    dscore, dquery = over_pairs(
        dscore_kernel, 44, pairs, meta, (*queries, *keys, in_hbm(probs), in_hbm(stats), tops),
        [anywhere] * 8 + [vmem],
        [anywhere, anywhere],
        [square, pltpu.HBM((NQ, HD, BLK), bf16)],
        [
            qd_scratch, kv_scratch, pltpu.VMEM((NK, HD, BLK), bf16), pltpu.VMEM((NQ, HD, BLK), f32),
            pltpu.VMEM((NQ, 2, BLK), f32), [pltpu.VMEM((BLK, CHUNK), f32)] * 2, tiles, two_steps, pltpu.VMEM((NQ, HD, BLK), bf16), dma((3,)), dma((NK,)), step_dma, dma((2, UNROLL)), dma((NQ,)),
        ],
    )
    dquery = lax.all_to_all(dquery, ("y", "c"), 0, 0, tiled=True)


    def key_grads(late, pairs):
        slots = 1 if late else NK - 1
        most = slots * NQ
        held = pltpu.VMEM((most, BLK, BLK), bf16)
        return over_pairs(
            functools.partial(key_kernel, late), 50, pairs, meta,
            (*queries, in_hbm(probs), in_hbm(dscore), tops, stats_all),
            [anywhere] * 4 + [vmem] * 2,
            [vmem] * slots,
            [shape((2, BLK, HD), bf16)] * slots,
            [
                qd_scratch, pltpu.VMEM((NQ, 1, BLK), f32), pltpu.VMEM((slots, 2, BLK, HD), f32), held, held,
                dma((2,)), dma((most,)), dma((most,)),
            ],
        )

    *sent, pairs = lax.optimization_barrier((*key_grads(False, pairs), pairs))
    arrived = {i: shifted(sent[i - 1], "x", -i, NX) for i in (2, 1, 3)}
    (kept,) = key_grads(True, pairs)
    query_grad = pl.pallas_call(
        finish_queries_kernel,
        grid_spec=pltpu.PrefetchScalarGridSpec(
            num_scalar_prefetch=1,
            grid=(1,),
            in_specs=[anywhere] * 2,
            out_specs=vmem,
            scratch_shapes=[pltpu.VMEM((NQ, HD, BLK), bf16), pltpu.VMEM((NQ, NQ, 2, BLK), f32), dma((2,))],
        ),
        out_shape=shape((BLK, HD), bf16),
        compiler_params=params(12),
    )(meta, dquery, stats_all)
    grads = pl.pallas_call(
        finish_kernel,
        in_specs=[anywhere] * 5,
        out_specs=vmem,
        out_shape=shape((HEADS, 3 * ROWS, HD), bf16),
        scratch_shapes=[pltpu.VMEM((NK, 2, BLK, HD), bf16), pltpu.VMEM((BLK, HD), bf16), dma((5,))],
        compiler_params=params(12),
    )(query_grad, kept, arrived[1], arrived[2], arrived[3])
    grads = lax.all_to_all(grads, "h", 0, 0, tiled=True)

    return pl.pallas_call(
        unpack_kernel,
        in_specs=[vmem],
        out_specs=[vmem] * 3,
        out_shape=[shape((ROWS, HEADS * HD), bf16)] * 3,
        compiler_params=params(8),
    )(grads)


def solution(mesh):
    wide = Mesh(mesh.devices.reshape(NX, NY, NC, HEADS), ("x", "y", "c", "h"))
    split = P(("x", "y", "c", "h"), None)
    return jax.shard_map(
        on_device,
        mesh=wide,
        in_specs=(split,) * 5 + (P(),) * 3,
        out_specs=(split,) * 3,
        check_vma=False,
    )
```

```python
import functools
import math

import jax
import jax.numpy as jnp
from jax import lax
from jax.experimental import pallas as pl
from jax.experimental.pallas import tpu as pltpu
from jax.sharding import Mesh, PartitionSpec as P

HD = 128
BLK = 512
HEADS = 16
ROWS = BLK // HEADS
NX, NY, NC = 4, 4, 2
NQ = NY * NC
NK = NX
NPAIR = NQ * NK
PACKED = 4 * ROWS + 16
QD_ROWS = 2 * BLK + 16
UNROLL = 4
CHUNK = 256
CHUNKS = BLK // CHUNK
SCALE = 1.0 / math.sqrt(HD)
SCALE2 = SCALE * math.log2(math.e)
LOW = -1e30
MIB = 1024 * 1024


def dot(a, b, contract):
    return lax.dot_general(a, b, ((contract[:1], contract[1:]), ((), ())), preferred_element_type=jnp.float32)


def query_slot(code, meta):
    return (code & NY) | ((code + meta[1]) & (NY - 1))


def query_place(code, meta):
    slot = query_slot(code, meta)
    return (slot & (NY - 1)) * NC + (meta[2] ^ (slot // NY))


def fetch_keys(blocks, kv, sems):
    return [pltpu.make_async_copy(block, kv.at[i], sems.at[i]) for i, block in enumerate(blocks)]


def query_rows(own, other, code, meta, rows):
    slot = query_slot(code, meta)
    here = slot & (NY - 1)
    return jnp.where(slot < NY, own[here, rows, :], other[here, rows, :])


def chunk(index):
    start = index % CHUNKS * CHUNK
    return index // CHUNKS, start, slice(start, start + CHUNK)


def probs_kernel(
    pairs, meta, own, other, kv0, kv1, kv2, kv3, probs, tops, copies,
    kv, stats, scores, tops_held, held, key_sems, out_sems, copy_sems,
):
    fetches = fetch_keys((kv0, kv1, kv2, kv3), kv, key_sems)
    for fetch in fetches:
        fetch.start()
    stats[:, 0, :] = jnp.full((NQ, BLK), LOW, jnp.float32)
    stats[:, 1, :] = jnp.zeros((NQ, BLK), jnp.float32)
    for fetch in fetches:
        fetch.wait()
    count = meta[0]
    steps = (count + UNROLL - 1) // UNROLL

    def store(step, u):
        return pltpu.make_async_copy(
            held.at[step & 1, u], probs.at[step * UNROLL + u], out_sems.at[step & 1, u]
        )

    def wait_stores(step):
        for u in range(UNROLL):
            store(step, u).wait()

    def product(step, index, first):
        u, start, part = chunk(index)
        code = pairs[jnp.minimum(step * UNROLL + u, NPAIR - 1)]
        found = dot(kv[code // NQ, :BLK, :], query_rows(own, other, code, meta, part), (1, 1))
        if first and u == 0:
            key_row = lax.broadcasted_iota(jnp.int32, found.shape, 0)
            query_row = lax.broadcasted_iota(jnp.int32, found.shape, 1) + start
            found = jnp.where(key_row <= query_row, found, LOW)
        tops_held[index % 2][...] = jnp.max(found, axis=0, keepdims=True) * SCALE2
        scores[index % 2][...] = found

    def normalize(step, index):
        u, _, part = chunk(index)
        t = step * UNROLL + u
        place = query_place(pairs[t], meta)
        top = tops_held[index % 2][...]
        values = jnp.exp2(scores[index % 2][...] * SCALE2 - top)
        total = jnp.sum(values, axis=0, keepdims=True)
        held[step & 1, u, :, part] = values.astype(jnp.bfloat16)
        tops[t, :, part] = top
        top = jnp.where(t < count, top, LOW)
        total = jnp.where(t < count, total, 0.0)
        old_top, old_total = stats[place, 0:1, part], stats[place, 1:2, part]
        new_top = jnp.maximum(old_top, top)
        stats[place, 0:1, part] = new_top
        stats[place, 1:2, part] = old_total * jnp.exp2(old_top - new_top) + total * jnp.exp2(top - new_top)

    def visit(step, first):
        @pl.when(step >= 2)
        def _():
            wait_stores(step - 2)

        for index in range(UNROLL * CHUNKS):
            product(step, index + 1, first)
            normalize(step, index)
            if index % CHUNKS == CHUNKS - 1:
                store(step, index // CHUNKS).start()

    product(0, 0, True)
    visit(0, True)

    def body(step, _):
        visit(step, False)
        return 0

    lax.fori_loop(1, steps, body, 0)
    sent = [pltpu.make_async_copy(stats, copies.at[i], copy_sems.at[i]) for i in range(NQ)]
    for copy in sent:
        copy.start()
    for copy in sent:
        copy.wait()
    wait_stores(steps - 1)

    @pl.when(steps >= 2)
    def _():
        wait_stores(steps - 2)


def dscore_kernel(
    pairs, meta, own, other, kv0, kv1, kv2, kv3, probs_in, stats_in, tops, dscore, dquery,
    kv, keys_t, total, stats, dprob, probs, held, dquery_held, sems, key_sems, in_sems, out_sems, dquery_sems,
):
    count = meta[0]
    steps = (count + UNROLL - 1) // UNROLL

    def load(step):
        span = pl.ds(step * UNROLL, UNROLL)
        return pltpu.make_async_copy(probs_in.at[span], probs.at[span], in_sems.at[step])

    def store(step, u):
        return pltpu.make_async_copy(
            held.at[step & 1, u], dscore.at[step * UNROLL + u], out_sems.at[step & 1, u]
        )

    def wait_stores(step):
        for u in range(UNROLL):
            store(step, u).wait()

    key_fetches = fetch_keys((kv0, kv1, kv2, kv3), kv, key_sems)
    fetches = [pltpu.make_async_copy(stats_in.at[0], stats, sems.at[0])]
    for fetch in key_fetches + fetches:
        fetch.start()

    def start(step, _):
        load(step).start()
        return 0

    lax.fori_loop(0, steps, start, 0)
    total[...] = jnp.zeros_like(total)
    for i, fetch in enumerate(key_fetches):
        fetch.wait()
        keys_t[i] = jnp.transpose(kv[i, :BLK, :])
    for fetch in fetches:
        fetch.wait()

    def product(step, index):
        u, start, _ = chunk(index)
        code = pairs[jnp.minimum(step * UNROLL + u, NPAIR - 1)]
        grads = query_rows(own, other, code, meta, slice(BLK + start, BLK + start + CHUNK))
        dprob[index % 2][...] = dot(kv[code // NQ, BLK:, :], grads, (1, 1))

    def differentiate(step, index):
        u, start, part = chunk(index)
        t = step * UNROLL + u
        pieces = query_rows(own, other, pairs[t], meta, slice(2 * BLK, QD_ROWS)).astype(jnp.float32)
        row_dot = pieces[0:4] + pieces[4:8] + pieces[8:12]
        lines = range(start // HD, (start + CHUNK) // HD)
        row_dot = jnp.concatenate([row_dot[i : i + 1] for i in lines], axis=1)
        low = probs[t, :, part].astype(jnp.float32) * (dprob[index % 2][...] - row_dot)
        held[step & 1, u, :, part] = low.astype(jnp.bfloat16)

    def accumulate(step, index):
        u, _, part = chunk(index)
        t = step * UNROLL + u
        code = pairs[t]
        place = query_place(code, meta)
        weight = jnp.where(t < count, jnp.exp2(tops[t, :, part] - stats[place, 0:1, part]), 0.0)
        total[place, :, part] += dot(keys_t[code // NQ], held[step & 1, u, :, part], (1, 0)) * weight

    def body(step, _):
        load(step).wait()

        @pl.when(step >= 2)
        def _():
            wait_stores(step - 2)

        for index in range(UNROLL * CHUNKS):
            product(step, index + 1)
            if index > 0:
                accumulate(step, index - 1)
            differentiate(step, index)
            if index % CHUNKS == CHUNKS - 1:
                store(step, index // CHUNKS).start()
        accumulate(step, UNROLL * CHUNKS - 1)
        return 0

    product(0, 0)
    lax.fori_loop(0, steps, body, 0)
    sent = [pltpu.make_async_copy(dquery_held.at[i], dquery.at[i], dquery_sems.at[i]) for i in range(NQ)]
    for i in range(NQ):
        dquery_held[i] = total[i].astype(jnp.bfloat16)
        sent[i].start()
    for copy in sent:
        copy.wait()
    wait_stores(steps - 1)

    @pl.when(steps >= 2)
    def _():
        wait_stores(steps - 2)


def log_norms(stats_all):
    tops, sums = stats_all[:, :, 0, :], stats_all[:, :, 1, :]
    top = jnp.max(tops, axis=0)
    return top + jnp.log2(jnp.sum(sums * jnp.exp2(tops - top[None]), axis=0))


def key_kernel(late, pairs, meta, own, other, probs_in, dscore_in, tops, stats_all, *rest):
    *outs, norms, total, probs, dscore, probs_sems, dscore_sems = rest
    begin, end = (0, meta[3]) if late else (meta[3], meta[0])
    steps = (end - begin + UNROLL - 1) // UNROLL

    def loads(step):
        copies = []
        for u in range(UNROLL):
            t = jnp.minimum(begin + step * UNROLL + u, end - 1)
            held = step * UNROLL + u
            copies.append(pltpu.make_async_copy(dscore_in.at[t], dscore.at[held], dscore_sems.at[held]))
            copies.append(pltpu.make_async_copy(probs_in.at[t], probs.at[held], probs_sems.at[held]))
        return copies

    def start(step, _):
        for copy in loads(step):
            copy.start()
        return 0

    lax.fori_loop(0, steps, start, 0)
    total[...] = jnp.zeros_like(total)
    norms[:, 0, :] = log_norms(stats_all[...])

    def body(step, _):
        for copy in loads(step):
            copy.wait()
        found = []
        for u in range(UNROLL):
            held = step * UNROLL + u
            t = jnp.minimum(begin + held, end - 1)
            code = pairs[t]
            place, key = query_place(code, meta), code // NQ
            weight = jnp.where(begin + held < end, jnp.exp2(tops[t] - norms[place]), 0.0)
            weight = jnp.transpose(jnp.broadcast_to(weight, (HD, BLK)))
            queries = (query_rows(own, other, code, meta, slice(0, BLK)).astype(jnp.float32) * (weight * SCALE)).astype(jnp.bfloat16)
            grads = (query_rows(own, other, code, meta, slice(BLK, 2 * BLK)).astype(jnp.float32) * weight).astype(jnp.bfloat16)
            slot = 0 if late else key - 1
            found.append((slot, dot(dscore[held], queries, (1, 0)), dot(probs[held], grads, (1, 0))))
        for slot, key_part, value_part in found:
            total[slot, 0] += key_part
            total[slot, 1] += value_part
        return 0

    lax.fori_loop(0, steps, body, 0)
    for i, out in enumerate(outs):
        out[...] = total[i].astype(jnp.bfloat16)


def pack_kernel(query_in, key_in, value_in, output_in, grad_in, out, held, sems):
    fetches = [
        pltpu.make_async_copy(source, held.at[i], sems.at[i])
        for i, source in enumerate((query_in, key_in, value_in, output_in, grad_in))
    ]
    for fetch in fetches:
        fetch.start()
    for fetch in fetches:
        fetch.wait()
    query, key, value, output, grad = (held.at[i] for i in range(5))
    lane = lax.broadcasted_iota(jnp.int32, (ROWS, HD), 1)
    row_dot = jnp.zeros((ROWS, HD), jnp.float32)
    for h in range(HEADS):
        part = slice(h * HD, (h + 1) * HD)
        for i, array in enumerate((query, grad, key, value)):
            out[h, i * ROWS : (i + 1) * ROWS, :] = array[:, part]
        products = grad[:, part].astype(jnp.float32) * output[:, part].astype(jnp.float32)
        row_dot = jnp.where(lane == h, jnp.sum(products, axis=1, keepdims=True), row_dot)
    row_dot = jnp.concatenate([row_dot, jnp.zeros((HD - ROWS, HD), jnp.float32)], axis=0)
    row_dot = jnp.transpose(row_dot)[:HEADS]
    high = row_dot.astype(jnp.bfloat16).astype(jnp.float32)
    middle = (row_dot - high).astype(jnp.bfloat16).astype(jnp.float32)
    row = lax.broadcasted_iota(jnp.int32, (HEADS, 16, HD), 1)
    pieces = jnp.zeros((HEADS, 16, HD), jnp.float32)
    for i, piece in enumerate((high, middle, row_dot - high - middle)):
        pieces = jnp.where(row == i, piece[:, None, :], pieces)
    out[:, 4 * ROWS :, :] = pieces.astype(jnp.bfloat16)


def finish_queries_kernel(meta, dquery_in, stats_in, out, dquery, stats_all, sems):
    fetches = [
        pltpu.make_async_copy(stats_in, stats_all, sems.at[0]),
        pltpu.make_async_copy(dquery_in, dquery, sems.at[1]),
    ]
    for fetch in fetches:
        fetch.start()
    for fetch in fetches:
        fetch.wait()
    place = meta[1] * NC + meta[2]
    tops, sums = stats_all[:, place, 0, :], stats_all[:, place, 1, :]
    top = jnp.max(tops, axis=0, keepdims=True)
    norm = top + jnp.log2(jnp.sum(sums * jnp.exp2(tops - top), axis=0, keepdims=True))
    weight = jnp.exp2(tops - norm) * SCALE
    grad = dquery[0].astype(jnp.float32) * weight[0:1]
    for i in range(1, NQ):
        grad += dquery[i].astype(jnp.float32) * weight[i : i + 1]
    out[...] = jnp.transpose(grad).astype(jnp.bfloat16)


def finish_kernel(query_grad, kept, first, second, third, out, parts, query_held, sems):
    fetches = [
        pltpu.make_async_copy(source, parts.at[i], sems.at[i])
        for i, source in enumerate((kept, first, second, third))
    ]
    fetches.append(pltpu.make_async_copy(query_grad, query_held, sems.at[4]))
    for fetch in fetches:
        fetch.start()
    for fetch in fetches:
        fetch.wait()
    out[:, 0:ROWS, :] = query_held[...].reshape(HEADS, ROWS, HD)
    for i in range(2):
        grad = (parts[0, i].astype(jnp.float32) + parts[1, i].astype(jnp.float32)) + (
            parts[2, i].astype(jnp.float32) + parts[3, i].astype(jnp.float32)
        )
        out[:, (i + 1) * ROWS : (i + 2) * ROWS, :] = grad.astype(jnp.bfloat16).reshape(HEADS, ROWS, HD)


def unpack_kernel(grads, *outs):
    for h in range(HEADS):
        for i, out in enumerate(outs):
            out[:, h * HD : (h + 1) * HD] = grads[h, i * ROWS : (i + 1) * ROWS, :]


def in_hbm(array):
    return pltpu.with_memory_space_constraint(array, pltpu.HBM)


def params(mib):
    return pltpu.CompilerParams(vmem_limit_bytes=mib * MIB)


def over_pairs(kernel, mib, pairs, meta, operands, in_specs, out_specs, out_shape, scratch):
    return pl.pallas_call(
        kernel,
        grid_spec=pltpu.PrefetchScalarGridSpec(
            num_scalar_prefetch=2,
            grid=(1,),
            in_specs=in_specs,
            out_specs=out_specs,
            scratch_shapes=scratch,
        ),
        out_shape=out_shape,
        compiler_params=params(mib),
    )(pairs, meta, *operands)


def pair_list(key_lists, key_counts, block_order, x, y, c):
    slot = jnp.arange(NQ, dtype=jnp.int32)
    query_at = x * NQ + ((y + slot) % NY) * NC + (c ^ (slot // NY))
    key_at = ((x - jnp.arange(NK, dtype=jnp.int32)) % NX) * NQ + y * NC + c
    query_blocks, key_blocks = block_order[query_at], block_order[key_at]
    lists, counts = key_lists[query_blocks], key_counts[query_blocks]
    used = jnp.arange(key_lists.shape[1], dtype=jnp.int32)[None, :] < counts[:, None]
    named = jnp.any((lists[None, :, :] == key_blocks[:, None, None]) & used[None, :, :], axis=2)
    named = named.reshape(NPAIR)
    code = jnp.arange(NPAIR, dtype=jnp.int32)
    rank = jnp.sum((code[None, :] < code[:, None]) & named[None, :], axis=1)
    count = jnp.sum(named.astype(jnp.int32))
    wanted = jnp.minimum(code, count - 1)
    pairs = jnp.sum(jnp.where(named[None, :] & (rank[None, :] == wanted[:, None]), code[None, :], 0), axis=1)
    return pairs.astype(jnp.int32), count, jnp.sum(named[:NQ].astype(jnp.int32))


def shifted(array, axis, by, size):
    return lax.ppermute(array, axis, [(i, (i + by) % size) for i in range(size)])


def on_device(query_data, key_data, value_data, output_data, output_grad, key_lists, key_counts, block_order):
    x, y, c = lax.axis_index("x"), lax.axis_index("y"), lax.axis_index("c")

    bf16, f32 = jnp.bfloat16, jnp.float32
    shape, vmem = jax.ShapeDtypeStruct, pl.BlockSpec(memory_space=pltpu.VMEM)
    anywhere = pl.BlockSpec(memory_space=pltpu.HBM)
    dma = pltpu.SemaphoreType.DMA

    packed = pl.pallas_call(
        pack_kernel,
        in_specs=[anywhere] * 5,
        out_specs=vmem,
        out_shape=shape((HEADS, PACKED, HD), bf16),
        scratch_shapes=[pltpu.VMEM((5, ROWS, HEADS * HD), bf16), dma((5,))],
        compiler_params=params(8),
    )(*(in_hbm(array) for array in (query_data, key_data, value_data, output_data, output_grad)))
    packed = lax.all_to_all(packed, "h", 0, 0, tiled=True)
    pairs, count, near = pair_list(key_lists, key_counts, block_order, x, y, c)
    meta = jnp.stack([count, y, c, near]).astype(jnp.int32)
    packed, pairs, meta = lax.optimization_barrier((packed, pairs, meta))

    def rows(i):
        return packed[:, i * ROWS : (i + 1) * ROWS, :].reshape(BLK, HD)

    pieces = jnp.transpose(packed[:, 4 * ROWS : 4 * ROWS + 3, :ROWS], (1, 0, 2)).reshape(12, HD)
    qd = jnp.concatenate([rows(0), rows(1), pieces, jnp.zeros((4, HD), bf16)], axis=0)
    kv = jnp.concatenate([rows(2), rows(3)], axis=0)

    own = lax.all_to_all(jnp.broadcast_to(qd[None], (NY, *qd.shape)), "y", 0, 0, tiled=True)
    keys = (kv, *(shifted(kv, "x", i, NX) for i in range(1, NX)))
    own, *keys = lax.optimization_barrier((own, *keys))
    queries = (own, shifted(own, "c", 1, NC))

    square, line = pltpu.HBM((NPAIR, BLK, BLK), bf16), shape((NPAIR, 1, BLK), f32)
    kv_scratch = pltpu.VMEM((NK, 2 * BLK, HD), bf16)
    probs, tops, stats = over_pairs(
        probs_kernel, 28, pairs, meta, (*queries, *keys),
        [vmem] * 2 + [anywhere] * 4,
        [anywhere, vmem, anywhere],
        [square, line, pltpu.HBM((NQ, NQ, 2, BLK), f32)],
        [
            kv_scratch, pltpu.VMEM((NQ, 2, BLK), f32), [pltpu.VMEM((BLK, CHUNK), f32)] * 2,
            [pltpu.VMEM((1, CHUNK), f32)] * 2, pltpu.VMEM((2, UNROLL, BLK, BLK), bf16),
            dma((NK,)), dma((2, UNROLL)), dma((NQ,)),
        ],
    )
    stats_all = lax.all_to_all(stats, ("y", "c"), 0, 0, tiled=True)
    tiles, two_steps = pltpu.VMEM((NPAIR, BLK, BLK), bf16), pltpu.VMEM((2, UNROLL, BLK, BLK), bf16)
    step_dma = dma((NPAIR // UNROLL,))
    dscore, dquery = over_pairs(
        dscore_kernel, 44, pairs, meta, (*queries, *keys, in_hbm(probs), in_hbm(stats), tops),
        [vmem] * 2 + [anywhere] * 6 + [vmem],
        [anywhere, anywhere],
        [square, pltpu.HBM((NQ, HD, BLK), bf16)],
        [
            kv_scratch, pltpu.VMEM((NK, HD, BLK), bf16), pltpu.VMEM((NQ, HD, BLK), f32),
            pltpu.VMEM((NQ, 2, BLK), f32), [pltpu.VMEM((BLK, CHUNK), f32)] * 2, tiles, two_steps, pltpu.VMEM((NQ, HD, BLK), bf16), dma((1,)), dma((NK,)), step_dma, dma((2, UNROLL)), dma((NQ,)),
        ],
    )
    dquery = lax.all_to_all(dquery, ("y", "c"), 0, 0, tiled=True)


    def key_grads(late, pairs):
        slots = 1 if late else NK - 1
        most = slots * NQ
        held = pltpu.VMEM((most, BLK, BLK), bf16)
        return over_pairs(
            functools.partial(key_kernel, late), 50, pairs, meta,
            (*queries, in_hbm(probs), in_hbm(dscore), tops, stats_all),
            [vmem] * 2 + [anywhere] * 2 + [vmem] * 2,
            [vmem] * slots,
            [shape((2, BLK, HD), bf16)] * slots,
            [
                pltpu.VMEM((NQ, 1, BLK), f32), pltpu.VMEM((slots, 2, BLK, HD), f32), held, held,
                dma((most,)), dma((most,)),
            ],
        )

    *sent, pairs = lax.optimization_barrier((*key_grads(False, pairs), pairs))
    arrived = {i: shifted(sent[i - 1], "x", -i, NX) for i in (2, 1, 3)}
    (kept,) = key_grads(True, pairs)
    query_grad = pl.pallas_call(
        finish_queries_kernel,
        grid_spec=pltpu.PrefetchScalarGridSpec(
            num_scalar_prefetch=1,
            grid=(1,),
            in_specs=[anywhere] * 2,
            out_specs=vmem,
            scratch_shapes=[pltpu.VMEM((NQ, HD, BLK), bf16), pltpu.VMEM((NQ, NQ, 2, BLK), f32), dma((2,))],
        ),
        out_shape=shape((BLK, HD), bf16),
        compiler_params=params(12),
    )(meta, dquery, stats_all)
    grads = pl.pallas_call(
        finish_kernel,
        in_specs=[anywhere] * 5,
        out_specs=vmem,
        out_shape=shape((HEADS, 3 * ROWS, HD), bf16),
        scratch_shapes=[pltpu.VMEM((NK, 2, BLK, HD), bf16), pltpu.VMEM((BLK, HD), bf16), dma((5,))],
        compiler_params=params(12),
    )(query_grad, kept, arrived[1], arrived[2], arrived[3])
    grads = lax.all_to_all(grads, "h", 0, 0, tiled=True)

    return pl.pallas_call(
        unpack_kernel,
        in_specs=[vmem],
        out_specs=[vmem] * 3,
        out_shape=[shape((ROWS, HEADS * HD), bf16)] * 3,
        compiler_params=params(8),
    )(grads)


def solution(mesh):
    wide = Mesh(mesh.devices.reshape(NX, NY, NC, HEADS), ("x", "y", "c", "h"))
    split = P(("x", "y", "c", "h"), None)
    return jax.shard_map(
        on_device,
        mesh=wide,
        in_specs=(split,) * 5 + (P(),) * 3,
        out_specs=(split,) * 3,
        check_vma=False,
    )
```

```python
import functools
import math

import jax
import jax.numpy as jnp
from jax import lax
from jax.experimental import pallas as pl
from jax.experimental.pallas import tpu as pltpu
from jax.sharding import Mesh, PartitionSpec as P

HD = 128
BLK = 512
HEADS = 16
ROWS = BLK // HEADS
NX, NY, NC = 4, 4, 2
NQ = NY * NC
NK = NX
NPAIR = NQ * NK
PACKED = 4 * ROWS + 16
QD_ROWS = 2 * BLK + 16
UNROLL = 4
CHUNK = 256
CHUNKS = BLK // CHUNK
SCALE = 1.0 / math.sqrt(HD)
SCALE2 = SCALE * math.log2(math.e)
LOW = -1e30
MIB = 1024 * 1024


def dot(a, b, contract):
    return lax.dot_general(a, b, ((contract[:1], contract[1:]), ((), ())), preferred_element_type=jnp.float32)


def query_slot(code, meta):
    return (code & NY) | ((code + meta[1]) & (NY - 1))


def query_place(code, meta):
    slot = query_slot(code, meta)
    return (slot & (NY - 1)) * NC + (meta[2] ^ (slot // NY))


def fetch_keys(blocks, kv, sems):
    return [pltpu.make_async_copy(block, kv.at[i], sems.at[i]) for i, block in enumerate(blocks)]


def fetch_queries(own, other, qd, sems):
    return [
        pltpu.make_async_copy(own, qd.at[pl.ds(0, NY)], sems.at[0]),
        pltpu.make_async_copy(other, qd.at[pl.ds(NY, NY)], sems.at[1]),
    ]


def chunk(index):
    start = index % CHUNKS * CHUNK
    return index // CHUNKS, start, slice(start, start + CHUNK)


def probs_kernel(
    pairs, meta, own, other, kv0, kv1, kv2, kv3, probs, tops, copies,
    qd, kv, stats, scores, tops_held, held, sems, key_sems, out_sems, copy_sems,
):
    fetches = fetch_queries(own, other, qd, sems) + fetch_keys((kv0, kv1, kv2, kv3), kv, key_sems)
    for fetch in fetches:
        fetch.start()
    stats[:, 0, :] = jnp.full((NQ, BLK), LOW, jnp.float32)
    stats[:, 1, :] = jnp.zeros((NQ, BLK), jnp.float32)
    for fetch in fetches:
        fetch.wait()
    count = meta[0]
    steps = (count + UNROLL - 1) // UNROLL

    def store(step, u):
        return pltpu.make_async_copy(
            held.at[step & 1, u], probs.at[step * UNROLL + u], out_sems.at[step & 1, u]
        )

    def wait_stores(step):
        for u in range(UNROLL):
            store(step, u).wait()

    def product(step, index, first):
        u, start, part = chunk(index)
        code = pairs[jnp.minimum(step * UNROLL + u, NPAIR - 1)]
        found = dot(kv[code // NQ, :BLK, :], qd[query_slot(code, meta), part, :], (1, 1))
        if first and u == 0:
            key_row = lax.broadcasted_iota(jnp.int32, found.shape, 0)
            query_row = lax.broadcasted_iota(jnp.int32, found.shape, 1) + start
            found = jnp.where(key_row <= query_row, found, LOW)
        tops_held[index % 2][...] = jnp.max(found, axis=0, keepdims=True) * SCALE2
        scores[index % 2][...] = found

    def normalize(step, index):
        u, _, part = chunk(index)
        t = step * UNROLL + u
        place = query_place(pairs[t], meta)
        top = tops_held[index % 2][...]
        values = jnp.exp2(scores[index % 2][...] * SCALE2 - top)
        total = jnp.sum(values, axis=0, keepdims=True)
        held[step & 1, u, :, part] = values.astype(jnp.bfloat16)
        tops[t, :, part] = top
        top = jnp.where(t < count, top, LOW)
        total = jnp.where(t < count, total, 0.0)
        old_top, old_total = stats[place, 0:1, part], stats[place, 1:2, part]
        new_top = jnp.maximum(old_top, top)
        stats[place, 0:1, part] = new_top
        stats[place, 1:2, part] = old_total * jnp.exp2(old_top - new_top) + total * jnp.exp2(top - new_top)

    def visit(step, first):
        @pl.when(step >= 2)
        def _():
            wait_stores(step - 2)

        for index in range(UNROLL * CHUNKS):
            product(step, index + 1, first)
            normalize(step, index)
            if index % CHUNKS == CHUNKS - 1:
                store(step, index // CHUNKS).start()

    product(0, 0, True)
    visit(0, True)

    def body(step, _):
        visit(step, False)
        return 0

    lax.fori_loop(1, steps, body, 0)
    sent = [pltpu.make_async_copy(stats, copies.at[i], copy_sems.at[i]) for i in range(NQ)]
    for copy in sent:
        copy.start()
    for copy in sent:
        copy.wait()
    wait_stores(steps - 1)

    @pl.when(steps >= 2)
    def _():
        wait_stores(steps - 2)


def dscore_kernel(
    pairs, meta, own, other, kv0, kv1, kv2, kv3, probs_in, stats_in, tops, dscore, dquery,
    qd, kv, keys_t, total, stats, dprob, probs, held, dquery_held, sems, key_sems, in_sems, out_sems, dquery_sems,
):
    count = meta[0]
    steps = (count + UNROLL - 1) // UNROLL

    def load(step):
        span = pl.ds(step * UNROLL, UNROLL)
        return pltpu.make_async_copy(probs_in.at[span], probs.at[span], in_sems.at[step])

    def store(step, u):
        return pltpu.make_async_copy(
            held.at[step & 1, u], dscore.at[step * UNROLL + u], out_sems.at[step & 1, u]
        )

    def wait_stores(step):
        for u in range(UNROLL):
            store(step, u).wait()

    key_fetches = fetch_keys((kv0, kv1, kv2, kv3), kv, key_sems)
    fetches = fetch_queries(own, other, qd, sems)
    fetches.append(pltpu.make_async_copy(stats_in.at[0], stats, sems.at[2]))
    for fetch in key_fetches + fetches:
        fetch.start()

    def start(step, _):
        load(step).start()
        return 0

    lax.fori_loop(0, steps, start, 0)
    total[...] = jnp.zeros_like(total)
    for i, fetch in enumerate(key_fetches):
        fetch.wait()
        keys_t[i] = jnp.transpose(kv[i, :BLK, :])
    for fetch in fetches:
        fetch.wait()

    def product(step, index):
        u, start, _ = chunk(index)
        code = pairs[jnp.minimum(step * UNROLL + u, NPAIR - 1)]
        grads = qd[query_slot(code, meta), BLK + start : BLK + start + CHUNK, :]
        dprob[index % 2][...] = dot(kv[code // NQ, BLK:, :], grads, (1, 1))

    def differentiate(step, index):
        u, start, part = chunk(index)
        t = step * UNROLL + u
        pieces = qd[query_slot(pairs[t], meta), 2 * BLK :, :].astype(jnp.float32)
        row_dot = pieces[0:4] + pieces[4:8] + pieces[8:12]
        lines = range(start // HD, (start + CHUNK) // HD)
        row_dot = jnp.concatenate([row_dot[i : i + 1] for i in lines], axis=1)
        low = probs[t, :, part].astype(jnp.float32) * (dprob[index % 2][...] - row_dot)
        held[step & 1, u, :, part] = low.astype(jnp.bfloat16)

    def accumulate(step, index):
        u, _, part = chunk(index)
        t = step * UNROLL + u
        code = pairs[t]
        place = query_place(code, meta)
        weight = jnp.where(t < count, jnp.exp2(tops[t, :, part] - stats[place, 0:1, part]), 0.0)
        total[place, :, part] += dot(keys_t[code // NQ], held[step & 1, u, :, part], (1, 0)) * weight

    def body(step, _):
        load(step).wait()

        @pl.when(step >= 2)
        def _():
            wait_stores(step - 2)

        for index in range(UNROLL * CHUNKS):
            product(step, index + 1)
            if index > 0:
                accumulate(step, index - 1)
            differentiate(step, index)
            if index % CHUNKS == CHUNKS - 1:
                store(step, index // CHUNKS).start()
        accumulate(step, UNROLL * CHUNKS - 1)
        return 0

    product(0, 0)
    lax.fori_loop(0, steps, body, 0)
    sent = [pltpu.make_async_copy(dquery_held.at[i], dquery.at[i], dquery_sems.at[i]) for i in range(NQ)]
    for i in range(NQ):
        dquery_held[i] = total[i].astype(jnp.bfloat16)
        sent[i].start()
    for copy in sent:
        copy.wait()
    wait_stores(steps - 1)

    @pl.when(steps >= 2)
    def _():
        wait_stores(steps - 2)


def log_norms(stats_all):
    tops, sums = stats_all[:, :, 0, :], stats_all[:, :, 1, :]
    top = jnp.max(tops, axis=0)
    return top + jnp.log2(jnp.sum(sums * jnp.exp2(tops - top[None]), axis=0))


def key_kernel(late, pairs, meta, own, other, probs_in, dscore_in, tops, stats_all, *rest):
    *outs, qd, norms, total, probs, dscore, sems, probs_sems, dscore_sems = rest
    begin, end = (0, meta[3]) if late else (meta[3], meta[0])
    steps = (end - begin + UNROLL - 1) // UNROLL

    def loads(step):
        copies = []
        for u in range(UNROLL):
            t = jnp.minimum(begin + step * UNROLL + u, end - 1)
            held = step * UNROLL + u
            copies.append(pltpu.make_async_copy(dscore_in.at[t], dscore.at[held], dscore_sems.at[held]))
            copies.append(pltpu.make_async_copy(probs_in.at[t], probs.at[held], probs_sems.at[held]))
        return copies

    def start(step, _):
        for copy in loads(step):
            copy.start()
        return 0

    lax.fori_loop(0, jnp.minimum(steps, 1), start, 0)
    fetches = fetch_queries(own, other, qd, sems)
    for fetch in fetches:
        fetch.start()
    lax.fori_loop(1, steps, start, 0)
    total[...] = jnp.zeros_like(total)
    norms[:, 0, :] = log_norms(stats_all[...])
    for fetch in fetches:
        fetch.wait()

    def body(step, _):
        for copy in loads(step):
            copy.wait()
        found = []
        for u in range(UNROLL):
            held = step * UNROLL + u
            t = jnp.minimum(begin + held, end - 1)
            code = pairs[t]
            place, key, query = query_place(code, meta), code // NQ, query_slot(code, meta)
            weight = jnp.where(begin + held < end, jnp.exp2(tops[t] - norms[place]), 0.0)
            weight = jnp.transpose(jnp.broadcast_to(weight, (HD, BLK)))
            queries = (qd[query, :BLK, :].astype(jnp.float32) * (weight * SCALE)).astype(jnp.bfloat16)
            grads = (qd[query, BLK : 2 * BLK, :].astype(jnp.float32) * weight).astype(jnp.bfloat16)
            slot = 0 if late else key - 1
            found.append((slot, dot(dscore[held], queries, (1, 0)), dot(probs[held], grads, (1, 0))))
        for slot, key_part, value_part in found:
            total[slot, 0] += key_part
            total[slot, 1] += value_part
        return 0

    lax.fori_loop(0, steps, body, 0)
    for i, out in enumerate(outs):
        out[...] = total[i].astype(jnp.bfloat16)


def pack_kernel(query_in, key_in, value_in, output_in, grad_in, out, held, sems):
    fetches = [
        pltpu.make_async_copy(source, held.at[i], sems.at[i])
        for i, source in enumerate((query_in, key_in, value_in, output_in, grad_in))
    ]
    for fetch in fetches:
        fetch.start()
    for fetch in fetches:
        fetch.wait()
    query, key, value, output, grad = (held.at[i] for i in range(5))
    lane = lax.broadcasted_iota(jnp.int32, (ROWS, HD), 1)
    row_dot = jnp.zeros((ROWS, HD), jnp.float32)
    for h in range(HEADS):
        part = slice(h * HD, (h + 1) * HD)
        for i, array in enumerate((query, grad, key, value)):
            out[h, i * ROWS : (i + 1) * ROWS, :] = array[:, part]
        products = grad[:, part].astype(jnp.float32) * output[:, part].astype(jnp.float32)
        row_dot = jnp.where(lane == h, jnp.sum(products, axis=1, keepdims=True), row_dot)
    row_dot = jnp.concatenate([row_dot, jnp.zeros((HD - ROWS, HD), jnp.float32)], axis=0)
    row_dot = jnp.transpose(row_dot)[:HEADS]
    high = row_dot.astype(jnp.bfloat16).astype(jnp.float32)
    middle = (row_dot - high).astype(jnp.bfloat16).astype(jnp.float32)
    row = lax.broadcasted_iota(jnp.int32, (HEADS, 16, HD), 1)
    pieces = jnp.zeros((HEADS, 16, HD), jnp.float32)
    for i, piece in enumerate((high, middle, row_dot - high - middle)):
        pieces = jnp.where(row == i, piece[:, None, :], pieces)
    out[:, 4 * ROWS :, :] = pieces.astype(jnp.bfloat16)


def finish_queries_kernel(meta, dquery_in, stats_in, out, dquery, stats_all, sems):
    fetches = [
        pltpu.make_async_copy(stats_in, stats_all, sems.at[0]),
        pltpu.make_async_copy(dquery_in, dquery, sems.at[1]),
    ]
    for fetch in fetches:
        fetch.start()
    for fetch in fetches:
        fetch.wait()
    place = meta[1] * NC + meta[2]
    tops, sums = stats_all[:, place, 0, :], stats_all[:, place, 1, :]
    top = jnp.max(tops, axis=0, keepdims=True)
    norm = top + jnp.log2(jnp.sum(sums * jnp.exp2(tops - top), axis=0, keepdims=True))
    weight = jnp.exp2(tops - norm) * SCALE
    grad = dquery[0].astype(jnp.float32) * weight[0:1]
    for i in range(1, NQ):
        grad += dquery[i].astype(jnp.float32) * weight[i : i + 1]
    out[...] = jnp.transpose(grad).astype(jnp.bfloat16)


def finish_kernel(query_grad, kept, first, second, third, out, parts, query_held, sems):
    fetches = [
        pltpu.make_async_copy(source, parts.at[i], sems.at[i])
        for i, source in enumerate((kept, first, second, third))
    ]
    fetches.append(pltpu.make_async_copy(query_grad, query_held, sems.at[4]))
    for fetch in fetches:
        fetch.start()
    for fetch in fetches:
        fetch.wait()
    out[:, 0:ROWS, :] = query_held[...].reshape(HEADS, ROWS, HD)
    for i in range(2):
        grad = (parts[0, i].astype(jnp.float32) + parts[1, i].astype(jnp.float32)) + (
            parts[2, i].astype(jnp.float32) + parts[3, i].astype(jnp.float32)
        )
        out[:, (i + 1) * ROWS : (i + 2) * ROWS, :] = grad.astype(jnp.bfloat16).reshape(HEADS, ROWS, HD)


def unpack_kernel(grads, *outs):
    for h in range(HEADS):
        for i, out in enumerate(outs):
            out[:, h * HD : (h + 1) * HD] = grads[h, i * ROWS : (i + 1) * ROWS, :]


def in_hbm(array):
    return pltpu.with_memory_space_constraint(array, pltpu.HBM)


def params(mib):
    return pltpu.CompilerParams(vmem_limit_bytes=mib * MIB)


def over_pairs(kernel, mib, pairs, meta, operands, in_specs, out_specs, out_shape, scratch):
    return pl.pallas_call(
        kernel,
        grid_spec=pltpu.PrefetchScalarGridSpec(
            num_scalar_prefetch=2,
            grid=(1,),
            in_specs=in_specs,
            out_specs=out_specs,
            scratch_shapes=scratch,
        ),
        out_shape=out_shape,
        compiler_params=params(mib),
    )(pairs, meta, *operands)


def pair_list(key_lists, key_counts, block_order, x, y, c):
    slot = jnp.arange(NQ, dtype=jnp.int32)
    query_at = x * NQ + ((y + slot) % NY) * NC + (c ^ (slot // NY))
    key_at = ((x - jnp.arange(NK, dtype=jnp.int32)) % NX) * NQ + y * NC + c
    query_blocks, key_blocks = block_order[query_at], block_order[key_at]
    lists, counts = key_lists[query_blocks], key_counts[query_blocks]
    used = jnp.arange(key_lists.shape[1], dtype=jnp.int32)[None, :] < counts[:, None]
    named = jnp.any((lists[None, :, :] == key_blocks[:, None, None]) & used[None, :, :], axis=2)
    named = named.reshape(NPAIR)
    code = jnp.arange(NPAIR, dtype=jnp.int32)
    rank = jnp.sum((code[None, :] < code[:, None]) & named[None, :], axis=1)
    count = jnp.sum(named.astype(jnp.int32))
    wanted = jnp.minimum(code, count - 1)
    pairs = jnp.sum(jnp.where(named[None, :] & (rank[None, :] == wanted[:, None]), code[None, :], 0), axis=1)
    return pairs.astype(jnp.int32), count, jnp.sum(named[:NQ].astype(jnp.int32))


def shifted(array, axis, by, size):
    return lax.ppermute(array, axis, [(i, (i + by) % size) for i in range(size)])


def on_device(query_data, key_data, value_data, output_data, output_grad, key_lists, key_counts, block_order):
    x, y, c = lax.axis_index("x"), lax.axis_index("y"), lax.axis_index("c")

    bf16, f32 = jnp.bfloat16, jnp.float32
    shape, vmem = jax.ShapeDtypeStruct, pl.BlockSpec(memory_space=pltpu.VMEM)
    anywhere = pl.BlockSpec(memory_space=pltpu.HBM)
    dma = pltpu.SemaphoreType.DMA

    packed = pl.pallas_call(
        pack_kernel,
        in_specs=[anywhere] * 5,
        out_specs=vmem,
        out_shape=shape((HEADS, PACKED, HD), bf16),
        scratch_shapes=[pltpu.VMEM((5, ROWS, HEADS * HD), bf16), dma((5,))],
        compiler_params=params(8),
    )(*(in_hbm(array) for array in (query_data, key_data, value_data, output_data, output_grad)))
    packed = lax.all_to_all(packed, "h", 0, 0, tiled=True)
    pairs, count, near = pair_list(key_lists, key_counts, block_order, x, y, c)
    meta = jnp.stack([count, y, c, near]).astype(jnp.int32)
    packed, pairs, meta = lax.optimization_barrier((packed, pairs, meta))

    def rows(i):
        return packed[:, i * ROWS : (i + 1) * ROWS, :].reshape(BLK, HD)

    pieces = jnp.transpose(packed[:, 4 * ROWS : 4 * ROWS + 3, :ROWS], (1, 0, 2)).reshape(12, HD)
    qd = jnp.concatenate([rows(0), rows(1), pieces, jnp.zeros((4, HD), bf16)], axis=0)
    kv = jnp.concatenate([rows(2), rows(3)], axis=0)

    own = lax.all_to_all(jnp.broadcast_to(qd[None], (NY, *qd.shape)), "y", 0, 0, tiled=True)
    keys = (kv, *(shifted(kv, "x", i, NX) for i in range(1, NX)))
    own, *keys = lax.optimization_barrier((own, *keys))
    queries = (own, shifted(own, "c", 1, NC))

    square, line = pltpu.HBM((NPAIR, BLK, BLK), bf16), shape((NPAIR, 1, BLK), f32)
    qd_scratch, kv_scratch = pltpu.VMEM((NQ, QD_ROWS, HD), bf16), pltpu.VMEM((NK, 2 * BLK, HD), bf16)
    probs, tops, stats = over_pairs(
        probs_kernel, 28, pairs, meta, (*queries, *keys),
        [anywhere] * 6,
        [anywhere, vmem, anywhere],
        [square, line, pltpu.HBM((NQ, NQ, 2, BLK), f32)],
        [
            qd_scratch, kv_scratch, pltpu.VMEM((NQ, 2, BLK), f32), [pltpu.VMEM((BLK, CHUNK), f32)] * 2,
            [pltpu.VMEM((1, CHUNK), f32)] * 2, pltpu.VMEM((2, UNROLL, BLK, BLK), bf16),
            dma((2,)), dma((NK,)), dma((2, UNROLL)), dma((NQ,)),
        ],
    )
    stats_all = lax.all_to_all(stats, ("y", "c"), 0, 0, tiled=True)
    tiles, two_steps = pltpu.VMEM((NPAIR, BLK, BLK), bf16), pltpu.VMEM((2, UNROLL, BLK, BLK), bf16)
    step_dma = dma((NPAIR // UNROLL,))
    dscore, dquery = over_pairs(
        dscore_kernel, 44, pairs, meta, (*queries, *keys, in_hbm(probs), in_hbm(stats), tops),
        [anywhere] * 8 + [vmem],
        [anywhere, anywhere],
        [square, pltpu.HBM((NQ, HD, BLK), bf16)],
        [
            qd_scratch, kv_scratch, pltpu.VMEM((NK, HD, BLK), bf16), pltpu.VMEM((NQ, HD, BLK), f32),
            pltpu.VMEM((NQ, 2, BLK), f32), [pltpu.VMEM((BLK, CHUNK), f32)] * 2, tiles, two_steps, pltpu.VMEM((NQ, HD, BLK), bf16), dma((3,)), dma((NK,)), step_dma, dma((2, UNROLL)), dma((NQ,)),
        ],
    )
    dquery = lax.all_to_all(dquery, ("y", "c"), 0, 0, tiled=True)


    def key_grads(late, pairs):
        slots = 1 if late else NK - 1
        most = slots * NQ
        held = pltpu.VMEM((most, BLK, BLK), bf16)
        return over_pairs(
            functools.partial(key_kernel, late), 50, pairs, meta,
            (*queries, in_hbm(probs), in_hbm(dscore), tops, stats_all),
            [anywhere] * 4 + [vmem] * 2,
            [vmem] * slots,
            [shape((2, BLK, HD), bf16)] * slots,
            [
                qd_scratch, pltpu.VMEM((NQ, 1, BLK), f32), pltpu.VMEM((slots, 2, BLK, HD), f32), held, held,
                dma((2,)), dma((most,)), dma((most,)),
            ],
        )

    *sent, pairs = lax.optimization_barrier((*key_grads(False, pairs), pairs))
    arrived = {i: shifted(sent[i - 1], "x", -i, NX) for i in (2, 1, 3)}
    (kept,) = key_grads(True, pairs)
    query_grad = pl.pallas_call(
        finish_queries_kernel,
        grid_spec=pltpu.PrefetchScalarGridSpec(
            num_scalar_prefetch=1,
            grid=(1,),
            in_specs=[anywhere] * 2,
            out_specs=vmem,
            scratch_shapes=[pltpu.VMEM((NQ, HD, BLK), bf16), pltpu.VMEM((NQ, NQ, 2, BLK), f32), dma((2,))],
        ),
        out_shape=shape((BLK, HD), bf16),
        compiler_params=params(12),
    )(meta, dquery, stats_all)
    grads = pl.pallas_call(
        finish_kernel,
        in_specs=[anywhere] * 5,
        out_specs=vmem,
        out_shape=shape((HEADS, 3 * ROWS, HD), bf16),
        scratch_shapes=[pltpu.VMEM((NK, 2, BLK, HD), bf16), pltpu.VMEM((BLK, HD), bf16), dma((5,))],
        compiler_params=params(12),
    )(query_grad, kept, arrived[2], arrived[1], arrived[3])
    grads = lax.all_to_all(grads, "h", 0, 0, tiled=True)

    return pl.pallas_call(
        unpack_kernel,
        in_specs=[vmem],
        out_specs=[vmem] * 3,
        out_shape=[shape((ROWS, HEADS * HD), bf16)] * 3,
        compiler_params=params(8),
    )(grads)


def solution(mesh):
    wide = Mesh(mesh.devices.reshape(NX, NY, NC, HEADS), ("x", "y", "c", "h"))
    split = P(("x", "y", "c", "h"), None)
    return jax.shard_map(
        on_device,
        mesh=wide,
        in_specs=(split,) * 5 + (P(),) * 3,
        out_specs=(split,) * 3,
        check_vma=False,
    )
```
